32 devices in a mesh: section: 2 (over core), dp: 16 (over z, y, x).
Axes of the slice: x: 2, y: 2, z: 4, core: 2. Of those that a mesh axis runs over, the one named last changes fastest.
Arguments:
- byte_ids: int32 [2, 16, 512], P(None, 'dp'), may hold values from 0 to 258
- lengths: int32 [2, 16], P(None, 'dp'), may hold values from 33 to 512, as said below
- groups: int32 [2, 16], P(None, 'dp'), may hold values from 0 to 15
- embedding: float32 [259, 768], P(None, ('section', 'dp')), may hold values from -6 to 6
- language: float32 [16, 768], P(None, ('section', 'dp')), may hold values from -3 to 3
- scorer: float32 [768], P(('section', 'dp')), may hold values from -0.21875 to 0.21875
- prenorm: float32 [768], P(('section', 'dp')), may hold values from 0.5 to 1.5
- query_weight: float32 [768, 768], P(('section', 'dp')), may hold values from -0.109375 to 0.109375
- key_weight: float32 [768, 768], P(('section', 'dp')), may hold values from -0.109375 to 0.109375
- value_weight: float32 [768, 768], P(('section', 'dp')), may hold values from -0.21875 to 0.21875
- output_weight: float32 [768, 768], P(('section', 'dp')), may hold values from -1.75 to 1.75
- midnorm: float32 [768], P(('section', 'dp')), may hold values from 0.5 to 1.5
- gate_weight: float32 [768, 2048], P(('section', 'dp')), may hold values from -0.21875 to 0.21875
- up_weight: float32 [768, 2048], P(('section', 'dp')), may hold values from -0.21875 to 0.21875
- down_weight: float32 [2048, 768], P(('section', 'dp')), may hold values from -0.125 to 0.125
- relative: float32 [32, 12], replicated, may hold values from -4 to 4
- cotangent: bfloat16 [2, 16, 256, 768], P(None, 'dp'), may hold values from -6 to 6
Outputs:
- encoded: bfloat16 [2, 16, 256, 768], P(None, 'dp', None, 'section')
- embedding_grad: float32 [259, 768], P(None, ('section', 'dp'))
- language_grad: float32 [16, 768], P(None, ('section', 'dp'))
- scorer_grad: float32 [768], P(('section', 'dp'))
- prenorm_grad: float32 [768], P(('section', 'dp'))
- query_grad: float32 [768, 768], P(('section', 'dp'))
- key_grad: float32 [768, 768], P(('section', 'dp'))
- value_grad: float32 [768, 768], P(('section', 'dp'))
- output_grad: float32 [768, 768], P(('section', 'dp'))
- midnorm_grad: float32 [768], P(('section', 'dp'))
- gate_grad: float32 [768, 2048], P(('section', 'dp'))
- up_grad: float32 [768, 2048], P(('section', 'dp'))
- down_grad: float32 [2048, 768], P(('section', 'dp'))
- relative_grad: float32 [32, 12], replicated
The draws below stay inside these ranges and needn't reach their ends.
Inputs may be any that keep to these rules, and one draw needn't show every extreme that they name: `lengths`: some row has 512 bytes.
All inputs are finite; a program needn't handle non-finite values.
Results may differ from the reference program's by a relative error of at most 0.014.
The reference program's roundings to bfloat16 on the way count: a program that leaves them out, or rounds other values in their place, can miss the bound.
Values may be sent and summed in bfloat16 or wider, within the bound.
A program may use at most 256 MiB of HBM per device.

```python
import jax
import jax.numpy as jnp
from jax import lax

D = 768
HEADS = 12
HEAD_DIM = 64
FF = 2048
VOCAB = 259
LANGS = 16
BUCKETS = 32
BLOCKS = 4
DOWN = 2
BYTES = 512
MICRO = 2
TOK = 256
ROWS = 16


def draw_lengths(key, part):
    first_key = jax.random.fold_in(key, 11)
    second_key = jax.random.fold_in(key, 23)
    divisor = jax.random.randint(first_key, (MICRO, ROWS), 1, 9)
    jitter = jax.random.randint(second_key, (MICRO, ROWS), 0, BYTES // 16)
    drawn = BYTES // divisor - jitter
    marker = jnp.zeros((MICRO, ROWS), jnp.int32).at[0, 0].set(1)
    return jnp.where(marker > 0, BYTES, drawn).astype(jnp.int32)


def place_ends(array, rng, smallest, high):
    dims = array.shape
    spot = [jax.random.randint(jax.random.fold_in(rng, axis), (), 0, dims[axis]) for axis in range(len(dims))]
    array = array.at[tuple(spot)].set(smallest)
    longest = dims.index(max(dims))
    spot[longest] = (spot[longest] + 1) % dims[longest]
    return array.at[tuple(spot)].set(high)


def levels(key, dims, shards, smallest, high):
    level, own = 1.0, jax.random.fold_in(key, 6)
    for axis_at, parts in shards:
        draws = jnp.exp(jax.random.uniform(jax.random.fold_in(own, axis_at), (parts,), jnp.float32, smallest / len(shards), high / len(shards)))
        level = level * jnp.repeat(draws, dims[axis_at] // parts).reshape([-1 if axis == axis_at else 1 for axis in range(len(dims))])
    return level


def bell_draw(rng, extent, deviation, most, split=(), held_as=jnp.bfloat16):
    entries = deviation * jax.random.normal(rng, extent, jnp.float32)
    if split:
        entries = entries * levels(rng, extent, split, -0.22, 0.18)
    return jnp.clip(entries, -most, most).astype(held_as)


def setup_inputs(seed: int = 0) -> dict:
    arg_keys = jax.random.split(jax.random.key(seed), 18)
    byte_ids = place_ends(jax.random.randint(arg_keys[0], (MICRO, ROWS, BYTES), 0, VOCAB), jax.random.fold_in(arg_keys[0], 1), 0, VOCAB - 1).astype(jnp.int32)
    lengths = draw_lengths(jax.random.fold_in(arg_keys[17], 71), 0)
    groups = place_ends(jax.random.randint(arg_keys[2], (MICRO, ROWS), 0, LANGS), jax.random.fold_in(arg_keys[2], 1), 0, LANGS - 1).astype(jnp.int32)
    embedding = bell_draw(arg_keys[3], (VOCAB, D), 1.0, 6.0, ((1, 32),), jnp.float32)
    language = bell_draw(arg_keys[4], (LANGS, D), 0.5, 3.0, ((1, 32),), jnp.float32)
    scorer = bell_draw(arg_keys[5], (D,), D ** -0.5, 0.21875, ((0, 32),), jnp.float32)
    prenorm = jnp.clip(1.0 + 0.1 * jax.random.normal(arg_keys[6], (D,), jnp.float32), 0.5, 1.5)
    query_weight = bell_draw(arg_keys[7], (D, D), (4 * D) ** -0.5, 0.109375, ((0, 32),), jnp.float32)
    key_weight = bell_draw(arg_keys[8], (D, D), (4 * D) ** -0.5, 0.109375, ((0, 32),), jnp.float32)
    value_weight = bell_draw(arg_keys[9], (D, D), D ** -0.5, 0.21875, ((0, 32),), jnp.float32)
    output_weight = bell_draw(arg_keys[10], (D, D), (D // HEAD_DIM) ** -0.5, 1.75, ((0, 32),), jnp.float32)
    midnorm = jnp.clip(1.0 + 0.1 * jax.random.normal(arg_keys[11], (D,), jnp.float32), 0.5, 1.5)
    gate_weight = bell_draw(arg_keys[12], (D, FF), D ** -0.5, 0.21875, ((0, 32),), jnp.float32)
    up_weight = bell_draw(arg_keys[13], (D, FF), D ** -0.5, 0.21875, ((0, 32),), jnp.float32)
    down_weight = bell_draw(arg_keys[14], (FF, D), FF ** -0.5, 0.125, ((0, 32),), jnp.float32)
    relative = bell_draw(arg_keys[15], (BUCKETS, HEADS), 1.0, 4.0, (), jnp.float32)
    cotangent = bell_draw(arg_keys[16], (MICRO, ROWS, TOK, D), 1.0, 6.0, ((1, 16),))
    return dict(byte_ids=byte_ids, lengths=lengths, groups=groups, embedding=embedding, language=language, scorer=scorer, prenorm=prenorm, query_weight=query_weight, key_weight=key_weight, value_weight=value_weight, output_weight=output_weight, midnorm=midnorm, gate_weight=gate_weight, up_weight=up_weight, down_weight=down_weight, relative=relative, cotangent=cotangent)


HIGHEST = lax.Precision.HIGHEST
EPSILON = 1e-06
NEGATIVE = -1000000000.0
LIMITS = (12, 16, 23, 32, 46, 64, 91)

@jax.custom_vjp
def low(v):
    return lax.optimization_barrier(v.astype(jnp.bfloat16)).astype(jnp.float32)

@jax.custom_vjp
def low_back(v):
    return v

def low_keep(v):
    return (low(v), None)

def low_pass(kept, grad):
    return (grad,)

def back_keep(v):
    return (v, None)

def back_low(kept, grad):
    return (low(grad),)
low.defvjp(low_keep, low_pass)
low_back.defvjp(back_keep, back_low)

def bucket_ids(offsets):
    distance = jnp.abs(offsets)
    larger = 8 + sum(((distance >= limit).astype(jnp.int32) for limit in LIMITS))
    inside = jnp.where(distance < 8, distance, larger)
    return jnp.where(offsets > 0, 16, 0).astype(jnp.int32) + inside

def tokenize(table, language, scorer, symbols, length, group):
    count = symbols.shape[1]
    positions = jnp.arange(count)
    valid = positions[None, :] < length[:, None]
    gathered = jnp.take(table, symbols, axis=0) + jnp.take(language, group, axis=0)[:, None, :]
    embedded = jnp.where(valid[:, :, None], gathered, 0.0)
    means = []
    scores = []
    for size in range(1, BLOCKS + 1):
        extra = -count % size
        padded = jnp.pad(embedded, ((0, 0), (0, extra), (0, 0)))
        pooled = padded.reshape(padded.shape[0], -1, size, padded.shape[2]).sum(2) / size
        rated = jnp.einsum('rjd,d->rj', pooled, scorer, precision=HIGHEST)
        means.append(jnp.repeat(pooled, size, axis=1)[:, :count])
        scores.append(jnp.repeat(rated, size, axis=1)[:, :count])
    chosen = jax.nn.softmax(jnp.stack(scores, -1), axis=-1)
    latent = sum((chosen[..., index, None] * means[index] for index in range(BLOCKS)))
    return latent.reshape(latent.shape[0], count // DOWN, DOWN, latent.shape[2]).mean(2)

def rms_scale(values, gain):
    return values * lax.rsqrt(lax.optimization_barrier(jnp.mean(values * values, -1, keepdims=True)) + EPSILON) * gain

def gelu_tanh(values):
    return jax.nn.gelu(values, approximate=True)

def encode(hidden, valid, weights, relative):
    prenorm, query_w, key_w, value_w, output_w, midnorm, gate_w, up_w, down_w = weights
    tokens = hidden.shape[0]
    normed = low(rms_scale(hidden, prenorm))

    def heads_of(matrix):
        projected = jnp.dot(normed, matrix, precision=HIGHEST)
        return low(low_back(projected)).reshape(tokens, HEADS, HEAD_DIM)
    queries = heads_of(query_w)
    keys = heads_of(key_w)
    values = heads_of(value_w)
    offsets = jnp.arange(tokens)[None, :] - jnp.arange(tokens)[:, None]
    bias = jnp.transpose(relative[bucket_ids(offsets)], (2, 0, 1))
    scores = jnp.einsum('qhe,khe->hqk', queries, keys, precision=HIGHEST) + bias
    scores = low_back(scores)
    scores = jnp.where(valid[None, None, :], scores, NEGATIVE)
    softmaxed = low(jax.nn.softmax(scores, axis=-1))
    mixed = jnp.einsum('hqk,khe->qhe', softmaxed, values, precision=HIGHEST)
    mixed = low(low_back(mixed)).reshape(tokens, HEADS * HEAD_DIM)
    middle = hidden + low_back(jnp.dot(mixed, output_w, precision=HIGHEST))
    second = low(rms_scale(middle, midnorm))
    gate = low_back(jnp.dot(second, gate_w, precision=HIGHEST))
    upper = low_back(jnp.dot(second, up_w, precision=HIGHEST))
    product = low(gelu_tanh(gate) * upper)
    return middle + jnp.dot(product, down_w, precision=HIGHEST)

def forward(params, symbols, length, group):
    rounded = tuple((low(item) for item in params[:12]))
    latent = tokenize(rounded[0], rounded[1], rounded[2], symbols[None], length[None], group[None])[0]
    hidden = low(low_back(latent))
    valid = jnp.arange(TOK) * DOWN < length
    return encode(hidden, valid, rounded[3:12], params[12])

def reference(byte_ids, lengths, groups, embedding, language, scorer, prenorm, query_weight, key_weight, value_weight, output_weight, midnorm, gate_weight, up_weight, down_weight, relative, cotangent):
    params = tuple((item.astype(jnp.float32) for item in (embedding, language, scorer, prenorm, query_weight, key_weight, value_weight, output_weight, midnorm, gate_weight, up_weight, down_weight, relative)))
    symbols_all = byte_ids.reshape(MICRO * ROWS, BYTES)
    length_all = lengths.reshape(MICRO * ROWS)
    group_all = groups.reshape(MICRO * ROWS)
    upstream_all = cotangent.reshape(MICRO * ROWS, TOK, D)

    def one_row(total, item):
        symbols, length, group, upstream = item

        def local(values):
            return forward(values, symbols, length, group)
        result, pullback = jax.vjp(local, params)
        grads = pullback(upstream.astype(jnp.float32))[0]
        return (jax.tree.map(jnp.add, total, grads), result.astype(jnp.bfloat16))
    zeros = tuple((jnp.zeros(item.shape, jnp.float32) for item in params))
    total, encoded = lax.scan(one_row, zeros, (symbols_all, length_all, group_all, upstream_all))
    encoded = encoded.reshape(MICRO, ROWS, TOK, D)
    return (encoded, total[0], total[1], total[2], total[3], total[4], total[5], total[6], total[7], total[8], total[9], total[10], total[11], total[12])
```

```python
import functools

import jax
import jax.numpy as jnp
from jax import lax
from jax.experimental import pallas as pl
from jax.experimental.pallas import tpu as pltpu
from jax.sharding import PartitionSpec as P

BLOCKS = 4
DOWN = 2
MICRO = 2
OUTER = 16
EPSILON = 1e-06
NEGATIVE = -1000000000.0
LIMITS = (12, 16, 23, 32, 46, 64, 91)
MESH = pl.DeviceIdType.MESH
BF = jnp.bfloat16
F32 = jnp.float32
I32 = jnp.int32

ELT, QKV, WO, GATE, UP, DOWNW = range(6)
ALL = (ELT, QKV, WO, GATE, UP, DOWNW)
VOC = 288
SCORER = 19


def dot(a, b):
    return lax.dot_general(a, b, (((1,), (0,)), ((), ())), preferred_element_type=F32)


def dot_nt(a, b):
    return lax.dot_general(a, b, (((1,), (1,)), ((), ())), preferred_element_type=F32)


def dot_tn(a, b):
    return lax.dot_general(a, b, (((0,), (0,)), ((), ())), preferred_element_type=F32)


def split3(x):
    hi = x.astype(BF)
    rest = x - hi.astype(F32)
    mid = rest.astype(BF)
    return hi, mid, (rest - mid.astype(F32)).astype(BF)


def iota(shape, axis):
    return lax.broadcasted_iota(I32, shape, axis)


def bucket_ids(offsets):
    distance = jnp.abs(offsets)
    larger = 8 + sum(((distance >= limit).astype(I32) for limit in LIMITS))
    inside = jnp.where(distance < 8, distance, larger)
    return jnp.where(offsets > 0, 16, 0).astype(I32) + inside


class Net:
    def __init__(self, inner, w, g, sb, x1, y1, zi, ch, tmp, fo, sems):
        self.w, self.g, self.sb, self.x1, self.y1 = w, g, sb, x1, y1
        self.zi, self.ch, self.tmp, self.fo = zi, ch, tmp, fo
        self.ag_s, self.ag_r, self.rs_s, self.rs_r, self.mi_s, self.mi_r = sems
        self.s = lax.axis_index("section")
        self.d = lax.axis_index("dp")
        outer = self.d // inner
        self.z = outer // 4
        self.yx = outer % 4
        y, x = self.yx // 2, self.yx % 2
        self.sib = (1 - self.s, self.d)
        self.yx_x = self.yx + 1 - 2 * x
        self.yx_y = self.yx + 2 - 4 * y
        self.yx_d = 3 - self.yx
        self.xn = (self.s, self.d + (1 - 2 * x) * inner)
        self.yn = (self.s, self.d + (1 - 2 * y) * 2 * inner)
        self.zz = [(self.z + k) % 4 for k in (1, 2, 3)]
        self.zn = [(self.s, self.d + (zz - self.z) * 4 * inner) for zz in self.zz]
        self.sent = []

    def barrier(self):
        barrier = pltpu.get_barrier_semaphore()
        for device in (self.sib, self.xn, self.yn, *self.zn):
            pl.semaphore_signal(barrier, inc=1, device_id=device, device_id_type=MESH)
        pl.semaphore_wait(barrier, 6)

    def copy(self, src, dst, send, recv, device):
        return pltpu.make_async_remote_copy(
            src_ref=src, dst_ref=dst, send_sem=send, recv_sem=recv,
            device_id=device, device_id_type=MESH,
        )

    def start(self, copy):
        copy.start()
        self.sent.append(copy)

    def finish(self):
        for copy in self.sent:
            copy.wait_send()
        self.sent = []

    def blk(self, ref, m, h, z, yx):
        return ref.at[h, :, z, yx] if m == DOWNW else ref.at[h, z, yx]

    def grp(self, ref, m, h, yx):
        return ref.at[h, :, :, yx] if m == DOWNW else ref.at[h, :, yx]

    def part(self, ref, m, h, z0, yx):
        return ref.at[h, :, pl.ds(z0, 2), yx] if m == DOWNW else ref.at[h, pl.ds(z0, 2), yx]

    def xy2(self, m):
        if m == DOWNW:
            return self.sb[m].at[0, pl.ds(0, 2)], self.sb[m].at[0, pl.ds(2, 2)]
        return self.sb[m].at[0], self.sb[m].at[1]

    def ag(self, m, slot):
        w, s = self.w[m], self.s
        pair = lambda src, dst, dev: self.copy(src, dst, self.ag_s.at[m, slot], self.ag_r.at[m, slot], dev)
        if slot == 0:
            if m == DOWNW:
                dst = self.ch[m].at[s]
            else:
                rows = self.tmp[m].shape[0]
                dst = self.ch[m].at[pl.ds(s * rows, rows)]
            return pair(self.tmp[m], dst, self.sib)
        if slot <= 3:
            ref = self.blk(w, m, s, self.z, self.yx)
            return pair(ref, ref, self.zn[slot - 1])
        if slot <= 5:
            ref = self.grp(w, m, s, self.yx)
            return pair(ref, ref, self.xn if slot == 4 else self.yn)
        if slot == 6:
            ref = self.part(w, m, s, 0, self.yx_x)
            return pair(ref, ref, self.yn)
        if slot == 7:
            ref = self.part(w, m, s, 2, self.yx_y)
            return pair(ref, ref, self.xn)
        ref = self.grp(w, m, s, (self.yx, self.yx_x, self.yx_y, self.yx_d)[slot - 8])
        return pair(ref, ref, self.sib)

    def ag0(self, m):
        self.start(self.ag(m, 0))

    def ag1(self, m):
        self.ag(m, 0).wait_recv()
        chunk = self.ch[m][...].astype(BF)
        if m == DOWNW:
            for sec in (0, 1):
                self.w[m][self.s, sec, self.z, self.yx] = chunk[sec]
        else:
            self.w[m][self.s, self.z, self.yx] = chunk
        for slot in (1, 2, 3):
            self.start(self.ag(m, slot))

    def ag2(self, m):
        for slot in (1, 2, 3):
            self.ag(m, slot).wait_recv()
        for slot in (4, 5, 8):
            self.start(self.ag(m, slot))

    def ag3(self, m):
        self.ag(m, 4).wait_recv()
        for slot in (6, 9):
            self.start(self.ag(m, slot))
        self.ag(m, 5).wait_recv()
        for slot in (7, 10):
            self.start(self.ag(m, slot))

    def ag4(self, m):
        for slot in (6, 7):
            self.ag(m, slot).wait_recv()
        self.start(self.ag(m, 11))

    def ag5(self, m):
        for slot in (8, 9, 10, 11):
            self.ag(m, slot).wait_recv()

    def rs(self, m, slot):
        g, s = self.g[m], self.s
        pair = lambda src, dst, dev: self.copy(src, dst, self.rs_s.at[m, slot], self.rs_r.at[m, slot], dev)
        if slot == 0:
            return pair(g.at[1 - s], self.sb[m], self.sib)
        if slot == 1:
            return pair(self.part(g, m, s, 0, self.yx_d), self.x1[m], self.xn)
        if slot == 2:
            return pair(self.part(g, m, s, 2, self.yx_d), self.y1[m], self.yn)
        if slot == 3:
            return pair(self.grp(g, m, s, self.yx_x), self.xy2(m)[0], self.xn)
        if slot == 4:
            return pair(self.grp(g, m, s, self.yx_y), self.xy2(m)[1], self.yn)
        if slot <= 7:
            k = slot - 5
            return pair(self.blk(g, m, s, self.zz[k], self.yx), self.zi[m].at[k], self.zn[k])
        if m == DOWNW:
            src = self.ch[m].at[1 - s]
        else:
            rows = self.fo[m].shape[0]
            src = self.ch[m].at[pl.ds((1 - s) * rows, rows)]
        return pair(src, self.fo[m], self.sib)

    def rs0(self, m):
        self.start(self.rs(m, 0))

    def rs1(self, m):
        self.rs(m, 0).wait_recv()
        g, sb, s = self.g[m], self.sb[m], self.s

        def add(i, carry):
            if m == DOWNW:
                at = (i // 4, i % 4)
                g[s, at[0], at[1]] = (g[s, at[0], at[1]].astype(F32) + sb[at[0], at[1]].astype(F32)).astype(BF)
            else:
                g[s, i // 4, i % 4] = (g[s, i // 4, i % 4].astype(F32) + sb[i // 4, i % 4].astype(F32)).astype(BF)
            return carry

        lax.fori_loop(0, 8 if m == DOWNW else 16, add, 0)
        self.start(self.rs(m, 1))
        self.start(self.rs(m, 2))

    def rs2(self, m):
        g, s = self.g[m], self.s
        for slot, ref, z0, yx in ((1, self.x1[m], 0, self.yx_y), (2, self.y1[m], 2, self.yx_x)):
            self.rs(m, slot).wait_recv()
            for j in (0, 1):
                if m == DOWNW:
                    for sec in (0, 1):
                        mine = g[s, sec, z0 + j, yx].astype(F32)
                        g[s, sec, z0 + j, yx] = (mine + ref[sec, j].astype(F32)).astype(BF)
                else:
                    mine = g[s, z0 + j, yx].astype(F32)
                    g[s, z0 + j, yx] = (mine + ref[j].astype(F32)).astype(BF)
        self.start(self.rs(m, 3))
        self.start(self.rs(m, 4))

    def rs3(self, m):
        self.rs(m, 3).wait_recv()
        self.rs(m, 4).wait_recv()
        g, s, yx = self.g[m], self.s, self.yx
        a, b = self.xy2(m)

        def total(sec, z):
            if m == DOWNW:
                return g[s, sec, z, yx].astype(F32) + a[sec, z].astype(F32) + b[sec, z].astype(F32)
            return g[s, z, yx].astype(F32) + a[z].astype(F32) + b[z].astype(F32)

        for slot in (5, 6, 7):
            zz = self.zz[slot - 5]
            if m == DOWNW:
                for sec in (0, 1):
                    g[s, sec, zz, yx] = total(sec, zz).astype(BF)
            else:
                g[s, zz, yx] = total(0, zz).astype(BF)
            self.start(self.rs(m, slot))
        if m == DOWNW:
            for sec in (0, 1):
                self.ch[m][sec] = total(sec, self.z)
        else:
            self.ch[m][...] = total(0, self.z)

    def rs4(self, m):
        for slot in (5, 6, 7):
            self.rs(m, slot).wait_recv()
        zi = self.zi[m]
        self.ch[m][...] += zi[0].astype(F32) + zi[1].astype(F32) + zi[2].astype(F32)
        self.start(self.rs(m, 8))

    def rs5(self, m):
        if m == DOWNW:
            mine = self.ch[m][self.s]
        else:
            rows = self.fo[m].shape[0]
            mine = self.ch[m][pl.ds(self.s * rows, rows)]
        self.rs(m, 8).wait_recv()
        return mine, self.fo[m][...]


def kernel(inner, sizes, *refs):
    (ints, rel, elt, wq, wk, wv, wo, wi0, wi1, wd, cot) = refs[:11]
    (enc_out, g_elt, g_q, g_k, g_v, g_o, g_0, g_1, g_d, g_rel) = refs[11:21]
    rest = refs[21:]
    take = lambda k: rest[6 * k : 6 * k + 6]
    w, g, sb, x1, y1, zi, ch, tmp, fo = (take(k) for k in range(9))
    rest = rest[54:]
    sems, rest = rest[:6], rest[6:]
    (pi, cb, prow, gthi, gtlo, rows_ref, hid, nrm, qs, ks, vs, bvec, pmat, mixed, mixp, mid, sec_ref,
     acc, encb, dq, dk, dv, dvec, relbuf, relin, cp) = rest
    tokens, width, half, ffh = sizes
    net = Net(inner, w, g, sb, x1, y1, zi, ch, tmp, fo, sems)
    s = net.s
    net.barrier()

    def lanes(ref, h, n):
        return ref[:, pl.ds(pl.multiple_of(h * n, 128), n)]

    pi[...] = jnp.where(iota((width, width), 0) == ints[3:4, :], 1.0, 0.0).astype(BF)

    wo_p = dot(wo[...].astype(BF), pi[...])
    wd_p = dot(wd[...].astype(BF), pi[...])
    rows_d, rows_f = elt.shape[0], wd.shape[0]
    fo_wo, fo_wd = fo[WO], fo[DOWNW]

    def halves(m, h):
        if m == ELT:
            return lanes(elt, h, 256)
        if m == QKV:
            return jnp.concatenate([lanes(r, h, half) for r in (wq, wk, wv)], axis=1)
        if m == GATE:
            return lanes(wi0, h, ffh)
        if m == UP:
            return lanes(wi1, h, ffh)
        value = wo_p if m == WO else wd_p
        return jnp.where(h == 0, value[:, :half], value[:, half:])

    for m in ALL:
        tmp[m][...] = halves(m, 1 - s)
        net.ag0(m)
        own = halves(m, s)
        if m == DOWNW:
            ch[m][s] = own
        else:
            ch[m][pl.ds(s * rows_d, rows_d)] = own
    for m in ALL:
        net.ag1(m)
    steps = (net.ag2, net.ag3, net.ag4, net.ag5)
    for t in range(len(ALL) + 3):
        for k, step in enumerate(steps):
            if 0 <= t - k < len(ALL):
                step(ALL[t - k])

    def wmat(m, h):
        return w[m][h].reshape(width, w[m].shape[-1])

    def gput(m, h, value):
        g[m][h] = value.astype(BF).reshape(g[m].shape[1:])

    cp[...] = dot(cot[s], pi[...]).astype(BF)

    span = 2 * tokens
    ohb = jnp.where(iota((128, span), 0) == bucket_ids(iota((128, span), 1) - (tokens - 1)), 1.0, 0.0).astype(BF)
    bv = sum(dot(part, ohb) for part in split3(rel[...]))
    heads = bvec.shape[0]
    for h in range(heads):
        bvec[h] = bv[h : h + 1, :]

    count = span
    ids, length, group = ints[0:1, :count], ints[1:2, :count], ints[2:3, :count]
    col = iota((1, count), 1)
    pos = jnp.where(col < tokens, 2 * col, 2 * (col - tokens) + 1)
    valid = pos < length
    symbol = iota((VOC, count), 0)
    onehot = jnp.where(((symbol == ids) | (symbol == group + 259)) & valid, 1.0, 0.0)
    cb[0] = onehot.astype(BF)

    def block_of(p, size):
        return p if size == 1 else p >> 1 if size == 2 else (p * 21846) >> 16 if size == 3 else p >> 2

    rowi = iota((count, 1), 0)
    posc = jnp.where(rowi < tokens, 2 * rowi, 2 * (rowi - tokens) + 1)
    for size in (2, 3, 4):
        pool = jnp.where(block_of(posc, size) == block_of(pos, size), 1.0, 0.0).astype(BF)
        cb[size - 1] = dot(cb[0], pool).astype(BF)

    e0, e1 = wmat(ELT, 0), wmat(ELT, 1)[:, :128]
    picks = jnp.where(iota((8, 128), 1) == iota((8, 128), 0) + SCORER, 1.0, 0.0).astype(BF)
    rows_ref[...] = dot_nt(picks, e1)
    g1, g2 = rows_ref[1:2, :], rows_ref[2:3, :]
    ew = jnp.concatenate([dot_tn(e0, e1), dot_tn(e1, e1)[: VOC - 256]], axis=0)[:, SCORER : SCORER + 1]
    ratings = [jnp.sum(cb[b].astype(F32) * ew, axis=0, keepdims=True) / (b + 1) for b in range(BLOCKS)]
    top = functools.reduce(jnp.maximum, ratings)
    raised = [jnp.exp(r - top) for r in ratings]
    total = sum(raised)
    chosen = [r / total for r in raised]
    mixw = 0.0
    for b in range(BLOCKS):
        prow[b : b + 1, :] = chosen[b]
        mixw = mixw + cb[b].astype(F32) * (chosen[b] / (2.0 * (b + 1)))
    gt = mixw[:, :tokens] + mixw[:, tokens:]
    gt = jnp.concatenate([gt, jnp.zeros((384 - VOC, tokens), F32)], axis=0).T
    gthi[...] = gt.astype(BF)
    gtlo[...] = (gt - gt.astype(BF).astype(F32)).astype(BF)
    latent = (
        dot_nt(gthi[:, :256], e0) + dot_nt(gthi[:, 256:], e1)
        + dot_nt(gtlo[:, :256], e0) + dot_nt(gtlo[:, 256:], e1)
    )
    hid[...] = latent.astype(BF)

    hidden = hid[...].astype(F32)
    r1 = lax.rsqrt(jnp.mean(hidden * hidden, -1, keepdims=True) + EPSILON)
    nrm[...] = (hidden * r1 * g1).astype(BF)
    for h in (0, 1):
        for j, ref in enumerate((qs, ks, vs)):
            out = dot(nrm[...], w[QKV][h, :, :, :, j * half : (j + 1) * half].reshape(width, half)).astype(BF)
            for i in range(half // 128):
                ref[h * (half // 128) + i] = out[:, i * 128 : (i + 1) * 128]

    tcol = iota((1, tokens), 1)
    valid_key = DOWN * tcol < ints[1:2, :tokens]
    lane = iota((1, 128), 1)
    masks = [jnp.where(lane < 64, 1.0 - e, float(e)).astype(BF) for e in (0, 1)]

    def forward_pair(i, carry):
        q2, k2, v2 = qs[i], ks[i], vs[i]
        out = 0.0
        for e in (0, 1):
            h = 2 * i + e
            line = jnp.broadcast_to(bvec[h], (tokens, span))
            bias = pltpu.roll(line, tokens + 1, 1, stride=1, stride_axis=0)[:, :tokens]
            scores = jnp.where(valid_key, dot_nt(q2, k2 * masks[e]) + bias, NEGATIVE)
            up = jnp.exp(scores - jnp.max(scores, -1, keepdims=True))
            prob = up * (1.0 / jnp.sum(up, -1, keepdims=True))
            pmat[h] = prob
            out = out + dot(prob.astype(BF), v2 * masks[e])
        mixed[:, pl.ds(pl.multiple_of(i * 128, 128), 128)] = out.astype(BF)
        return carry

    lax.fori_loop(0, width // 128, forward_pair, 0)
    mixp[...] = dot(mixed[...], pi[...]).astype(BF)
    for h in (0, 1):
        cols = slice(h * half, (h + 1) * half)
        mid[:, cols] = hid[:, cols].astype(F32) + dot(mixp[...], wmat(WO, h))
    middle = mid[...]
    r2 = lax.rsqrt(jnp.mean(middle * middle, -1, keepdims=True) + EPSILON)
    sec_ref[...] = (middle * r2 * g2).astype(BF)

    acc[...] = jnp.zeros_like(acc)
    encb[...] = mid[...]

    def feed(i, carry):
        h = i // 4
        cols = pl.ds(pl.multiple_of((i % 4) * 256, 256), 256)
        wg = w[GATE][h, :, :, :, cols].reshape(width, 256)
        wu = w[UP][h, :, :, :, cols].reshape(width, 256)
        wdn = [w[DOWNW][j, h, i % 4].reshape(256, half) for j in (0, 1)]
        gate, upper = dot(sec_ref[...], wg), dot(sec_ref[...], wu)
        pdelta = dot_nt(cp[:, :half], wdn[0]) + dot_nt(cp[:, half:], wdn[1])
        square = gate * gate
        tanh = jnp.tanh(0.7978845608 * (gate + 0.044715 * square * gate))
        act = 0.5 * gate * (1.0 + tanh)
        slope = 0.5 * (1.0 + tanh) + 0.5 * gate * (1.0 - tanh * tanh) * 0.7978845608 * (1.0 + 0.134145 * square)
        product = (act * upper).astype(BF)
        gdelta = (pdelta * upper * slope).astype(BF)
        udelta = (pdelta * act).astype(BF)
        g[GATE][h, :, :, :, cols] = dot_tn(sec_ref[...], gdelta).astype(BF).reshape(4, 4, -1, 256)
        g[UP][h, :, :, :, cols] = dot_tn(sec_ref[...], udelta).astype(BF).reshape(4, 4, -1, 256)
        for j in (0, 1):
            out = slice(j * half, (j + 1) * half)
            g[DOWNW][j, h, i % 4] = dot_tn(product, cp[:, out]).astype(BF).reshape(4, -1, half)
            encb[:, out] += dot(product, wdn[j])
        acc[...] += dot_nt(gdelta, wg) + dot_nt(udelta, wu)
        return carry

    lax.fori_loop(0, 8, feed, 0)

    encoded = dot_nt(encb[...].astype(BF), pi[...]).astype(BF)
    for h in (0, 1):
        mixed[:, h * half : (h + 1) * half] = encoded[:, h * half : (h + 1) * half]
    enc_out[s] = lanes(mixed, s, half)
    enc_copy = net.copy(
        mixed.at[:, pl.ds(pl.multiple_of((1 - s) * half, 128), half)], enc_out.at[s],
        net.mi_s.at[0], net.mi_r.at[0], net.sib,
    )
    net.start(enc_copy)

    middle = mid[...]
    r2 = lax.rsqrt(jnp.mean(middle * middle, -1, keepdims=True) + EPSILON)
    n2 = middle * r2
    sdelta = acc[...]
    scaled = sdelta * g2
    mid_grad = jnp.sum(sdelta * n2, axis=0, keepdims=True)
    mdel = encb
    mdel[...] = cp[...].astype(F32) + r2 * (scaled - n2 * jnp.mean(scaled * n2, -1, keepdims=True))
    adel = mdel[...].astype(BF)
    sec_ref[...] = adel
    for h in (0, 1):
        gput(WO, h, dot_tn(mixp[...], sec_ref[:, h * half : (h + 1) * half]))
    back = dot_nt(sec_ref[:, :half], wmat(WO, 0)) + dot_nt(sec_ref[:, half:], wmat(WO, 1))
    mixp[...] = dot_nt(back.astype(BF), pi[...]).astype(BF)

    flip = jnp.where(iota((tokens, tokens), 0) + iota((tokens, tokens), 1) == tokens - 1, 1.0, 0.0).astype(BF)

    def backward_pair(i, carry):
        cols = pl.ds(pl.multiple_of(i * 128, 128), 128)
        q2, k2, v2, m2 = qs[i], ks[i], vs[i], mixp[:, cols]
        outq = outk = outv = 0.0
        for e in (0, 1):
            h = 2 * i + e
            prob = pmat[h]
            wdelta = dot_nt(m2, v2 * masks[e])
            lean = jnp.sum(prob * wdelta, -1, keepdims=True)
            sd = jnp.where(valid_key, prob * (wdelta - lean), 0.0).astype(BF)
            outq = outq + dot(sd, k2 * masks[e])
            outk = outk + dot_tn(sd, q2 * masks[e])
            outv = outv + dot_tn(prob.astype(BF), m2 * masks[e])
            turned = jnp.concatenate([dot(sd, flip), jnp.zeros((tokens, tokens), F32)], axis=1)
            skew = pltpu.roll(turned, 0, 1, stride=1, stride_axis=0)
            dvec[h] = jnp.sum(skew, axis=0, keepdims=True)
        dq[:, cols], dk[:, cols], dv[:, cols] = outq.astype(BF), outk.astype(BF), outv.astype(BF)
        return carry

    lax.fori_loop(0, width // 128, backward_pair, 0)

    norm_delta = 0.0
    for h in (0, 1):
        for j, ref in enumerate((dq, dk, dv)):
            part = ref[:, h * half : (h + 1) * half]
            cols = slice(j * half, (j + 1) * half)
            g[QKV][h, :, :, :, cols] = dot_tn(nrm[...], part).astype(BF).reshape(4, 4, -1, half)
            norm_delta = norm_delta + dot_nt(part, w[QKV][h, :, :, :, cols].reshape(width, half))
    hidden = hid[...].astype(F32)
    r1 = lax.rsqrt(jnp.mean(hidden * hidden, -1, keepdims=True) + EPSILON)
    n1 = hidden * r1
    scaled = norm_delta * g1
    pre_grad = jnp.sum(norm_delta * n1, axis=0, keepdims=True)
    hdel = (mdel[...] + r1 * (scaled - n1 * jnp.mean(scaled * n1, -1, keepdims=True))).astype(BF)

    back = jnp.concatenate([dot(hdel, e0), dot(hdel, e1)], axis=1).T[:VOC]
    back = jnp.concatenate([back, back], axis=1)
    pdel = [jnp.sum(cb[b].astype(F32) * back, axis=0, keepdims=True) / (2.0 * (b + 1)) for b in range(BLOCKS)]
    lean = sum(prow[b : b + 1, :] * pdel[b] for b in range(BLOCKS))
    flow = 0.0
    for b in range(BLOCKS):
        flow = flow + cb[b].astype(F32) * (prow[b : b + 1, :] * (pdel[b] - lean) / (b + 1))
    gs = jnp.sum(flow, axis=1, keepdims=True)
    lane_v = iota((VOC, 128), 1)
    parts = [p.astype(F32) for p in split3(gs)]
    gs3 = jnp.where(lane_v == 0, parts[0], jnp.where(lane_v == 1, parts[1], jnp.where(lane_v == 2, parts[2], 0.0)))
    gs3 = gs3.astype(BF)
    lane_w = iota((width, 128), 1)
    wcol = jnp.where(lane_w < 3, e1.astype(F32)[:, SCORER : SCORER + 1], 0.0).astype(BF)
    gput(ELT, 0, dot_tn(hdel, gthi[:, :256]) + dot_tn(hdel, gtlo[:, :256]) + dot_nt(wcol, gs3[:256]))
    gs_tail = jnp.concatenate([gs3[256:], jnp.zeros((128 + 256 - VOC, 128), BF)], axis=0)
    tail = dot_tn(hdel, gthi[:, 256:]) + dot_tn(hdel, gtlo[:, 256:]) + dot_nt(wcol, gs_tail)
    scorer_grad = jnp.sum(dot(e0, gs3[:256]) + dot(e1, gs_tail), axis=1, keepdims=True)
    gains = [p.astype(F32) for p in (*split3(pre_grad), *split3(mid_grad))]
    gains = jnp.concatenate([*gains, jnp.zeros((10, width), F32)], axis=0).astype(BF)
    place_row, place_col = iota((16, 128), 0), iota((16, 128), 1)
    place = (place_row < 6) & (place_col == jnp.where(place_row < 3, SCORER + 1, SCORER + 2))
    tail = tail + dot_tn(gains, jnp.where(place, 1.0, 0.0).astype(BF))
    tail = jnp.where(lane_w == SCORER, scorer_grad, tail)
    gput(ELT, 1, jnp.concatenate([tail, jnp.zeros((width, 128), F32)], axis=1))

    ohr = jnp.where(iota((128, span), 0) == bucket_ids((tokens - 1) - iota((128, span), 1)), 1.0, 0.0).astype(BF)
    lines = jnp.concatenate([dvec[h] for h in range(heads)] + [jnp.zeros((16 - heads, span), F32)], axis=0)
    relbuf[0] = sum(dot_nt(part, ohr) for part in split3(lines))

    def rel_copy(slot, level, device):
        return net.copy(relbuf.at[level], relin.at[slot], net.mi_s.at[1 + slot], net.mi_r.at[1 + slot], device)

    for level, partners in enumerate((((0, net.sib),), ((1, net.xn),), ((2, net.yn),), ((3, net.zn[0]), (4, net.zn[1]), (5, net.zn[2])))):
        for slot, device in partners:
            net.start(rel_copy(slot, level, device))
        for slot, device in partners:
            rel_copy(slot, level, device).wait_recv()
        if level < 3:
            relbuf[level + 1] = relbuf[level] + relin[level]
    place = [jnp.where(net.z == k, 1.0, 0.0) for k in range(4)]
    level = [relbuf[3], relin[3], relin[4], relin[5]]
    summed = 0.0
    for k in range(4):
        summed = summed + sum(place[z] * level[(z - k) % 4] for z in range(4))
    g_rel[...] = summed

    order = (DOWNW, UP, GATE, WO, QKV, ELT)
    for m in order:
        net.rs0(m)
    results = {}

    def last(m):
        results[m] = True
        mine, other = net.rs5(m)
        n = mine.shape[1]
        if m in (WO, DOWNW):
            first = jnp.where(s == 0, mine, other)
            second = jnp.where(s == 0, other, mine)
            both = jnp.concatenate([first, second], axis=1)
            out = g_o if m == WO else g_d
            out[...] = sum(dot_nt(part, pi[...]) for part in split3(both))
            return
        targets = {ELT: (g_elt,), QKV: (g_q, g_k, g_v), GATE: (g_0,), UP: (g_1,)}[m]
        n = n // len(targets)
        for j, ref in enumerate(targets):
            ref[:, pl.ds(pl.multiple_of(s * n, 128), n)] = mine[:, j * n : (j + 1) * n]
            ref[:, pl.ds(pl.multiple_of((1 - s) * n, 128), n)] = other[:, j * n : (j + 1) * n]

    steps = (net.rs1, net.rs2, net.rs3, net.rs4, last)
    for t in range(len(order) + 4):
        for k, step in enumerate(steps):
            if 0 <= t - k < len(order):
                step(order[t - k])
    enc_copy.wait_recv()
    net.finish()


def call(inner, ints, rel, elt, wq, wk, wv, wo, wi0, wi1, wd, cot):
    rows_d, width = wq.shape
    rows_f = wd.shape[0]
    half, ffh = width // 2, wi0.shape[1] // 2
    tokens = cot.shape[1]
    span = 2 * tokens
    heads = width // 64
    wide = {ELT: 256, QKV: 3 * half, WO: half, GATE: ffh, UP: ffh, DOWNW: half}
    chip = {m: (2, rows_f) if m == DOWNW else (2 * rows_d,) for m in ALL}

    def shape(m, lead, sec, tail):
        return (*lead, *((2,) if m == DOWNW and sec else ()), *tail)

    def full(m):
        return (2, 4, 4, rows_f, wide[m]) if m == DOWNW else (4, 4, 2 * rows_d, wide[m])

    def part(m):
        return (2, 2, rows_f, wide[m]) if m == DOWNW else (2, 2 * rows_d, wide[m])

    scratch = []
    scratch += [pltpu.VMEM((2, *full(m)), BF) for m in ALL]
    scratch += [pltpu.VMEM((2, *full(m)), BF) for m in ALL]
    scratch += [pltpu.VMEM(full(m), BF) for m in ALL]
    scratch += [pltpu.VMEM(part(m), BF) for m in ALL]
    scratch += [pltpu.VMEM(part(m), BF) for m in ALL]
    scratch += [pltpu.VMEM((3, *chip[m], wide[m]), BF) for m in ALL]
    scratch += [pltpu.VMEM((*chip[m], wide[m]), F32) for m in ALL]
    scratch += [pltpu.VMEM((chip[m][-1] if m == DOWNW else rows_d, wide[m]), F32) for m in ALL]
    scratch += [pltpu.VMEM((chip[m][-1] if m == DOWNW else rows_d, wide[m]), F32) for m in ALL]
    dma = pltpu.SemaphoreType.DMA
    scratch += [dma((6, 12)), dma((6, 12)), dma((6, 9)), dma((6, 9)), dma((7,)), dma((7,))]
    act = (tokens, width)
    scratch += [
        pltpu.VMEM((width, width), BF),
        pltpu.VMEM((BLOCKS, VOC, span), BF),
        pltpu.VMEM((8, span), F32),
        pltpu.VMEM((tokens, 384), BF),
        pltpu.VMEM((tokens, 384), BF),
        pltpu.VMEM((8, width), F32),
        pltpu.VMEM(act, BF),
        pltpu.VMEM(act, BF),
        pltpu.VMEM((width // 128, tokens, 128), BF),
        pltpu.VMEM((width // 128, tokens, 128), BF),
        pltpu.VMEM((width // 128, tokens, 128), BF),
        pltpu.VMEM((heads, 1, span), F32),
        pltpu.VMEM((heads, tokens, tokens), F32),
        pltpu.VMEM(act, BF),
        pltpu.VMEM(act, BF),
        pltpu.VMEM(act, F32),
        pltpu.VMEM(act, BF),
        pltpu.VMEM(act, F32),
        pltpu.VMEM(act, F32),
        pltpu.VMEM(act, BF),
        pltpu.VMEM(act, BF),
        pltpu.VMEM(act, BF),
        pltpu.VMEM((heads, 1, span), F32),
        pltpu.VMEM((4, 16, 128), F32),
        pltpu.VMEM((6, 16, 128), F32),
        pltpu.VMEM(act, BF),
    ]
    outs = [
        jax.ShapeDtypeStruct((MICRO, tokens, half), BF),
        jax.ShapeDtypeStruct(elt.shape, F32),
        *[jax.ShapeDtypeStruct(item.shape, F32) for item in (wq, wk, wv, wo, wi0, wi1, wd)],
        jax.ShapeDtypeStruct((16, 128), F32),
    ]
    vmem = pl.BlockSpec(memory_space=pltpu.VMEM)
    return pl.pallas_call(
        functools.partial(kernel, inner, (tokens, width, half, ffh)),
        out_shape=outs,
        in_specs=[vmem] * 11,
        out_specs=[vmem] * len(outs),
        scratch_shapes=scratch,
        compiler_params=pltpu.CompilerParams(
            collective_id=0, has_side_effects=True, vmem_limit_bytes=63 * 2**20
        ),
    )(ints, rel, elt, wq, wk, wv, wo, wi0, wi1, wd, cot)


def body(
    byte_ids, lengths, groups, embedding, language, scorer, prenorm, query_weight, key_weight, value_weight,
    output_weight, midnorm, gate_weight, up_weight, down_weight, relative, cotangent,
):
    section = lax.axis_index("section")
    inner = lax.axis_size("dp") // OUTER
    vocab, langs = embedding.shape[0], language.shape[0]
    table = jnp.concatenate([embedding, language, scorer[None], prenorm[None], midnorm[None]], axis=0)
    elt = jnp.pad(table, ((0, 512 - table.shape[0]), (0, 0))).T
    shards = [elt, query_weight, key_weight, value_weight, output_weight, gate_weight, up_weight, down_weight]
    teams = [[o * inner + i for i in range(inner)] for o in range(OUTER)]
    if inner > 1:
        shards = [lax.all_gather(item, "dp", axis_index_groups=teams, axis=0, tiled=True) for item in shards]
    width = query_weight.shape[1]
    rows = shards[1].shape[0]
    count = byte_ids.shape[2]
    place = jnp.arange(width)
    natural = (place % (2 * rows)) // rows * (width // 2) + place // (2 * rows) * rows + place % rows
    pick = lambda item: lax.dynamic_index_in_dim(item, section, 0, False)
    ids = pick(byte_ids)[0].reshape(count // 2, 2).T.reshape(count)
    fill = jnp.zeros((width - count,), jnp.int32)
    ints = jnp.stack(
        [
            jnp.concatenate([ids, fill]),
            jnp.broadcast_to(pick(lengths), (width,)),
            jnp.broadcast_to(pick(groups), (width,)),
            natural.astype(jnp.int32),
        ]
        + [jnp.zeros((width,), jnp.int32)] * 4
    )
    rel = jnp.pad(relative.T, ((0, 16 - relative.shape[1]), (0, 128 - relative.shape[0])))
    encoded, *grads, rel_grad = call(inner, ints, rel, *shards, cotangent[:, 0])
    if inner > 1:
        grads = [
            lax.psum_scatter(item, "dp", axis_index_groups=teams, scatter_dimension=0, tiled=True) for item in grads
        ]
        rel_grad = lax.psum(rel_grad, "dp", axis_index_groups=teams)
    table = grads[0].T
    gains = table[vocab + langs : vocab + langs + 3]
    return (
        encoded[:, None],
        table[:vocab],
        table[vocab : vocab + langs],
        gains[0],
        gains[1],
        *grads[1:5],
        gains[2],
        *grads[5:8],
        rel_grad[: relative.shape[1], : relative.shape[0]].T,
    )


def solution(mesh):
    both = ("section", "dp")
    wide = P(both, None)
    return jax.shard_map(
        body,
        mesh=mesh,
        in_specs=(
            P(None, "dp", None), P(None, "dp"), P(None, "dp"), P(None, both), P(None, both), P(both), P(both),
            wide, wide, wide, wide, P(both), wide, wide, wide, P(), P(None, "dp", None, None),
        ),
        out_specs=(
            P(None, "dp", None, "section"), P(None, both), P(None, both), P(both), P(both),
            wide, wide, wide, wide, P(both), wide, wide, wide, P(),
        ),
        check_vma=False,
    )
```

```python
import functools

import jax
import jax.numpy as jnp
from jax import lax
from jax.experimental import pallas as pl
from jax.experimental.pallas import tpu as pltpu
from jax.sharding import PartitionSpec as P

BLOCKS = 4
DOWN = 2
MICRO = 2
OUTER = 16
EPSILON = 1e-06
NEGATIVE = -1000000000.0
LIMITS = (12, 16, 23, 32, 46, 64, 91)
MESH = pl.DeviceIdType.MESH
BF = jnp.bfloat16
F32 = jnp.float32
I32 = jnp.int32

ELT, WQ, WK, WV, WO, DOWNW, GU0, GU1, GU2, GU3 = range(10)
GU = (GU0, GU1, GU2, GU3)
ALL = tuple(range(10))
N = len(ALL)
VOC = 288
SCORER = 19


def dot(a, b):
    return lax.dot_general(a, b, (((1,), (0,)), ((), ())), preferred_element_type=F32)


def dot_nt(a, b):
    return lax.dot_general(a, b, (((1,), (1,)), ((), ())), preferred_element_type=F32)


def dot_tn(a, b):
    return lax.dot_general(a, b, (((0,), (0,)), ((), ())), preferred_element_type=F32)


def split3(x):
    hi = x.astype(BF)
    rest = x - hi.astype(F32)
    mid = rest.astype(BF)
    return hi, mid, (rest - mid.astype(F32)).astype(BF)


def iota(shape, axis):
    return lax.broadcasted_iota(I32, shape, axis)


def over(value, n):
    return (value * (65536 // n + 1)) >> 16


def bucket_ids(offsets):
    distance = jnp.abs(offsets)
    larger = 8 + sum(((distance >= limit).astype(I32) for limit in LIMITS))
    inside = jnp.where(distance < 8, distance, larger)
    return jnp.where(offsets > 0, 16, 0).astype(I32) + inside


class Net:
    def __init__(self, inner, w, g, sb, x1, y1, zi, ch, tmp, fo, sems):
        self.w, self.g, self.sb, self.x1, self.y1 = w, g, sb, x1, y1
        self.zi, self.ch, self.tmp, self.fo = zi, ch, tmp, fo
        self.ag_s, self.ag_r, self.rs_s, self.rs_r, self.mi_s, self.mi_r = sems
        self.s = lax.axis_index("section")
        self.d = lax.axis_index("dp")
        outer = self.d // inner
        self.z = outer // 4
        self.yx = outer % 4
        y, x = self.yx // 2, self.yx % 2
        self.sib = (1 - self.s, self.d)
        self.yx_x = self.yx + 1 - 2 * x
        self.yx_y = self.yx + 2 - 4 * y
        self.yx_d = 3 - self.yx
        self.xn = (self.s, self.d + (1 - 2 * x) * inner)
        self.yn = (self.s, self.d + (1 - 2 * y) * 2 * inner)
        self.zz = [(self.z + k) % 4 for k in (1, 2, 3)]
        self.zn = [(self.s, self.d + (zz - self.z) * 4 * inner) for zz in self.zz]
        self.sent = []

    def hello(self):
        barrier = pltpu.get_barrier_semaphore()
        for device in (self.sib, self.xn, self.yn, *self.zn):
            pl.semaphore_signal(barrier, inc=1, device_id=device, device_id_type=MESH)
        pl.semaphore_wait(barrier, 6)

    def copy(self, src, dst, send, recv, device):
        return pltpu.make_async_remote_copy(
            src_ref=src, dst_ref=dst, send_sem=send, recv_sem=recv,
            device_id=device, device_id_type=MESH,
        )

    def start(self, copy):
        copy.start()
        self.sent.append(copy)

    def finish(self):
        for copy in self.sent:
            copy.wait_send()
        self.sent = []

    def blk(self, ref, m, h, z, yx):
        return ref.at[h, :, z, yx] if m == DOWNW else ref.at[h, z, yx]

    def grp(self, ref, m, h, yx):
        return ref.at[h, :, :, yx] if m == DOWNW else ref.at[h, :, yx]

    def part(self, ref, m, h, z0, yx):
        return ref.at[h, :, pl.ds(z0, 2), yx] if m == DOWNW else ref.at[h, pl.ds(z0, 2), yx]

    def xy2(self, m):
        if m == DOWNW:
            return self.sb[m].at[0, pl.ds(0, 2)], self.sb[m].at[0, pl.ds(2, 2)]
        return self.sb[m].at[0], self.sb[m].at[1]

    def ag(self, m, slot):
        w, s = self.w[m], self.s
        pair = lambda src, dst, dev: self.copy(src, dst, self.ag_s.at[m, slot], self.ag_r.at[m, slot], dev)
        if slot == 0:
            if m == DOWNW:
                dst = self.ch[m].at[s]
            else:
                rows = self.tmp[m].shape[0]
                dst = self.ch[m].at[pl.ds(s * rows, rows)]
            return pair(self.tmp[m], dst, self.sib)
        if slot <= 3:
            ref = self.blk(w, m, s, self.z, self.yx)
            return pair(ref, ref, self.zn[slot - 1])
        if slot <= 5:
            ref = self.grp(w, m, s, self.yx)
            return pair(ref, ref, self.xn if slot == 4 else self.yn)
        if slot == 6:
            ref = self.part(w, m, s, 0, self.yx_x)
            return pair(ref, ref, self.yn)
        if slot == 7:
            ref = self.part(w, m, s, 2, self.yx_y)
            return pair(ref, ref, self.xn)
        ref = self.grp(w, m, s, (self.yx, self.yx_x, self.yx_y, self.yx_d)[slot - 8])
        return pair(ref, ref, self.sib)

    def ag0(self, m):
        self.start(self.ag(m, 0))

    def own(self, m):
        self.ag(m, 0).wait_recv()
        chunk = self.ch[m][...].astype(BF)
        if m == DOWNW:
            for sec in (0, 1):
                self.w[m][self.s, sec, self.z, self.yx] = chunk[sec]
        else:
            self.w[m][self.s, self.z, self.yx] = chunk

    def ag1(self, m):
        for slot in (1, 2, 3):
            self.start(self.ag(m, slot))

    def ag2(self, m):
        for slot in (1, 2, 3):
            self.ag(m, slot).wait_recv()
        for slot in (4, 5, 8):
            self.start(self.ag(m, slot))

    def ag3(self, m):
        self.ag(m, 4).wait_recv()
        for slot in (6, 9):
            self.start(self.ag(m, slot))
        self.ag(m, 5).wait_recv()
        for slot in (7, 10):
            self.start(self.ag(m, slot))

    def ag4(self, m):
        for slot in (6, 7):
            self.ag(m, slot).wait_recv()
        self.start(self.ag(m, 11))

    def ag5(self, m):
        for slot in (8, 9, 10, 11):
            self.ag(m, slot).wait_recv()

    def rs(self, m, slot):
        g, s = self.g[m], self.s
        pair = lambda src, dst, dev: self.copy(src, dst, self.rs_s.at[m, slot], self.rs_r.at[m, slot], dev)
        if slot == 0:
            return pair(g.at[1 - s], self.sb[m], self.sib)
        if slot == 1:
            return pair(self.part(g, m, s, 0, self.yx_d), self.x1[m], self.xn)
        if slot == 2:
            return pair(self.part(g, m, s, 2, self.yx_d), self.y1[m], self.yn)
        if slot == 3:
            return pair(self.grp(g, m, s, self.yx_x), self.xy2(m)[0], self.xn)
        if slot == 4:
            return pair(self.grp(g, m, s, self.yx_y), self.xy2(m)[1], self.yn)
        if slot <= 7:
            k = slot - 5
            return pair(self.blk(g, m, s, self.zz[k], self.yx), self.zi[m].at[k], self.zn[k])
        if m == DOWNW:
            src = self.ch[m].at[1 - s]
        else:
            rows = self.fo[m].shape[0]
            src = self.ch[m].at[pl.ds((1 - s) * rows, rows)]
        return pair(src, self.fo[m], self.sib)

    def rs0(self, m):
        self.start(self.rs(m, 0))

    def rs1(self, m):
        self.rs(m, 0).wait_recv()
        g, sb, s = self.g[m], self.sb[m], self.s

        def add(i, carry):
            if m == DOWNW:
                at = (i // 4, i % 4)
                g[s, at[0], at[1]] = (g[s, at[0], at[1]].astype(F32) + sb[at[0], at[1]].astype(F32)).astype(BF)
            else:
                g[s, i // 4, i % 4] = (g[s, i // 4, i % 4].astype(F32) + sb[i // 4, i % 4].astype(F32)).astype(BF)
            return carry

        lax.fori_loop(0, 8 if m == DOWNW else 16, add, 0)
        self.start(self.rs(m, 1))
        self.start(self.rs(m, 2))

    def rs2(self, m):
        g, s = self.g[m], self.s
        for slot, ref, z0, yx in ((1, self.x1[m], 0, self.yx_y), (2, self.y1[m], 2, self.yx_x)):
            self.rs(m, slot).wait_recv()
            for j in (0, 1):
                if m == DOWNW:
                    for sec in (0, 1):
                        mine = g[s, sec, z0 + j, yx].astype(F32)
                        g[s, sec, z0 + j, yx] = (mine + ref[sec, j].astype(F32)).astype(BF)
                else:
                    mine = g[s, z0 + j, yx].astype(F32)
                    g[s, z0 + j, yx] = (mine + ref[j].astype(F32)).astype(BF)
        self.start(self.rs(m, 3))
        self.start(self.rs(m, 4))

    def rs3(self, m):
        self.rs(m, 3).wait_recv()
        self.rs(m, 4).wait_recv()
        g, s, yx = self.g[m], self.s, self.yx
        a, b = self.xy2(m)

        def total(sec, z):
            if m == DOWNW:
                return g[s, sec, z, yx].astype(F32) + a[sec, z].astype(F32) + b[sec, z].astype(F32)
            return g[s, z, yx].astype(F32) + a[z].astype(F32) + b[z].astype(F32)

        for slot in (5, 6, 7):
            zz = self.zz[slot - 5]
            if m == DOWNW:
                for sec in (0, 1):
                    g[s, sec, zz, yx] = total(sec, zz).astype(BF)
            else:
                g[s, zz, yx] = total(0, zz).astype(BF)
            self.start(self.rs(m, slot))
        if m == DOWNW:
            for sec in (0, 1):
                self.ch[m][sec] = total(sec, self.z)
        else:
            self.ch[m][...] = total(0, self.z)

    def rs4(self, m):
        for slot in (5, 6, 7):
            self.rs(m, slot).wait_recv()
        zi = self.zi[m]
        self.ch[m][...] += zi[0].astype(F32) + zi[1].astype(F32) + zi[2].astype(F32)
        self.start(self.rs(m, 8))

    def rs5(self, m):
        if m == DOWNW:
            mine = self.ch[m][self.s]
        else:
            rows = self.fo[m].shape[0]
            mine = self.ch[m][pl.ds(self.s * rows, rows)]
        self.rs(m, 8).wait_recv()
        return mine, self.fo[m][...]


def kernel(inner, sizes, *refs):
    (byte_ids, lengths, groups, emb, lang, scorer, prenorm, midnorm, rel, wq, wk, wv, wo, wi0, wi1, wd, cot) = refs[:17]
    (enc_out, g_elt, g_q, g_k, g_v, g_o, g_0, g_1, g_d, g_rel) = refs[17:27]
    rest = refs[27:]
    take = lambda k: rest[N * k : N * k + N]
    w, g, sb, x1, y1, zi, ch, tmp, fo = (take(k) for k in range(9))
    rest = rest[9 * N :]
    sems, rest = rest[:6], rest[6:]
    (pi, cb, prow, gthi, gtlo, rows_ref, hid, nrm, nrmt, qs, ks, vs, bvec, pmat, mixed, mixp, mid, sec_ref, sect,
     acc, encb, dq, dk, dv, dvec, relbuf, relin, cp) = rest
    tokens, width, half, ffh = sizes
    quarter = ffh // 4
    net = Net(inner, w, g, sb, x1, y1, zi, ch, tmp, fo, sems)
    s = net.s
    net.hello()

    def lanes(ref, h, n):
        return ref[:, pl.ds(pl.multiple_of(h * n, 128), n)]

    def wmat(m, h):
        return w[m][h].reshape(width, w[m].shape[-1])

    def gput(m, h, value):
        g[m][h] = value.astype(BF).reshape(g[m].shape[1:])

    rows_d = wq.shape[0]
    vocab, langs = emb.shape[0], lang.shape[0]

    def turned(value, at):
        rows = value.shape[0]
        more = -rows % 8
        if more:
            value = jnp.concatenate([value, jnp.zeros((more, rows_d), F32)], axis=0)
        row = iota((rows + more, 512), 0)
        spot = (row + at == iota((rows + more, 512), 1)) & (row < rows)
        return dot_tn(value.astype(BF), jnp.where(spot, 1.0, 0.0).astype(BF))

    vectors = jnp.concatenate([scorer[...], prenorm[...], midnorm[...]], axis=0)
    elt = turned(emb[...], 0) + turned(lang[...], vocab) + turned(vectors, 256 + SCORER)
    wide = {}

    def halves(m, h):
        if m == ELT:
            return jnp.where(h == 0, elt[:, :256], elt[:, 256:])
        if m in (WQ, WK, WV):
            return lanes({WQ: wq, WK: wk, WV: wv}[m], h, half)
        if m in GU:
            cols = pl.ds(pl.multiple_of(h * ffh + (m - GU0) * quarter, 128), quarter)
            return jnp.concatenate([wi0[:, cols], wi1[:, cols]], axis=1)
        value = wide[m]
        return jnp.where(h == 0, value[:, :half], value[:, half:])

    def exchange(m):
        tmp[m][...] = halves(m, 1 - s)
        net.ag0(m)
        mine = halves(m, s)
        if m == DOWNW:
            ch[m][s] = mine
        else:
            ch[m][pl.ds(s * rows_d, rows_d)] = mine

    for m in (ELT, WQ, WK, WV, *GU):
        exchange(m)
    for m in (ELT, WQ, WK):
        net.own(m)
        net.ag1(m)

    col = iota((1, width), 1)
    chip = over(col, 2 * rows_d)
    inside = col - chip * (2 * rows_d)
    natural = jnp.where(inside < rows_d, chip * rows_d + inside, half + (chip - 1) * rows_d + inside)
    pi[...] = jnp.where(iota((width, width), 0) == natural, 1.0, 0.0).astype(BF)
    wide[WO] = dot(wo[...].astype(BF), pi[...])
    wide[DOWNW] = dot(wd[...].astype(BF), pi[...])
    exchange(WO)
    exchange(DOWNW)
    for m in (WV, WO, DOWNW, *GU):
        net.own(m)

    gather = {"Z": net.ag2, "X": net.ag3, "D": net.ag4, "S": net.ag5, "A": net.ag1}
    reduce = {"a": net.rs0, "b": net.rs1, "c": net.rs2, "d": net.rs3, "e": net.rs4}

    def run(text):
        for word in text.split():
            m = int(word[1:])
            if word[0] in gather:
                gather[word[0]](m)
                if word[0] == "Z" and m + 3 < N:
                    net.ag1(m + 3)
            elif word[0] == "f":
                last(m)
            else:
                reduce[word[0]](m)

    run("Z0")
    cp[...] = dot(cot[s], pi[...]).astype(BF)

    span = 2 * tokens
    buckets, heads = rel.shape
    ohb = jnp.where(iota((buckets, span), 0) == bucket_ids(iota((buckets, span), 1) - (tokens - 1)), 1.0, 0.0).astype(BF)
    bv = sum(dot_tn(part, ohb) for part in split3(rel[...]))
    for h in range(heads):
        bvec[h] = bv[h : h + 1, :]
    run("X0 Z1")

    length = jnp.where(s == 0, lengths[0:1, :], lengths[1:2, :])
    group = jnp.where(s == 0, groups[0:1, :], groups[1:2, :])
    col = iota((1, span), 1)
    pos = jnp.where(col < tokens, 2 * col, 2 * (col - tokens) + 1)
    symbol = iota((VOC, span), 0)
    onehot = jnp.where(((symbol == byte_ids[s]) | (symbol == group + vocab)) & (col < length), 1.0, 0.0).astype(BF)

    def block_of(p, size):
        return p if size == 1 else p >> 1 if size == 2 else over(p, 3) if size == 3 else p >> 2

    rowi = iota((span, 1), 0)
    for size in range(1, BLOCKS + 1):
        pool = jnp.where(block_of(rowi, size) == block_of(pos, size), 1.0, 0.0).astype(BF)
        cb[size - 1] = dot(onehot, pool).astype(BF)
    run("D0 Z2 S0 X1")

    e0, e1 = wmat(ELT, 0), wmat(ELT, 1)[:, :128]
    picks = jnp.where(iota((8, 128), 1) == iota((8, 128), 0) + SCORER, 1.0, 0.0).astype(BF)
    rows_ref[...] = dot_nt(picks, e1)
    g1, g2 = rows_ref[1:2, :], rows_ref[2:3, :]
    ew = jnp.concatenate([dot_tn(e0, e1), dot_tn(e1, e1)[: VOC - 256]], axis=0)[:, SCORER : SCORER + 1]
    ratings = [jnp.sum(cb[b].astype(F32) * ew, axis=0, keepdims=True) / (b + 1) for b in range(BLOCKS)]
    top = functools.reduce(jnp.maximum, ratings)
    raised = [jnp.exp(r - top) for r in ratings]
    total = sum(raised)
    chosen = [r / total for r in raised]
    mixw = 0.0
    for b in range(BLOCKS):
        prow[b : b + 1, :] = chosen[b]
        mixw = mixw + cb[b].astype(F32) * (chosen[b] / (2.0 * (b + 1)))
    gt = mixw[:, :tokens] + mixw[:, tokens:]
    gt = jnp.concatenate([gt, jnp.zeros((384 - VOC, tokens), F32)], axis=0).T
    gthi[...] = gt.astype(BF)
    gtlo[...] = (gt - gt.astype(BF).astype(F32)).astype(BF)
    run("Z3 D1 X2")
    latent = (
        dot_nt(gthi[:, :256], e0) + dot_nt(gthi[:, 256:], e1)
        + dot_nt(gtlo[:, :256], e0) + dot_nt(gtlo[:, 256:], e1)
    )
    hid[...] = latent.astype(BF)

    hidden = hid[...].astype(F32)
    r1 = lax.rsqrt(jnp.mean(hidden * hidden, -1, keepdims=True) + EPSILON)
    normed = hidden * r1 * g1
    nrm[...] = normed.astype(BF)
    nrmt[...] = normed.T.astype(BF)

    def project(m, ref):
        for h in (0, 1):
            out = dot(nrm[...], wmat(m, h)).astype(BF)
            for i in range(half // 128):
                ref[h * (half // 128) + i] = out[:, i * 128 : (i + 1) * 128]

    run("Z4 S1 D2 X3")
    project(WQ, qs)
    run("Z5 S2 D3 X4")
    project(WK, ks)
    run("S3 D4")
    project(WV, vs)
    run("Z6")

    tcol = iota((1, tokens), 1)
    valid_key = DOWN * tcol < length
    lane = iota((1, 128), 1)
    masks = [jnp.where(lane < 64, 1.0 - e, float(e)).astype(BF) for e in (0, 1)]

    def forward_pair(i, carry):
        q2, k2, v2 = qs[i], ks[i], vs[i]
        out = 0.0
        for e in (0, 1):
            h = 2 * i + e
            line = jnp.broadcast_to(bvec[h], (tokens, span))
            bias = pltpu.roll(line, tokens + 1, 1, stride=1, stride_axis=0)[:, :tokens]
            scores = jnp.where(valid_key, dot_nt(q2, k2 * masks[e]) + bias, NEGATIVE)
            up = jnp.exp(scores - jnp.max(scores, -1, keepdims=True))
            prob = up * (1.0 / jnp.sum(up, -1, keepdims=True))
            pmat[h] = prob
            out = out + dot(prob.astype(BF), v2 * masks[e])
        mixed[:, pl.ds(pl.multiple_of(i * 128, 128), 128)] = out.astype(BF)
        return carry

    pairs = width // 128
    lax.fori_loop(0, pairs // 2, forward_pair, 0)
    run("X5 S4 Z7")
    lax.fori_loop(pairs // 2, pairs, forward_pair, 0)
    run("D5 X6")
    mixp[...] = dot(mixed[...], pi[...]).astype(BF)
    for h in (0, 1):
        cols = slice(h * half, (h + 1) * half)
        mid[:, cols] = hid[:, cols].astype(F32) + dot(mixp[...], wmat(WO, h))
    middle = mid[...]
    r2 = lax.rsqrt(jnp.mean(middle * middle, -1, keepdims=True) + EPSILON)
    second = middle * r2 * g2
    sec_ref[...] = second.astype(BF)
    sect[...] = second.T.astype(BF)
    acc[...] = jnp.zeros_like(acc)
    encb[...] = mid[...]
    run("Z8 S5 D6 X7 Z9")

    def feed(c):
        def one(h, carry):
            wgu = w[GU0 + c][h].reshape(width, 2 * quarter)
            wdn = [w[DOWNW][j, h, c].reshape(quarter, half) for j in (0, 1)]
            both = dot(sec_ref[...], wgu)
            gate, upper = both[:, :quarter], both[:, quarter:]
            pdelta = dot_nt(cp[:, :half], wdn[0]) + dot_nt(cp[:, half:], wdn[1])
            square = gate * gate
            tanh = jnp.tanh(0.7978845608 * (gate + 0.044715 * square * gate))
            act = 0.5 * gate * (1.0 + tanh)
            slope = 0.5 * (1.0 + tanh) + 0.5 * gate * (1.0 - tanh * tanh) * 0.7978845608 * (1.0 + 0.134145 * square)
            product = (act * upper).astype(BF)
            delta = jnp.concatenate([(pdelta * upper * slope).astype(BF), (pdelta * act).astype(BF)], axis=1)
            gput(GU0 + c, h, dot(sect[...], delta))
            for j in (0, 1):
                out = slice(j * half, (j + 1) * half)
                g[DOWNW][j, h, c] = dot_tn(product, cp[:, out]).astype(BF).reshape(4, -1, half)
                encb[:, out] += dot(product, wdn[j])
            acc[...] += dot_nt(delta, wgu)
            return carry

        lax.fori_loop(0, 2, one, 0)

    run("S6")
    feed(0)
    run("a6 D7 X8 S7")
    feed(1)
    run("a7 D8 X9 S8 b6")
    feed(2)
    run("a8 D9 b7 S9 c6")
    feed(3)
    run("a9 a5 b8 c7 d6")

    middle = mid[...]
    r2 = lax.rsqrt(jnp.mean(middle * middle, -1, keepdims=True) + EPSILON)
    n2 = middle * r2
    sdelta = acc[...]
    scaled = sdelta * g2
    mid_grad = jnp.sum(sdelta * n2, axis=0, keepdims=True)
    mdel = acc
    mdel[...] = cp[...].astype(F32) + r2 * (scaled - n2 * jnp.mean(scaled * n2, -1, keepdims=True))
    sec_ref[...] = mdel[...].astype(BF)
    run("b9 b5")
    for h in (0, 1):
        gput(WO, h, dot_tn(mixp[...], sec_ref[:, h * half : (h + 1) * half]))
    run("a4 c8 d7")
    back = dot_nt(sec_ref[:, :half], wmat(WO, 0)) + dot_nt(sec_ref[:, half:], wmat(WO, 1))
    mixp[...] = dot_nt(back.astype(BF), pi[...]).astype(BF)
    flip = jnp.where(iota((tokens, tokens), 0) + iota((tokens, tokens), 1) == tokens - 1, 1.0, 0.0).astype(BF)
    run("b4 c9 c5 d8")

    def backward_pair(i, carry):
        cols = pl.ds(pl.multiple_of(i * 128, 128), 128)
        q2, k2, v2, m2 = qs[i], ks[i], vs[i], mixp[:, cols]
        outq = outk = outv = 0.0
        for e in (0, 1):
            h = 2 * i + e
            prob = pmat[h]
            wdelta = dot_nt(m2, v2 * masks[e])
            lean = jnp.sum(prob * wdelta, -1, keepdims=True)
            sd = jnp.where(valid_key, prob * (wdelta - lean), 0.0).astype(BF)
            outq = outq + dot(sd, k2 * masks[e])
            outk = outk + dot_tn(sd, q2 * masks[e])
            outv = outv + dot_tn(prob.astype(BF), m2 * masks[e])
            reverse = jnp.concatenate([dot(sd, flip), jnp.zeros((tokens, tokens), F32)], axis=1)
            skew = pltpu.roll(reverse, 0, 1, stride=1, stride_axis=0)
            dvec[h] = jnp.sum(skew, axis=0, keepdims=True)
        dq[:, cols], dk[:, cols], dv[:, cols] = outq.astype(BF), outk.astype(BF), outv.astype(BF)
        return carry

    lax.fori_loop(0, pairs // 2, backward_pair, 0)
    run("d9 d5 c4")
    lax.fori_loop(pairs // 2, pairs, backward_pair, 0)
    run("e6 e7")

    ohr = jnp.where(iota((buckets, span), 0) == bucket_ids((tokens - 1) - iota((buckets, span), 1)), 1.0, 0.0).astype(BF)
    lines = jnp.concatenate([dvec[h] for h in range(heads)] + [jnp.zeros((128 - heads, span), F32)], axis=0)
    relbuf[0] = sum(dot_nt(ohr, part) for part in split3(lines))
    levels = (
        ((0, net.sib),), ((1, net.xn),), ((2, net.yn),), ((3, net.zn[0]), (4, net.zn[1]), (5, net.zn[2])),
    )

    def rel_copy(slot, level, device):
        return net.copy(relbuf.at[level], relin.at[slot], net.mi_s.at[1 + slot], net.mi_r.at[1 + slot], device)

    def rel_step(level):
        if level:
            for slot, device in levels[level - 1]:
                rel_copy(slot, level - 1, device).wait_recv()
        if level in (1, 2, 3):
            relbuf[level] = relbuf[level - 1] + relin[level - 1]
        if level < 4:
            for slot, device in levels[level]:
                net.start(rel_copy(slot, level, device))
            return
        place = [jnp.where(net.z == k, 1.0, 0.0) for k in range(4)]
        level = [relbuf[3], relin[3], relin[4], relin[5]]
        summed = 0.0
        for k in range(4):
            summed = summed + sum(place[z] * level[(z - k) % 4] for z in range(4))
        g_rel[...] = summed

    rel_step(0)

    norm_delta = 0.0
    for m, ref in ((WQ, dq), (WK, dk), (WV, dv)):
        for h in (0, 1):
            part = ref[:, h * half : (h + 1) * half]
            gput(m, h, dot(nrmt[...], part))
            norm_delta = norm_delta + dot_nt(part, wmat(m, h))
        run(f"a{m}")
    rel_step(1)
    run("d4 b1 e8")
    hidden = hid[...].astype(F32)
    r1 = lax.rsqrt(jnp.mean(hidden * hidden, -1, keepdims=True) + EPSILON)
    n1 = hidden * r1
    scaled = norm_delta * g1
    pre_grad = jnp.sum(norm_delta * n1, axis=0, keepdims=True)
    hdel = (mdel[...] + r1 * (scaled - n1 * jnp.mean(scaled * n1, -1, keepdims=True))).astype(BF)
    rel_step(2)
    run("b2 b3 e9 c1")

    back = jnp.concatenate([dot(hdel, e0), dot(hdel, e1)], axis=1).T[:VOC]
    back = jnp.concatenate([back, back], axis=1)
    pdel = [jnp.sum(cb[b].astype(F32) * back, axis=0, keepdims=True) / (2.0 * (b + 1)) for b in range(BLOCKS)]
    lean = sum(prow[b : b + 1, :] * pdel[b] for b in range(BLOCKS))
    flow = 0.0
    for b in range(BLOCKS):
        flow = flow + cb[b].astype(F32) * (prow[b : b + 1, :] * (pdel[b] - lean) / (b + 1))
    gs = jnp.sum(flow, axis=1, keepdims=True)
    lane_v = iota((VOC, 128), 1)
    parts = [p.astype(F32) for p in split3(gs)]
    gs3 = jnp.where(lane_v == 0, parts[0], jnp.where(lane_v == 1, parts[1], jnp.where(lane_v == 2, parts[2], 0.0)))
    gs3 = gs3.astype(BF)
    rel_step(3)
    run("c2 c3 d1 e5")
    lane_w = iota((width, 128), 1)
    wcol = jnp.where(lane_w < 3, e1.astype(F32)[:, SCORER : SCORER + 1], 0.0).astype(BF)
    gput(ELT, 0, dot_tn(hdel, gthi[:, :256]) + dot_tn(hdel, gtlo[:, :256]) + dot_nt(wcol, gs3[:256]))
    gs_tail = jnp.concatenate([gs3[256:], jnp.zeros((128 + 256 - VOC, 128), BF)], axis=0)
    tail = dot_tn(hdel, gthi[:, 256:]) + dot_tn(hdel, gtlo[:, 256:]) + dot_nt(wcol, gs_tail)
    scorer_grad = jnp.sum(dot(e0, gs3[:256]) + dot(e1, gs_tail), axis=1, keepdims=True)
    gains = [p.astype(F32) for p in (*split3(pre_grad), *split3(mid_grad))]
    gains = jnp.concatenate([*gains, jnp.zeros((10, width), F32)], axis=0).astype(BF)
    place_row, place_col = iota((16, 128), 0), iota((16, 128), 1)
    place = (place_row < 6) & (place_col == jnp.where(place_row < 3, SCORER + 1, SCORER + 2))
    tail = tail + dot_tn(gains, jnp.where(place, 1.0, 0.0).astype(BF))
    tail = jnp.where(lane_w == SCORER, scorer_grad, tail)
    gput(ELT, 1, jnp.concatenate([tail, jnp.zeros((width, 128), F32)], axis=1))
    run("a0")
    rel_step(4)

    encoded = dot_nt(encb[...].astype(BF), pi[...]).astype(BF)
    for h in (0, 1):
        mixed[:, h * half : (h + 1) * half] = encoded[:, h * half : (h + 1) * half]
    enc_out[s] = lanes(mixed, s, half)
    enc_copy = net.copy(
        mixed.at[:, pl.ds(pl.multiple_of((1 - s) * half, 128), half)], enc_out.at[s],
        net.mi_s.at[0], net.mi_r.at[0], net.sib,
    )
    net.start(enc_copy)

    def last(m):
        mine, other = net.rs5(m)
        if m in (WO, DOWNW):
            first = jnp.where(s == 0, mine, other)
            second = jnp.where(s == 0, other, mine)
            both = jnp.concatenate([first, second], axis=1)
            out = g_o if m == WO else g_d
            out[...] = sum(dot_nt(part, pi[...]) for part in split3(both))
            return
        for h, value in ((s, mine), (1 - s, other)):
            if m in GU:
                cols = pl.ds(pl.multiple_of(h * ffh + (m - GU0) * quarter, 128), quarter)
                g_0[:, cols] = value[:, :quarter]
                g_1[:, cols] = value[:, quarter:]
            else:
                n = value.shape[1]
                target = {ELT: g_elt, WQ: g_q, WK: g_k, WV: g_v}[m]
                target[:, pl.ds(pl.multiple_of(h * n, 128), n)] = value

    run("b0 f6 f7 f8 c0 f9 f5 d2 d3 e4 f4 d0 e1 e2 e3 f1 e0 f2 f3 f0")
    enc_copy.wait_recv()
    net.finish()


VMEM = pl.BlockSpec(memory_space=pltpu.VMEM)


def call(inner, *args):
    wq, wi0, wd, cot = args[9], args[13], args[15], args[16]
    rows_d, width = wq.shape
    rows_f = wd.shape[0]
    half, ffh = width // 2, wi0.shape[1] // 2
    tokens = cot.shape[1]
    span = 2 * tokens
    buckets, heads = args[8].shape
    wide = {m: 256 if m == ELT else ffh // 2 if m in GU else half for m in ALL}
    chip = {m: (2, rows_f) if m == DOWNW else (2 * rows_d,) for m in ALL}
    mine = {m: rows_f if m == DOWNW else rows_d for m in ALL}

    def full(m):
        return (2, 4, 4, rows_f, wide[m]) if m == DOWNW else (4, 4, 2 * rows_d, wide[m])

    def part(m):
        return (2, 2, rows_f, wide[m]) if m == DOWNW else (2, 2 * rows_d, wide[m])

    scratch = []
    scratch += [pltpu.VMEM((2, *full(m)), BF) for m in ALL]
    scratch += [pltpu.VMEM((2, *full(m)), BF) for m in ALL]
    scratch += [pltpu.VMEM(full(m), BF) for m in ALL]
    scratch += [pltpu.VMEM(part(m), BF) for m in ALL]
    scratch += [pltpu.VMEM(part(m), BF) for m in ALL]
    scratch += [pltpu.VMEM((3, *chip[m], wide[m]), BF) for m in ALL]
    scratch += [pltpu.VMEM((*chip[m], wide[m]), F32) for m in ALL]
    scratch += [pltpu.VMEM((mine[m], wide[m]), F32) for m in ALL]
    scratch += [pltpu.VMEM((mine[m], wide[m]), F32) for m in ALL]
    dma = pltpu.SemaphoreType.DMA
    scratch += [dma((N, 12)), dma((N, 12)), dma((N, 9)), dma((N, 9)), dma((7,)), dma((7,))]
    act = (tokens, width)
    scratch += [
        pltpu.VMEM((width, width), BF),
        pltpu.VMEM((BLOCKS, VOC, span), BF),
        pltpu.VMEM((8, span), F32),
        pltpu.VMEM((tokens, 384), BF),
        pltpu.VMEM((tokens, 384), BF),
        pltpu.VMEM((8, width), F32),
        pltpu.VMEM(act, BF),
        pltpu.VMEM(act, BF),
        pltpu.VMEM((width, tokens), BF),
        pltpu.VMEM((width // 128, tokens, 128), BF),
        pltpu.VMEM((width // 128, tokens, 128), BF),
        pltpu.VMEM((width // 128, tokens, 128), BF),
        pltpu.VMEM((heads, 1, span), F32),
        pltpu.VMEM((heads, tokens, tokens), F32),
        pltpu.VMEM(act, BF),
        pltpu.VMEM(act, BF),
        pltpu.VMEM(act, F32),
        pltpu.VMEM(act, BF),
        pltpu.VMEM((width, tokens), BF),
        pltpu.VMEM(act, F32),
        pltpu.VMEM(act, F32),
        pltpu.VMEM(act, BF),
        pltpu.VMEM(act, BF),
        pltpu.VMEM(act, BF),
        pltpu.VMEM((heads, 1, span), F32),
        pltpu.VMEM((4, buckets, 128), F32),
        pltpu.VMEM((6, buckets, 128), F32),
        pltpu.VMEM(act, BF),
    ]
    outs = [
        jax.ShapeDtypeStruct((MICRO, tokens, half), BF),
        jax.ShapeDtypeStruct((rows_d, 512), F32),
        *[jax.ShapeDtypeStruct(item.shape, F32) for item in args[9:16]],
        jax.ShapeDtypeStruct((buckets, 128), F32),
    ]
    return pl.pallas_call(
        functools.partial(kernel, inner, (tokens, width, half, ffh)),
        out_shape=outs,
        in_specs=[VMEM] * len(args),
        out_specs=[VMEM] * len(outs),
        scratch_shapes=scratch,
        compiler_params=pltpu.CompilerParams(
            collective_id=0, has_side_effects=True, vmem_limit_bytes=63 * 2**20
        ),
    )(*args)


def settle(vocab, langs, heads, *refs):
    ins, outs = refs[:10], refs[10:]
    outs[0][:, 0] = ins[0][...]
    rows = ins[1].shape[0]
    table = ins[1][...]
    table = jnp.concatenate([table, jnp.zeros((128 - rows, table.shape[1]), F32)], axis=0).T[:, :rows]
    outs[1][...] = table[:vocab]
    outs[2][...] = table[vocab : vocab + langs]
    at = vocab + langs
    for k, i in enumerate((3, 4, 9)):
        outs[i][...] = table[at + k : at + k + 1]
    for i, k in zip((5, 6, 7, 8, 10, 11, 12), range(2, 9)):
        outs[i][...] = ins[k][...]
    outs[13][...] = ins[9][:, :heads]


def body(
    byte_ids, lengths, groups, embedding, language, scorer, prenorm, query_weight, key_weight, value_weight,
    output_weight, midnorm, gate_weight, up_weight, down_weight, relative, cotangent,
):
    inner = lax.axis_size("dp") // OUTER
    vocab, langs = embedding.shape[0], language.shape[0]
    tables = [embedding, language, scorer[None], prenorm[None], midnorm[None]]
    weights = [query_weight, key_weight, value_weight, output_weight, gate_weight, up_weight, down_weight]
    teams = [[o * inner + i for i in range(inner)] for o in range(OUTER)]
    if inner > 1:
        tables = [lax.all_gather(item, "dp", axis_index_groups=teams, axis=1, tiled=True) for item in tables]
        weights = [lax.all_gather(item, "dp", axis_index_groups=teams, axis=0, tiled=True) for item in weights]
    results = call(inner, byte_ids, lengths, groups, *tables, relative, *weights, cotangent[:, 0])
    if inner > 1:
        grads = [
            lax.psum_scatter(item, "dp", axis_index_groups=teams, scatter_dimension=0, tiled=True)
            for item in results[1:9]
        ]
        results = [results[0], *grads, lax.psum(results[9], "dp", axis_index_groups=teams)]
    buckets, heads = relative.shape
    rows = results[1].shape[0]
    line = jax.ShapeDtypeStruct((1, rows), F32)
    like = [jax.ShapeDtypeStruct(item.shape, F32) for item in results[2:9]]
    shapes = [
        jax.ShapeDtypeStruct(cotangent.shape[:3] + (results[0].shape[2],), BF),
        jax.ShapeDtypeStruct((vocab, rows), F32),
        jax.ShapeDtypeStruct((langs, rows), F32),
        line, line, *like[:4], line, *like[4:],
        jax.ShapeDtypeStruct((buckets, heads), F32),
    ]
    outs = pl.pallas_call(
        functools.partial(settle, vocab, langs, heads),
        out_shape=shapes,
        in_specs=[VMEM] * 10,
        out_specs=[VMEM] * 14,
        compiler_params=pltpu.CompilerParams(vmem_limit_bytes=24 * 2**20),
    )(*results)
    return tuple(item[0] if i in (3, 4, 9) else item for i, item in enumerate(outs))


def solution(mesh):
    both = ("section", "dp")
    wide = P(both, None)
    return jax.shard_map(
        body,
        mesh=mesh,
        in_specs=(
            P(None, "dp", None), P(None, "dp"), P(None, "dp"), P(None, both), P(None, both), P(both), P(both),
            wide, wide, wide, wide, P(both), wide, wide, wide, P(), P(None, "dp", None, None),
        ),
        out_specs=(
            P(None, "dp", None, "section"), P(None, both), P(None, both), P(both), P(both),
            wide, wide, wide, wide, P(both), wide, wide, wide, P(),
        ),
        check_vma=False,
    )
```

```python
import functools

import jax
import jax.numpy as jnp
from jax import lax
from jax.experimental import pallas as pl
from jax.experimental.pallas import tpu as pltpu
from jax.sharding import PartitionSpec as P

BLOCKS = 4
DOWN = 2
MICRO = 2
OUTER = 16
EPSILON = 1e-06
NEGATIVE = -1000000000.0
LIMITS = (12, 16, 23, 32, 46, 64, 91)
MESH = pl.DeviceIdType.MESH
BF = jnp.bfloat16
F32 = jnp.float32
I32 = jnp.int32

ELT, WQ, WK, WV, WO, DNA, DNB, GU0, GU1, GU2, GU3 = range(11)
DN = (DNA, DNB)
GU = (GU0, GU1, GU2, GU3)
ALL = tuple(range(11))
N = len(ALL)
PLANE_GATHER = ()
PLANE_REDUCE = ()
SCHEDULE = (
    ("A", 6), ("p", 0), ("p", 1), ("p", 2), ("Z", 0), ("A", 2), ("Z", 6), ("A", 1), ("X", 0), ("Z", 2), ("A", 3),
    ("D", 0), ("X", 6), ("Z", 1), ("A", 4), ("S", 0), ("p", 3), ("p", 4), ("Z", 3), ("A", 7), ("X", 2), ("D", 6),
    ("Z", 4), ("A", 5), ("X", 1), ("S", 6), ("D", 2), ("S", 2), ("Z", 7), ("D", 1), ("A", 8), ("X", 3), ("X", 4),
    ("Z", 5), ("A", 9), ("S", 1), ("p", 5), ("p", 6), ("D", 3), ("D", 4), ("Z", 8), ("A", 10), ("S", 3), ("p", 7),
    ("S", 4), ("Z", 9), ("X", 7), ("p", 8), ("X", 5), ("p", 9), ("p", 10), ("Z", 10), ("p", 11), ("D", 7), ("X", 8),
    ("S", 7), ("D", 5), ("X", 9), ("S", 5), ("p", 12), ("D", 8), ("a", 7), ("X", 10), ("D", 9), ("S", 8), ("p", 13),
    ("S", 9), ("D", 10), ("b", 7), ("a", 8), ("p", 14), ("c", 7), ("S", 10), ("b", 8), ("a", 9), ("p", 15), ("b", 9),
    ("a", 10), ("a", 6), ("a", 5), ("p", 16), ("c", 8), ("a", 4), ("p", 17), ("d", 7), ("p", 18), ("c", 9), ("b", 10),
    ("b", 6), ("b", 4), ("b", 5), ("d", 8), ("p", 19), ("e", 7), ("p", 20), ("p", 21), ("p", 22), ("e", 8), ("p", 23),
    ("c", 10), ("c", 4), ("p", 24), ("c", 6), ("c", 5), ("p", 25), ("p", 26), ("p", 27), ("p", 28), ("f", 7),
    ("f", 8), ("d", 9), ("r", 1), ("a", 3), ("a", 1), ("a", 0), ("a", 2), ("r", 2), ("b", 0), ("d", 4), ("r", 3),
    ("b", 3), ("b", 1), ("b", 2), ("e", 9), ("d", 10), ("r", 4), ("f", 9), ("c", 0), ("e", 4), ("d", 6), ("d", 5),
    ("c", 3), ("f", 4), ("c", 1), ("c", 2), ("e", 10), ("d", 0), ("f", 10), ("d", 3), ("d", 1), ("d", 2), ("e", 6),
    ("e", 0), ("e", 5), ("f", 6), ("f", 0), ("f", 5), ("e", 3), ("f", 3), ("e", 1), ("e", 2), ("f", 1), ("f", 2),
)
VOC = 288
SCORER = 19


def dot(a, b):
    return lax.dot_general(a, b, (((1,), (0,)), ((), ())), preferred_element_type=F32)


def dot_nt(a, b):
    return lax.dot_general(a, b, (((1,), (1,)), ((), ())), preferred_element_type=F32)


def dot_tn(a, b):
    return lax.dot_general(a, b, (((0,), (0,)), ((), ())), preferred_element_type=F32)


def split3(x):
    hi = x.astype(BF)
    rest = x - hi.astype(F32)
    mid = rest.astype(BF)
    return hi, mid, (rest - mid.astype(F32)).astype(BF)


def iota(shape, axis):
    return lax.broadcasted_iota(I32, shape, axis)


def over(value, n):
    return (value * (65536 // n + 1)) >> 16


def bucket_ids(offsets):
    distance = jnp.abs(offsets)
    larger = 8 + sum(((distance >= limit).astype(I32) for limit in LIMITS))
    inside = jnp.where(distance < 8, distance, larger)
    return jnp.where(offsets > 0, 16, 0).astype(I32) + inside


class Net:
    def __init__(self, inner, w, g, sb, x1, y1, zi, ch, tmp, fo, sems):
        self.w, self.g, self.sb, self.x1, self.y1 = w, g, sb, x1, y1
        self.zi, self.ch, self.tmp, self.fo = zi, ch, tmp, fo
        self.ag_s, self.ag_r, self.rs_s, self.rs_r, self.mi_s, self.mi_r = sems
        self.s = lax.axis_index("section")
        self.d = lax.axis_index("dp")
        outer = self.d // inner
        self.z = outer // 4
        self.yx = outer % 4
        y, x = self.yx // 2, self.yx % 2
        self.sib = (1 - self.s, self.d)
        self.yx_x = self.yx + 1 - 2 * x
        self.yx_y = self.yx + 2 - 4 * y
        self.yx_d = 3 - self.yx
        self.xn = (self.s, self.d + (1 - 2 * x) * inner)
        self.yn = (self.s, self.d + (1 - 2 * y) * 2 * inner)
        self.dn = (self.s, self.d + (1 - 2 * x) * inner + (1 - 2 * y) * 2 * inner)
        self.zz = [(self.z + k) % 4 for k in (1, 2, 3)]
        self.zn = [(self.s, self.d + (zz - self.z) * 4 * inner) for zz in self.zz]
        self.sent = []

    def hello(self):
        barrier = pltpu.get_barrier_semaphore()
        for device in (self.sib, self.xn, self.yn, self.dn, *self.zn):
            pl.semaphore_signal(barrier, inc=1, device_id=device, device_id_type=MESH)
        pl.semaphore_wait(barrier, 7)

    def copy(self, src, dst, send, recv, device):
        return pltpu.make_async_remote_copy(
            src_ref=src, dst_ref=dst, send_sem=send, recv_sem=recv,
            device_id=device, device_id_type=MESH,
        )

    def start(self, copy):
        copy.start()
        self.sent.append(copy)

    def finish(self):
        for copy in self.sent:
            copy.wait_send()
        self.sent = []

    def blk(self, ref, m, h, z, yx):
        return ref.at[h, :, z, yx] if m in DN else ref.at[h, z, yx]

    def grp(self, ref, m, h, yx):
        return ref.at[h, :, :, yx] if m in DN else ref.at[h, :, yx]

    def part(self, ref, m, h, z0, yx):
        return ref.at[h, :, pl.ds(z0, 2), yx] if m in DN else ref.at[h, pl.ds(z0, 2), yx]

    def plane(self, ref, m, h, z):
        return ref.at[h, :, z] if m in DN else ref.at[h, z]

    def xy2(self, m):
        if m in DN:
            return self.sb[m].at[0, pl.ds(0, 2)], self.sb[m].at[0, pl.ds(2, 2)]
        return self.sb[m].at[0], self.sb[m].at[1]

    def ag(self, m, slot):
        w, s = self.w[m], self.s
        pair = lambda src, dst, dev: self.copy(src, dst, self.ag_s.at[m, slot], self.ag_r.at[m, slot], dev)
        if slot == 0:
            if m in DN:
                dst = self.ch[m].at[s]
            else:
                rows = self.tmp[m].shape[0]
                dst = self.ch[m].at[pl.ds(s * rows, rows)]
            return pair(self.tmp[m], dst, self.sib)
        if m in PLANE_GATHER:
            if slot <= 3:
                ref = self.blk(w, m, s, self.z, self.yx)
                return pair(ref, ref, (self.xn, self.yn, self.dn)[slot - 1])
            ref = self.plane(w, m, s, (self.z, *self.zz)[(0, 0, 0, 0, 3, 2, 1)[slot - 4]] if slot > 7 else self.z)
            return pair(ref, ref, self.sib if slot >= 7 else self.zn[slot - 4])
        if slot <= 3:
            ref = self.blk(w, m, s, self.z, self.yx)
            return pair(ref, ref, self.zn[slot - 1])
        if slot <= 5:
            ref = self.grp(w, m, s, self.yx)
            return pair(ref, ref, self.xn if slot == 4 else self.yn)
        if slot == 6:
            ref = self.part(w, m, s, 0, self.yx_x)
            return pair(ref, ref, self.yn)
        if slot == 7:
            ref = self.part(w, m, s, 2, self.yx_y)
            return pair(ref, ref, self.xn)
        ref = self.grp(w, m, s, (self.yx, self.yx_x, self.yx_y, self.yx_d)[slot - 8])
        return pair(ref, ref, self.sib)

    def ag0(self, m):
        self.start(self.ag(m, 0))

    def own(self, m):
        self.ag(m, 0).wait_recv()
        chunk = self.ch[m][...].astype(BF)
        if m in DN:
            for sec in (0, 1):
                self.w[m][self.s, sec, self.z, self.yx] = chunk[sec]
        else:
            self.w[m][self.s, self.z, self.yx] = chunk

    def ag1(self, m):
        for slot in (1, 2, 3):
            self.start(self.ag(m, slot))

    def ag2(self, m):
        for slot in (1, 2, 3):
            self.ag(m, slot).wait_recv()
        for slot in (4, 5, 6, 7) if m in PLANE_GATHER else (4, 5, 8):
            self.start(self.ag(m, slot))

    def ag3(self, m):
        chain = ((4, (8,)), (5, (9,)), (6, (10,))) if m in PLANE_GATHER else ((4, (6, 9)), (5, (7, 10)))
        for slot, onward in chain:
            self.ag(m, slot).wait_recv()
            for then in onward:
                self.start(self.ag(m, then))

    def ag4(self, m):
        if m in PLANE_GATHER:
            return
        for slot in (6, 7):
            self.ag(m, slot).wait_recv()
        self.start(self.ag(m, 11))

    def ag5(self, m):
        for slot in (7, 8, 9, 10) if m in PLANE_GATHER else (8, 9, 10, 11):
            self.ag(m, slot).wait_recv()

    def rs(self, m, slot):
        g, s = self.g[m], self.s
        pair = lambda src, dst, dev: self.copy(src, dst, self.rs_s.at[m, slot], self.rs_r.at[m, slot], dev)
        if slot == 0:
            return pair(g.at[1 - s], self.sb[m], self.sib)
        if m in PLANE_REDUCE and slot <= 6:
            if slot <= 3:
                return pair(self.plane(g, m, s, self.zz[slot - 1]), self.zi[m].at[slot - 1], self.zn[slot - 1])
            k = slot - 4
            ref = self.blk(g, m, s, self.z, (self.yx_x, self.yx_y, self.yx_d)[k])
            return pair(ref, self.x1[m].at[k], (self.xn, self.yn, self.dn)[k])
        if slot == 1:
            return pair(self.part(g, m, s, 0, self.yx_d), self.x1[m], self.xn)
        if slot == 2:
            return pair(self.part(g, m, s, 2, self.yx_d), self.y1[m], self.yn)
        if slot == 3:
            return pair(self.grp(g, m, s, self.yx_x), self.xy2(m)[0], self.xn)
        if slot == 4:
            return pair(self.grp(g, m, s, self.yx_y), self.xy2(m)[1], self.yn)
        if slot <= 7:
            k = slot - 5
            return pair(self.blk(g, m, s, self.zz[k], self.yx), self.zi[m].at[k], self.zn[k])
        if m in DN:
            src = self.ch[m].at[1 - s]
        else:
            rows = self.fo[m].shape[0]
            src = self.ch[m].at[pl.ds((1 - s) * rows, rows)]
        return pair(src, self.fo[m], self.sib)

    def rs0(self, m):
        self.start(self.rs(m, 0))

    def rs1(self, m):
        self.rs(m, 0).wait_recv()
        g, sb, s = self.g[m], self.sb[m], self.s

        def add(i, carry):
            if m in DN:
                at = (i // 4, i % 4)
                g[s, at[0], at[1]] = (g[s, at[0], at[1]].astype(F32) + sb[at[0], at[1]].astype(F32)).astype(BF)
            else:
                g[s, i // 4, i % 4] = (g[s, i // 4, i % 4].astype(F32) + sb[i // 4, i % 4].astype(F32)).astype(BF)
            return carry

        lax.fori_loop(0, 8 if m in DN else 16, add, 0)
        for slot in (1, 2, 3) if m in PLANE_REDUCE else (1, 2):
            self.start(self.rs(m, slot))

    def rs2(self, m):
        g, s = self.g[m], self.s
        if m in PLANE_REDUCE:
            for slot in (1, 2, 3):
                self.rs(m, slot).wait_recv()
            zi = self.zi[m]

            def whole(yx):
                parts = [zi[k, yx].astype(F32) for k in (0, 1, 2)]
                return g[s, self.z, yx].astype(F32) + (parts[0] + parts[1] + parts[2])

            for slot, yx in ((4, self.yx_x), (5, self.yx_y), (6, self.yx_d)):
                g[s, self.z, yx] = whole(yx).astype(BF)
                self.start(self.rs(m, slot))
            self.ch[m][...] = whole(self.yx)
            return
        for slot, ref, z0, yx in ((1, self.x1[m], 0, self.yx_y), (2, self.y1[m], 2, self.yx_x)):
            self.rs(m, slot).wait_recv()
            for j in (0, 1):
                if m in DN:
                    for sec in (0, 1):
                        mine = g[s, sec, z0 + j, yx].astype(F32)
                        g[s, sec, z0 + j, yx] = (mine + ref[sec, j].astype(F32)).astype(BF)
                else:
                    mine = g[s, z0 + j, yx].astype(F32)
                    g[s, z0 + j, yx] = (mine + ref[j].astype(F32)).astype(BF)
        self.start(self.rs(m, 3))
        self.start(self.rs(m, 4))

    def rs3(self, m):
        if m in PLANE_REDUCE:
            for slot in (4, 5, 6):
                self.rs(m, slot).wait_recv()
            x1 = self.x1[m]
            self.ch[m][...] += x1[0].astype(F32) + x1[1].astype(F32) + x1[2].astype(F32)
            self.start(self.rs(m, 8))
            return
        self.rs(m, 3).wait_recv()
        self.rs(m, 4).wait_recv()
        g, s, yx = self.g[m], self.s, self.yx
        a, b = self.xy2(m)

        def total(sec, z):
            if m in DN:
                return g[s, sec, z, yx].astype(F32) + a[sec, z].astype(F32) + b[sec, z].astype(F32)
            return g[s, z, yx].astype(F32) + a[z].astype(F32) + b[z].astype(F32)

        for slot in (5, 6, 7):
            zz = self.zz[slot - 5]
            if m in DN:
                for sec in (0, 1):
                    g[s, sec, zz, yx] = total(sec, zz).astype(BF)
            else:
                g[s, zz, yx] = total(0, zz).astype(BF)
            self.start(self.rs(m, slot))
        if m in DN:
            for sec in (0, 1):
                self.ch[m][sec] = total(sec, self.z)
        else:
            self.ch[m][...] = total(0, self.z)

    def rs4(self, m):
        if m in PLANE_REDUCE:
            return
        for slot in (5, 6, 7):
            self.rs(m, slot).wait_recv()
        zi = self.zi[m]
        self.ch[m][...] += zi[0].astype(F32) + zi[1].astype(F32) + zi[2].astype(F32)
        self.start(self.rs(m, 8))

    def rs5(self, m):
        if m in DN:
            mine = self.ch[m][self.s]
        else:
            rows = self.fo[m].shape[0]
            mine = self.ch[m][pl.ds(self.s * rows, rows)]
        self.rs(m, 8).wait_recv()
        return mine, self.fo[m][...]


def kernel(inner, sizes, *refs):
    (byte_ids, lengths, groups, emb, lang, scorer, prenorm, midnorm, rel, wq, wk, wv, wo, wi0, wi1, wd, cot) = refs[:17]
    (enc_out, g_elt, g_q, g_k, g_v, g_o, g_0, g_1, g_d, g_rel) = refs[17:27]
    rest = refs[27:]
    take = lambda k: rest[N * k : N * k + N]
    w, g, sb, x1, y1, zi, ch, tmp, fo = (take(k) for k in range(9))
    rest = rest[9 * N :]
    sems, rest = rest[:6], rest[6:]
    (pi, cb, prow, gthi, gtlo, rows_ref, hid, nrm, nrmt, qs, ks, vs, bvec, pmat, mixed, mixp, mid, sec_ref, sect,
     acc, encb, dq, dk, dv, dvec, relbuf, relin, cp) = rest
    tokens, width, half, ffh = sizes
    quarter = ffh // 4
    net = Net(inner, w, g, sb, x1, y1, zi, ch, tmp, fo, sems)
    s = net.s
    net.hello()

    def lanes(ref, h, n):
        return ref[:, pl.ds(pl.multiple_of(h * n, 128), n)]

    def wmat(m, h):
        return w[m][h].reshape(width, w[m].shape[-1])

    def gput(m, h, value):
        g[m][h] = value.astype(BF).reshape(g[m].shape[1:])

    rows_d = wq.shape[0]
    vocab, langs = emb.shape[1], lang.shape[0]

    def turned(value, at):
        rows = value.shape[0]
        more = -rows % 8
        if more:
            value = jnp.concatenate([value, jnp.zeros((more, rows_d), F32)], axis=0)
        row = iota((rows + more, 512), 0)
        spot = (row + at == iota((rows + more, 512), 1)) & (row < rows)
        return dot_tn(value.astype(BF), jnp.where(spot, 1.0, 0.0).astype(BF))

    vectors = jnp.concatenate([scorer[...], prenorm[...], midnorm[...]], axis=0)
    spread = jnp.where(iota((vocab, 512), 0) == iota((vocab, 512), 1), 1.0, 0.0).astype(BF)
    elt = dot(emb[...].astype(BF), spread) + turned(lang[...], vocab) + turned(vectors, 256 + SCORER)
    wide = {}

    def halves(m, h):
        if m == ELT:
            return jnp.where(h == 0, elt[:, :256], elt[:, 256:])
        if m in (WQ, WK, WV):
            return lanes({WQ: wq, WK: wk, WV: wv}[m], h, half)
        if m in GU:
            cols = pl.ds(pl.multiple_of(h * ffh + (m - GU0) * quarter, 128), quarter)
            return jnp.concatenate([wi0[:, cols], wi1[:, cols]], axis=1)
        value = wide[m]
        return jnp.where(h == 0, value[:, :half], value[:, half:])

    def exchange(m):
        tmp[m][...] = halves(m, 1 - s)
        net.ag0(m)
        mine = halves(m, s)
        if m in DN:
            ch[m][s] = mine
        else:
            ch[m][pl.ds(s * rows_d, rows_d)] = mine

    for m in (ELT, WQ, WK, WV, *GU):
        exchange(m)
    first = (0,)
    for m in first:
        net.own(m)
        net.ag1(m)

    col = iota((1, width), 1)
    chip = over(col, 2 * rows_d)
    inside = col - chip * (2 * rows_d)
    natural = jnp.where(inside < rows_d, chip * rows_d + inside, half + (chip - 1) * rows_d + inside)
    pi[...] = jnp.where(iota((width, width), 0) == natural, 1.0, 0.0).astype(BF)
    wide[WO] = dot(wo[...].astype(BF), pi[...])
    down_p = dot(wd[...].astype(BF), pi[...])
    wide[DNA], wide[DNB] = down_p[: wd.shape[0] // 2], down_p[wd.shape[0] // 2 :]
    for m in (WO, *DN):
        exchange(m)
    for m in ALL:
        if m not in first:
            net.own(m)

    span = 2 * tokens
    heads, buckets = rel.shape
    pairs = width // 128
    keep = {}
    mdel = acc

    def turn_cotangent():
        cp[...] = dot(cot[s], pi[...]).astype(BF)


    def bias_lines():
        ohb = jnp.where(iota((buckets, span), 0) == bucket_ids(iota((buckets, span), 1) - (tokens - 1)), 1.0, 0.0)
        bv = sum(dot(part, ohb.astype(BF)) for part in split3(rel[...]))
        for h in range(heads):
            bvec[h] = bv[h : h + 1, :]

    length = jnp.where(s == 0, lengths[:, 0:1], lengths[:, 1:2])
    group = jnp.where(s == 0, groups[:, 0:1], groups[:, 1:2])

    def block_of(p, size):
        return p if size == 1 else p >> 1 if size == 2 else over(p, 3) if size == 3 else p >> 2

    def count_blocks():
        col = iota((1, span), 1)
        pos = jnp.where(col < tokens, 2 * col, 2 * (col - tokens) + 1)
        symbol = iota((VOC, span), 0)
        onehot = jnp.where(((symbol == byte_ids[s]) | (symbol == group + vocab)) & (col < length), 1.0, 0.0).astype(BF)
        rowi = iota((span, 1), 0)
        for size in range(1, BLOCKS + 1):
            pool = jnp.where(block_of(rowi, size) == block_of(pos, size), 1.0, 0.0).astype(BF)
            cb[size - 1] = dot(onehot, pool).astype(BF)

    def table():
        return wmat(ELT, 0), wmat(ELT, 1)[:, :128]

    def choose_blocks():
        e0, e1 = table()
        picks = jnp.where(iota((8, 128), 1) == iota((8, 128), 0) + SCORER, 1.0, 0.0).astype(BF)
        rows_ref[...] = dot_nt(picks, e1)
        ew = jnp.concatenate([dot_tn(e0, e1), dot_tn(e1, e1)[: VOC - 256]], axis=0)[:, SCORER : SCORER + 1]
        ratings = [jnp.sum(cb[b].astype(F32) * ew, axis=0, keepdims=True) / (b + 1) for b in range(BLOCKS)]
        top = functools.reduce(jnp.maximum, ratings)
        raised = [jnp.exp(r - top) for r in ratings]
        total = sum(raised)
        chosen = [r / total for r in raised]
        mixw = 0.0
        for b in range(BLOCKS):
            prow[b : b + 1, :] = chosen[b]
            mixw = mixw + cb[b].astype(F32) * (chosen[b] / (2.0 * (b + 1)))
        gt = mixw[:, :tokens] + mixw[:, tokens:]
        gt = jnp.concatenate([gt, jnp.zeros((384 - VOC, tokens), F32)], axis=0).T
        gthi[...] = gt.astype(BF)
        gtlo[...] = (gt - gt.astype(BF).astype(F32)).astype(BF)

    def make_hidden():
        e0, e1 = table()
        latent = (
            dot_nt(gthi[:, :256], e0) + dot_nt(gthi[:, 256:], e1)
            + dot_nt(gtlo[:, :256], e0) + dot_nt(gtlo[:, 256:], e1)
        )
        hid[...] = latent.astype(BF)

        hidden = hid[...].astype(F32)
        r1 = lax.rsqrt(jnp.mean(hidden * hidden, -1, keepdims=True) + EPSILON)
        normed = hidden * r1 * rows_ref[1:2, :]
        nrm[...] = normed.astype(BF)
        nrmt[...] = normed.T.astype(BF)

    def project(m, ref):
        for h in (0, 1):
            out = dot(nrm[...], wmat(m, h)).astype(BF)
            for i in range(half // 128):
                ref[h * (half // 128) + i] = out[:, i * 128 : (i + 1) * 128]

    tcol = iota((1, tokens), 1)
    valid_key = DOWN * tcol < length
    lane = iota((1, 128), 1)
    masks = [jnp.where(lane < 64, 1.0 - e, float(e)).astype(BF) for e in (0, 1)]

    def forward_pair(i, carry):
        q2, k2, v2 = qs[i], ks[i], vs[i]
        out = 0.0
        for e in (0, 1):
            h = 2 * i + e
            line = jnp.broadcast_to(bvec[h], (tokens, span))
            bias = pltpu.roll(line, tokens + 1, 1, stride=1, stride_axis=0)[:, :tokens]
            scores = jnp.where(valid_key, dot_nt(q2, k2 * masks[e]) + bias, NEGATIVE)
            up = jnp.exp(scores - jnp.max(scores, -1, keepdims=True))
            prob = up * (1.0 / jnp.sum(up, -1, keepdims=True))
            pmat[h] = prob
            out = out + dot(prob.astype(BF), v2 * masks[e])
        mixed[:, pl.ds(pl.multiple_of(i * 128, 128), 128)] = out.astype(BF)
        return carry

    def forward_pairs(k):
        lax.fori_loop(2 * k, 2 * k + 2, forward_pair, 0)

    def make_middle():
        mixp[...] = dot(mixed[...], pi[...]).astype(BF)
        for h in (0, 1):
            cols = slice(h * half, (h + 1) * half)
            mid[:, cols] = hid[:, cols].astype(F32) + dot(mixp[...], wmat(WO, h))
        middle = mid[...]
        r2 = lax.rsqrt(jnp.mean(middle * middle, -1, keepdims=True) + EPSILON)
        second = middle * r2 * rows_ref[2:3, :]
        sec_ref[...] = second.astype(BF)
        sect[...] = second.T.astype(BF)
        acc[...] = jnp.zeros_like(acc)
        encb[...] = mid[...]

    def feed(c):
        def one(h, carry):
            wgu = w[GU0 + c][h].reshape(width, 2 * quarter)
            wdn = [
                jnp.concatenate([w[m][j, h, c] for m in DN], axis=1).reshape(quarter, half) for j in (0, 1)
            ]
            both = dot(sec_ref[...], wgu)
            gate, upper = both[:, :quarter], both[:, quarter:]
            pdelta = dot_nt(cp[:, :half], wdn[0]) + dot_nt(cp[:, half:], wdn[1])
            square = gate * gate
            tanh = jnp.tanh(0.7978845608 * (gate + 0.044715 * square * gate))
            act = 0.5 * gate * (1.0 + tanh)
            slope = 0.5 * (1.0 + tanh) + 0.5 * gate * (1.0 - tanh * tanh) * 0.7978845608 * (1.0 + 0.134145 * square)
            product = (act * upper).astype(BF)
            delta = jnp.concatenate([(pdelta * upper * slope).astype(BF), (pdelta * act).astype(BF)], axis=1)
            gput(GU0 + c, h, dot(sect[...], delta))
            for j in (0, 1):
                out = slice(j * half, (j + 1) * half)
                grad = dot_tn(product, cp[:, out]).astype(BF).reshape(4, -1, half)
                few = grad.shape[1] // 2
                g[DNA][j, h, c], g[DNB][j, h, c] = grad[:, :few], grad[:, few:]
                encb[:, out] += dot(product, wdn[j])
            acc[...] += dot_nt(delta, wgu)
            return carry

        lax.fori_loop(0, 2, one, 0)

    def middle_back():
        middle = mid[...]
        r2 = lax.rsqrt(jnp.mean(middle * middle, -1, keepdims=True) + EPSILON)
        n2 = middle * r2
        sdelta = acc[...]
        scaled = sdelta * rows_ref[2:3, :]
        rows_ref[4:5, :] = jnp.sum(sdelta * n2, axis=0, keepdims=True)
        mdel[...] = cp[...].astype(F32) + r2 * (scaled - n2 * jnp.mean(scaled * n2, -1, keepdims=True))
        sec_ref[...] = mdel[...].astype(BF)
        for h in (0, 1):
            gput(WO, h, dot_tn(mixp[...], sec_ref[:, h * half : (h + 1) * half]))

    def mixed_back():
        back = dot_nt(sec_ref[:, :half], wmat(WO, 0)) + dot_nt(sec_ref[:, half:], wmat(WO, 1))
        mixp[...] = dot_nt(back.astype(BF), pi[...]).astype(BF)
        mid[...] = jnp.zeros_like(mid)

    flip = jnp.where(iota((tokens, tokens), 0) + iota((tokens, tokens), 1) == tokens - 1, 1.0, 0.0).astype(BF)

    def backward_pair(i, carry):
        cols = pl.ds(pl.multiple_of(i * 128, 128), 128)
        q2, k2, v2, m2 = qs[i], ks[i], vs[i], mixp[:, cols]
        outq = outk = outv = 0.0
        for e in (0, 1):
            h = 2 * i + e
            prob = pmat[h]
            wdelta = dot_nt(m2, v2 * masks[e])
            lean = jnp.sum(prob * wdelta, -1, keepdims=True)
            sd = jnp.where(valid_key, prob * (wdelta - lean), 0.0).astype(BF)
            outq = outq + dot(sd, k2 * masks[e])
            outk = outk + dot_tn(sd, q2 * masks[e])
            outv = outv + dot_tn(prob.astype(BF), m2 * masks[e])
            reverse = jnp.concatenate([dot(sd, flip), jnp.zeros((tokens, tokens), F32)], axis=1)
            skew = pltpu.roll(reverse, 0, 1, stride=1, stride_axis=0)
            dvec[h] = jnp.sum(skew, axis=0, keepdims=True)
        dq[:, cols], dk[:, cols], dv[:, cols] = outq.astype(BF), outk.astype(BF), outv.astype(BF)
        return carry

    def backward_pairs(k):
        lax.fori_loop(2 * k, 2 * k + 2, backward_pair, 0)

    def relative_back():
        ohr = jnp.where(iota((128, span), 0) == bucket_ids((tokens - 1) - iota((128, span), 1)), 1.0, 0.0).astype(BF)
        lines = jnp.concatenate([dvec[h] for h in range(heads)] + [jnp.zeros((16 - heads, span), F32)], axis=0)
        relbuf[0] = sum(dot_nt(part, ohr) for part in split3(lines))
        rel_step(0)

    levels = (
        ((0, net.sib),), ((1, net.xn),), ((2, net.yn),), ((3, net.zn[0]), (4, net.zn[1]), (5, net.zn[2])),
    )

    def rel_copy(slot, level, device):
        return net.copy(relbuf.at[level], relin.at[slot], net.mi_s.at[1 + slot], net.mi_r.at[1 + slot], device)

    def rel_step(level):
        if level:
            for slot, device in levels[level - 1]:
                rel_copy(slot, level - 1, device).wait_recv()
        if level in (1, 2, 3):
            relbuf[level] = relbuf[level - 1] + relin[level - 1]
        if level < 4:
            for slot, device in levels[level]:
                net.start(rel_copy(slot, level, device))
            return
        place = [jnp.where(net.z == k, 1.0, 0.0) for k in range(4)]
        level = [relbuf[3], relin[3], relin[4], relin[5]]
        summed = 0.0
        for k in range(4):
            summed = summed + sum(place[z] * level[(z - k) % 4] for z in range(4))
        g_rel[...] = summed

    def weight_back(k):
        m, ref = ((WQ, dq), (WK, dk), (WV, dv))[k]
        for h in (0, 1):
            part = ref[:, h * half : (h + 1) * half]
            gput(m, h, dot(nrmt[...], part))
            mid[...] += dot_nt(part, wmat(m, h))

    def hidden_back():
        hidden = hid[...].astype(F32)
        norm_delta = mid[...]
        r1 = lax.rsqrt(jnp.mean(hidden * hidden, -1, keepdims=True) + EPSILON)
        n1 = hidden * r1
        scaled = norm_delta * rows_ref[1:2, :]
        rows_ref[3:4, :] = jnp.sum(norm_delta * n1, axis=0, keepdims=True)
        delta = mdel[...] + r1 * (scaled - n1 * jnp.mean(scaled * n1, -1, keepdims=True))
        sec_ref[...] = delta.astype(BF)

    def choice_back():
        e0, e1 = table()
        hdel = sec_ref[...]
        back = jnp.concatenate([dot(hdel, e0), dot(hdel, e1)], axis=1).T[:VOC]
        back = jnp.concatenate([back, back], axis=1)
        pdel = [jnp.sum(cb[b].astype(F32) * back, axis=0, keepdims=True) / (2.0 * (b + 1)) for b in range(BLOCKS)]
        lean = sum(prow[b : b + 1, :] * pdel[b] for b in range(BLOCKS))
        flow = 0.0
        for b in range(BLOCKS):
            flow = flow + cb[b].astype(F32) * (prow[b : b + 1, :] * (pdel[b] - lean) / (b + 1))
        gs = jnp.sum(flow, axis=1, keepdims=True)
        lane_v = iota((VOC, 128), 1)
        parts = [p.astype(F32) for p in split3(gs)]
        gs3 = jnp.where(lane_v == 0, parts[0], jnp.where(lane_v == 1, parts[1], jnp.where(lane_v == 2, parts[2], 0.0)))
        gs3 = gs3.astype(BF)
        keep[0] = gs3

    def table_back():
        e0, e1 = table()
        hdel, gs3 = sec_ref[...], keep[0]
        lane_w = iota((width, 128), 1)
        wcol = jnp.where(lane_w < 3, e1.astype(F32)[:, SCORER : SCORER + 1], 0.0).astype(BF)
        gput(ELT, 0, dot_tn(hdel, gthi[:, :256]) + dot_tn(hdel, gtlo[:, :256]) + dot_nt(wcol, gs3[:256]))
        gs_tail = jnp.concatenate([gs3[256:], jnp.zeros((128 + 256 - VOC, 128), BF)], axis=0)
        tail = dot_tn(hdel, gthi[:, 256:]) + dot_tn(hdel, gtlo[:, 256:]) + dot_nt(wcol, gs_tail)
        scorer_grad = jnp.sum(dot(e0, gs3[:256]) + dot(e1, gs_tail), axis=1, keepdims=True)
        gains = [p.astype(F32) for p in (*split3(rows_ref[3:4, :]), *split3(rows_ref[4:5, :]))]
        gains = jnp.concatenate([*gains, jnp.zeros((10, width), F32)], axis=0).astype(BF)
        place_row, place_col = iota((16, 128), 0), iota((16, 128), 1)
        place = (place_row < 6) & (place_col == jnp.where(place_row < 3, SCORER + 1, SCORER + 2))
        tail = tail + dot_tn(gains, jnp.where(place, 1.0, 0.0).astype(BF))
        tail = jnp.where(lane_w == SCORER, scorer_grad, tail)
        gput(ELT, 1, jnp.concatenate([tail, jnp.zeros((width, 128), F32)], axis=1))


    enc_copy = net.copy(
        mixed.at[:, pl.ds(pl.multiple_of((1 - s) * half, 128), half)], enc_out.at[s],
        net.mi_s.at[0], net.mi_r.at[0], net.sib,
    )

    def send_encoded():
        encoded = dot_nt(encb[...].astype(BF), pi[...]).astype(BF)
        for h in (0, 1):
            mixed[:, h * half : (h + 1) * half] = encoded[:, h * half : (h + 1) * half]
        enc_out[s] = lanes(mixed, s, half)
        net.start(enc_copy)

    def last(m):
        mine, other = net.rs5(m)
        if m == WO or m in DN:
            first = jnp.where(s == 0, mine, other)
            second = jnp.where(s == 0, other, mine)
            both = jnp.concatenate([first, second], axis=1)
            value = sum(dot_nt(part, pi[...]) for part in split3(both))
            if m == WO:
                g_o[...] = value
            else:
                rows = value.shape[0]
                g_d[(m - DNA) * rows : (m - DNA + 1) * rows, :] = value
            return
        for h, value in ((s, mine), (1 - s, other)):
            if m in GU:
                cols = pl.ds(pl.multiple_of(h * ffh + (m - GU0) * quarter, 128), quarter)
                g_0[:, cols] = value[:, :quarter]
                g_1[:, cols] = value[:, quarter:]
            else:
                n = value.shape[1]
                target = {ELT: g_elt, WQ: g_q, WK: g_k, WV: g_v}[m]
                target[:, pl.ds(pl.multiple_of(h * n, 128), n)] = value

    pieces = (
        turn_cotangent, bias_lines, count_blocks, choose_blocks, make_hidden,
        *(functools.partial(project, *item) for item in ((WQ, qs), (WK, ks), (WV, vs))),
        *(functools.partial(forward_pairs, k) for k in range(pairs // 2)),
        make_middle,
        *(functools.partial(feed, c) for c in range(4)),
        middle_back, mixed_back,
        *(functools.partial(backward_pairs, k) for k in range(pairs // 2)),
        relative_back,
        *(functools.partial(weight_back, k) for k in range(3)),
        hidden_back, choice_back, table_back, send_encoded,
    )
    steps = {
        "A": net.ag1, "Z": net.ag2, "X": net.ag3, "D": net.ag4, "S": net.ag5,
        "a": net.rs0, "b": net.rs1, "c": net.rs2, "d": net.rs3, "e": net.rs4, "f": last,
        "p": lambda k: pieces[k](), "r": rel_step,
    }
    for kind, index in SCHEDULE:
        steps[kind](index)
    enc_copy.wait_recv()
    net.finish()


VMEM = pl.BlockSpec(memory_space=pltpu.VMEM)


def call(inner, *args):
    wq, wi0, wd, cot = args[9], args[13], args[15], args[16]
    rows_d, width = wq.shape
    rows_f = wd.shape[0] // 2
    half, ffh = width // 2, wi0.shape[1] // 2
    tokens = cot.shape[1]
    span = 2 * tokens
    heads, buckets = args[8].shape
    wide = {m: 256 if m == ELT else ffh // 2 if m in GU else half for m in ALL}
    chip = {m: (2, rows_f) if m in DN else (2 * rows_d,) for m in ALL}
    mine = {m: rows_f if m in DN else rows_d for m in ALL}

    def full(m):
        return (2, 4, 4, rows_f, wide[m]) if m in DN else (4, 4, 2 * rows_d, wide[m])

    def part(m):
        return (2, 2, rows_f, wide[m]) if m in DN else (2, 2 * rows_d, wide[m])

    scratch = []
    scratch += [pltpu.VMEM((2, *full(m)), BF) for m in ALL]
    scratch += [pltpu.VMEM((2, *full(m)), BF) for m in ALL]
    scratch += [pltpu.VMEM(full(m), BF) for m in ALL]
    scratch += [
        pltpu.VMEM((3, *part(m)[1:]) if m in PLANE_REDUCE else part(m), BF) for m in ALL
    ]
    scratch += [pltpu.VMEM((16, 128) if m in PLANE_REDUCE else part(m), BF) for m in ALL]
    scratch += [
        pltpu.VMEM((3, *((4,) if m in PLANE_REDUCE else ()), *chip[m], wide[m]), BF) for m in ALL
    ]
    scratch += [pltpu.VMEM((*chip[m], wide[m]), F32) for m in ALL]
    scratch += [pltpu.VMEM((mine[m], wide[m]), F32) for m in ALL]
    scratch += [pltpu.VMEM((mine[m], wide[m]), F32) for m in ALL]
    dma = pltpu.SemaphoreType.DMA
    scratch += [dma((N, 12)), dma((N, 12)), dma((N, 9)), dma((N, 9)), dma((7,)), dma((7,))]
    act = (tokens, width)
    scratch += [
        pltpu.VMEM((width, width), BF),
        pltpu.VMEM((BLOCKS, VOC, span), BF),
        pltpu.VMEM((8, span), F32),
        pltpu.VMEM((tokens, 384), BF),
        pltpu.VMEM((tokens, 384), BF),
        pltpu.VMEM((8, width), F32),
        pltpu.VMEM(act, BF),
        pltpu.VMEM(act, BF),
        pltpu.VMEM((width, tokens), BF),
        pltpu.VMEM((width // 128, tokens, 128), BF),
        pltpu.VMEM((width // 128, tokens, 128), BF),
        pltpu.VMEM((width // 128, tokens, 128), BF),
        pltpu.VMEM((heads, 1, span), F32),
        pltpu.VMEM((heads, tokens, tokens), F32),
        pltpu.VMEM(act, BF),
        pltpu.VMEM(act, BF),
        pltpu.VMEM(act, F32),
        pltpu.VMEM(act, BF),
        pltpu.VMEM((width, tokens), BF),
        pltpu.VMEM(act, F32),
        pltpu.VMEM(act, F32),
        pltpu.VMEM(act, BF),
        pltpu.VMEM(act, BF),
        pltpu.VMEM(act, BF),
        pltpu.VMEM((heads, 1, span), F32),
        pltpu.VMEM((4, 16, 128), F32),
        pltpu.VMEM((6, 16, 128), F32),
        pltpu.VMEM(act, BF),
    ]
    outs = [
        jax.ShapeDtypeStruct((MICRO, tokens, half), BF),
        jax.ShapeDtypeStruct((rows_d, 512), F32),
        *[jax.ShapeDtypeStruct(item.shape, F32) for item in args[9:16]],
        jax.ShapeDtypeStruct((16, 128), F32),
    ]
    return pl.pallas_call(
        functools.partial(kernel, inner, (tokens, width, half, ffh)),
        out_shape=outs,
        in_specs=[VMEM] * len(args),
        out_specs=[VMEM] * len(outs),
        scratch_shapes=scratch,
        compiler_params=pltpu.CompilerParams(
            collective_id=0, has_side_effects=True, vmem_limit_bytes=63 * 2**20
        ),
    )(*args)


def settle(vocab, langs, heads, buckets, *refs):
    ins, outs = refs[:10], refs[10:]
    outs[0][:, 0] = ins[0][...]
    rows = ins[1].shape[0]
    outs[1][...] = ins[1][:, :vocab]
    table = ins[1][:, 256:]
    table = jnp.concatenate([table, jnp.zeros((128 - rows, 256), F32)], axis=0).T[:, :rows]
    at = vocab - 256
    outs[2][...] = table[at : at + langs]
    at = at + langs
    for k, i in enumerate((3, 4, 9)):
        outs[i][...] = table[at + k : at + k + 1]
    for i, k in zip((5, 6, 7, 8, 10, 11, 12), range(2, 9)):
        outs[i][...] = ins[k][...]
    outs[13][...] = ins[9][:heads, :buckets]


def body(
    byte_ids, lengths, groups, embedding, language, scorer, prenorm, query_weight, key_weight, value_weight,
    output_weight, midnorm, gate_weight, up_weight, down_weight, relative, cotangent,
):
    inner = lax.axis_size("dp") // OUTER
    vocab, langs = embedding.shape[0], language.shape[0]
    tables = [embedding.T, language, scorer[None], prenorm[None], midnorm[None]]
    weights = [query_weight, key_weight, value_weight, output_weight, gate_weight, up_weight, down_weight]
    teams = [[o * inner + i for i in range(inner)] for o in range(OUTER)]
    if inner > 1:
        tables = [
            lax.all_gather(item, "dp", axis_index_groups=teams, axis=min(i, 1), tiled=True)
            for i, item in enumerate(tables)
        ]
        weights = [lax.all_gather(item, "dp", axis_index_groups=teams, axis=0, tiled=True) for item in weights]
    results = call(inner, byte_ids, lengths.T, groups.T, *tables, relative.T, *weights, cotangent[:, 0])
    if inner > 1:
        grads = [
            lax.psum_scatter(item, "dp", axis_index_groups=teams, scatter_dimension=0, tiled=True)
            for item in results[1:9]
        ]
        results = [results[0], *grads, lax.psum(results[9], "dp", axis_index_groups=teams)]
    buckets, heads = relative.shape
    rows = results[1].shape[0]
    line = jax.ShapeDtypeStruct((1, rows), F32)
    like = [jax.ShapeDtypeStruct(item.shape, F32) for item in results[2:9]]
    shapes = [
        jax.ShapeDtypeStruct(cotangent.shape[:3] + (results[0].shape[2],), BF),
        jax.ShapeDtypeStruct((rows, vocab), F32),
        jax.ShapeDtypeStruct((langs, rows), F32),
        line, line, *like[:4], line, *like[4:],
        jax.ShapeDtypeStruct((heads, buckets), F32),
    ]
    outs = pl.pallas_call(
        functools.partial(settle, vocab, langs, heads, buckets),
        out_shape=shapes,
        in_specs=[VMEM] * 10,
        out_specs=[VMEM] * 14,
        compiler_params=pltpu.CompilerParams(vmem_limit_bytes=60 * 2**20),
    )(*results)
    return tuple(item[0] if i in (3, 4, 9) else item.T if i in (1, 13) else item for i, item in enumerate(outs))


def solution(mesh):
    both = ("section", "dp")
    wide = P(both, None)
    return jax.shard_map(
        body,
        mesh=mesh,
        in_specs=(
            P(None, "dp", None), P(None, "dp"), P(None, "dp"), P(None, both), P(None, both), P(both), P(both),
            wide, wide, wide, wide, P(both), wide, wide, wide, P(), P(None, "dp", None, None),
        ),
        out_specs=(
            P(None, "dp", None, "section"), P(None, both), P(None, both), P(both), P(both),
            wide, wide, wide, wide, P(both), wide, wide, wide, P(),
        ),
        check_vma=False,
    )
```

```python
import functools

import jax
import jax.numpy as jnp
from jax import lax
from jax.experimental import pallas as pl
from jax.experimental.pallas import tpu as pltpu
from jax.sharding import PartitionSpec as P

BLOCKS = 4
DOWN = 2
MICRO = 2
OUTER = 16
EPSILON = 1e-06
NEGATIVE = -1000000000.0
LIMITS = (12, 16, 23, 32, 46, 64, 91)
MESH = pl.DeviceIdType.MESH
BF = jnp.bfloat16
F32 = jnp.float32
I32 = jnp.int32

ELT, WQ, WK, WV, WO, DNA, DNB, GU0, GU1, GU2, GU3 = range(11)
DN = (DNA, DNB)
GU = (GU0, GU1, GU2, GU3)
ALL = tuple(range(11))
N = len(ALL)
PLANE_GATHER = (10,)
PLANE_REDUCE = ()
SCHEDULE = (
    ("A", 10), ("Z", 0), ("A", 2), ("p", 0), ("p", 1), ("Z", 1), ("A", 3), ("X", 0), ("p", 2), ("Z", 2), ("A", 4),
    ("X", 1), ("D", 0), ("S", 0), ("p", 3), ("Z", 3), ("A", 5), ("X", 2), ("D", 1), ("p", 4), ("S", 1), ("p", 5),
    ("Z", 4), ("A", 6), ("X", 3), ("D", 2), ("S", 2), ("p", 6), ("Z", 5), ("A", 7), ("X", 4), ("D", 3), ("S", 3),
    ("p", 7), ("p", 8), ("Z", 6), ("A", 8), ("X", 5), ("D", 4), ("p", 9), ("S", 4), ("p", 10), ("Z", 7), ("A", 9),
    ("X", 6), ("D", 5), ("p", 11), ("S", 5), ("Z", 8), ("X", 7), ("D", 6), ("S", 6), ("Z", 9), ("Z", 10), ("X", 8),
    ("D", 7), ("S", 7), ("p", 12), ("a", 7), ("X", 9), ("D", 8), ("S", 8), ("b", 7), ("p", 13), ("a", 8), ("D", 9),
    ("b", 8), ("c", 7), ("S", 9), ("p", 14), ("a", 9), ("b", 9), ("c", 8), ("d", 7), ("X", 10), ("S", 10), ("p", 15),
    ("a", 10), ("a", 5), ("a", 6), ("c", 9), ("d", 8), ("e", 7), ("p", 16), ("b", 10), ("b", 5), ("a", 4), ("c", 10),
    ("d", 9), ("e", 8), ("p", 17), ("p", 18), ("p", 19), ("b", 6), ("c", 5), ("d", 10), ("e", 9), ("f", 7), ("p", 20),
    ("p", 21), ("p", 22), ("a", 1), ("b", 4), ("c", 6), ("d", 5), ("e", 10), ("p", 23), ("a", 2), ("p", 24), ("a", 3),
    ("b", 1), ("c", 4), ("d", 6), ("e", 5), ("f", 8), ("p", 25), ("r", 1), ("p", 26), ("b", 2), ("c", 1), ("d", 4),
    ("e", 6), ("p", 27), ("a", 0), ("r", 2), ("b", 3), ("c", 2), ("d", 1), ("e", 4), ("f", 9), ("f", 10), ("p", 28),
    ("r", 3), ("b", 0), ("c", 3), ("d", 2), ("e", 1), ("f", 5), ("f", 6), ("r", 4), ("c", 0), ("d", 3), ("e", 2),
    ("f", 1), ("f", 4), ("d", 0), ("e", 3), ("f", 2), ("e", 0), ("f", 3), ("f", 0),
)
VOC = 288
SCORER = 19


def dot(a, b):
    return lax.dot_general(a, b, (((1,), (0,)), ((), ())), preferred_element_type=F32)


def dot_nt(a, b):
    return lax.dot_general(a, b, (((1,), (1,)), ((), ())), preferred_element_type=F32)


def dot_tn(a, b):
    return lax.dot_general(a, b, (((0,), (0,)), ((), ())), preferred_element_type=F32)


def split3(x):
    hi = x.astype(BF)
    rest = x - hi.astype(F32)
    mid = rest.astype(BF)
    return hi, mid, (rest - mid.astype(F32)).astype(BF)


def iota(shape, axis):
    return lax.broadcasted_iota(I32, shape, axis)


def over(value, n):
    return (value * (65536 // n + 1)) >> 16


def bucket_ids(offsets):
    distance = jnp.abs(offsets)
    larger = 8 + sum(((distance >= limit).astype(I32) for limit in LIMITS))
    inside = jnp.where(distance < 8, distance, larger)
    return jnp.where(offsets > 0, 16, 0).astype(I32) + inside


class Net:
    def __init__(self, inner, w, g, sb, x1, y1, zi, ch, tmp, fo, sems):
        self.w, self.g, self.sb, self.x1, self.y1 = w, g, sb, x1, y1
        self.zi, self.ch, self.tmp, self.fo = zi, ch, tmp, fo
        self.ag_s, self.ag_r, self.rs_s, self.rs_r, self.mi_s, self.mi_r = sems
        self.s = lax.axis_index("section")
        self.d = lax.axis_index("dp")
        outer = self.d // inner
        self.z = outer // 4
        self.yx = outer % 4
        y, x = self.yx // 2, self.yx % 2
        self.sib = (1 - self.s, self.d)
        self.yx_x = self.yx + 1 - 2 * x
        self.yx_y = self.yx + 2 - 4 * y
        self.yx_d = 3 - self.yx
        self.xn = (self.s, self.d + (1 - 2 * x) * inner)
        self.yn = (self.s, self.d + (1 - 2 * y) * 2 * inner)
        self.dn = (self.s, self.d + (1 - 2 * x) * inner + (1 - 2 * y) * 2 * inner)
        self.zz = [(self.z + k) % 4 for k in (1, 2, 3)]
        self.zn = [(self.s, self.d + (zz - self.z) * 4 * inner) for zz in self.zz]
        self.sent = []

    def hello(self):
        barrier = pltpu.get_barrier_semaphore()
        for device in (self.sib, self.xn, self.yn, self.dn, *self.zn):
            pl.semaphore_signal(barrier, inc=1, device_id=device, device_id_type=MESH)
        pl.semaphore_wait(barrier, 7)

    def copy(self, src, dst, send, recv, device):
        return pltpu.make_async_remote_copy(
            src_ref=src, dst_ref=dst, send_sem=send, recv_sem=recv,
            device_id=device, device_id_type=MESH,
        )

    def start(self, copy):
        copy.start()
        self.sent.append(copy)

    def finish(self):
        for copy in self.sent:
            copy.wait_send()
        self.sent = []

    def blk(self, ref, m, h, z, yx):
        return ref.at[h, :, z, yx] if m in DN else ref.at[h, z, yx]

    def grp(self, ref, m, h, yx):
        return ref.at[h, :, :, yx] if m in DN else ref.at[h, :, yx]

    def part(self, ref, m, h, z0, yx):
        return ref.at[h, :, pl.ds(z0, 2), yx] if m in DN else ref.at[h, pl.ds(z0, 2), yx]

    def plane(self, ref, m, h, z):
        return ref.at[h, :, z] if m in DN else ref.at[h, z]

    def xy2(self, m):
        if m in DN:
            return self.sb[m].at[0, pl.ds(0, 2)], self.sb[m].at[0, pl.ds(2, 2)]
        return self.sb[m].at[0], self.sb[m].at[1]

    def ag(self, m, slot):
        w, s = self.w[m], self.s
        pair = lambda src, dst, dev: self.copy(src, dst, self.ag_s.at[m, slot], self.ag_r.at[m, slot], dev)
        if slot == 0:
            if m in DN:
                dst = self.ch[m].at[s]
            else:
                rows = self.tmp[m].shape[0]
                dst = self.ch[m].at[pl.ds(s * rows, rows)]
            return pair(self.tmp[m], dst, self.sib)
        if m in PLANE_GATHER:
            if slot <= 3:
                ref = self.blk(w, m, s, self.z, self.yx)
                return pair(ref, ref, (self.xn, self.yn, self.dn)[slot - 1])
            ref = self.plane(w, m, s, (self.z, *self.zz)[(0, 0, 0, 0, 3, 2, 1)[slot - 4]] if slot > 7 else self.z)
            return pair(ref, ref, self.sib if slot >= 7 else self.zn[slot - 4])
        if slot <= 3:
            ref = self.blk(w, m, s, self.z, self.yx)
            return pair(ref, ref, self.zn[slot - 1])
        if slot <= 5:
            ref = self.grp(w, m, s, self.yx)
            return pair(ref, ref, self.xn if slot == 4 else self.yn)
        if slot == 6:
            ref = self.part(w, m, s, 0, self.yx_x)
            return pair(ref, ref, self.yn)
        if slot == 7:
            ref = self.part(w, m, s, 2, self.yx_y)
            return pair(ref, ref, self.xn)
        ref = self.grp(w, m, s, (self.yx, self.yx_x, self.yx_y, self.yx_d)[slot - 8])
        return pair(ref, ref, self.sib)

    def ag0(self, m):
        self.start(self.ag(m, 0))

    def own(self, m):
        self.ag(m, 0).wait_recv()
        chunk = self.ch[m][...].astype(BF)
        if m in DN:
            for sec in (0, 1):
                self.w[m][self.s, sec, self.z, self.yx] = chunk[sec]
        else:
            self.w[m][self.s, self.z, self.yx] = chunk

    def ag1(self, m):
        for slot in (1, 2, 3):
            self.start(self.ag(m, slot))

    def ag2(self, m):
        for slot in (1, 2, 3):
            self.ag(m, slot).wait_recv()
        for slot in (4, 5, 6, 7) if m in PLANE_GATHER else (4, 5, 8):
            self.start(self.ag(m, slot))

    def ag3(self, m):
        chain = ((4, (8,)), (5, (9,)), (6, (10,))) if m in PLANE_GATHER else ((4, (6, 9)), (5, (7, 10)))
        for slot, onward in chain:
            self.ag(m, slot).wait_recv()
            for then in onward:
                self.start(self.ag(m, then))

    def ag4(self, m):
        if m in PLANE_GATHER:
            return
        for slot in (6, 7):
            self.ag(m, slot).wait_recv()
        self.start(self.ag(m, 11))

    def ag5(self, m):
        for slot in (7, 8, 9, 10) if m in PLANE_GATHER else (8, 9, 10, 11):
            self.ag(m, slot).wait_recv()

    def rs(self, m, slot):
        g, s = self.g[m], self.s
        pair = lambda src, dst, dev: self.copy(src, dst, self.rs_s.at[m, slot], self.rs_r.at[m, slot], dev)
        if slot == 0:
            return pair(g.at[1 - s], self.sb[m], self.sib)
        if m in PLANE_REDUCE and slot <= 6:
            if slot <= 3:
                return pair(self.plane(g, m, s, self.zz[slot - 1]), self.zi[m].at[slot - 1], self.zn[slot - 1])
            k = slot - 4
            ref = self.blk(g, m, s, self.z, (self.yx_x, self.yx_y, self.yx_d)[k])
            return pair(ref, self.x1[m].at[k], (self.xn, self.yn, self.dn)[k])
        if slot == 1:
            return pair(self.part(g, m, s, 0, self.yx_d), self.x1[m], self.xn)
        if slot == 2:
            return pair(self.part(g, m, s, 2, self.yx_d), self.y1[m], self.yn)
        if slot == 3:
            return pair(self.grp(g, m, s, self.yx_x), self.xy2(m)[0], self.xn)
        if slot == 4:
            return pair(self.grp(g, m, s, self.yx_y), self.xy2(m)[1], self.yn)
        if slot <= 7:
            k = slot - 5
            return pair(self.blk(g, m, s, self.zz[k], self.yx), self.zi[m].at[k], self.zn[k])
        if m in DN:
            src = self.ch[m].at[1 - s]
        else:
            rows = self.fo[m].shape[0]
            src = self.ch[m].at[pl.ds((1 - s) * rows, rows)]
        return pair(src, self.fo[m], self.sib)

    def rs0(self, m):
        self.start(self.rs(m, 0))

    def rs1(self, m):
        self.rs(m, 0).wait_recv()
        g, sb, s = self.g[m], self.sb[m], self.s

        def add(i, carry):
            if m in DN:
                at = (i // 4, i % 4)
                g[s, at[0], at[1]] = (g[s, at[0], at[1]].astype(F32) + sb[at[0], at[1]].astype(F32)).astype(BF)
            else:
                g[s, i // 4, i % 4] = (g[s, i // 4, i % 4].astype(F32) + sb[i // 4, i % 4].astype(F32)).astype(BF)
            return carry

        lax.fori_loop(0, 8 if m in DN else 16, add, 0)
        for slot in (1, 2, 3) if m in PLANE_REDUCE else (1, 2):
            self.start(self.rs(m, slot))

    def rs2(self, m):
        g, s = self.g[m], self.s
        if m in PLANE_REDUCE:
            for slot in (1, 2, 3):
                self.rs(m, slot).wait_recv()
            zi = self.zi[m]

            def whole(yx):
                parts = [zi[k, yx].astype(F32) for k in (0, 1, 2)]
                return g[s, self.z, yx].astype(F32) + (parts[0] + parts[1] + parts[2])

            for slot, yx in ((4, self.yx_x), (5, self.yx_y), (6, self.yx_d)):
                g[s, self.z, yx] = whole(yx).astype(BF)
                self.start(self.rs(m, slot))
            self.ch[m][...] = whole(self.yx)
            return
        for slot, ref, z0, yx in ((1, self.x1[m], 0, self.yx_y), (2, self.y1[m], 2, self.yx_x)):
            self.rs(m, slot).wait_recv()
            for j in (0, 1):
                if m in DN:
                    for sec in (0, 1):
                        mine = g[s, sec, z0 + j, yx].astype(F32)
                        g[s, sec, z0 + j, yx] = (mine + ref[sec, j].astype(F32)).astype(BF)
                else:
                    mine = g[s, z0 + j, yx].astype(F32)
                    g[s, z0 + j, yx] = (mine + ref[j].astype(F32)).astype(BF)
        self.start(self.rs(m, 3))
        self.start(self.rs(m, 4))

    def rs3(self, m):
        if m in PLANE_REDUCE:
            for slot in (4, 5, 6):
                self.rs(m, slot).wait_recv()
            x1 = self.x1[m]
            self.ch[m][...] += x1[0].astype(F32) + x1[1].astype(F32) + x1[2].astype(F32)
            self.start(self.rs(m, 8))
            return
        self.rs(m, 3).wait_recv()
        self.rs(m, 4).wait_recv()
        g, s, yx = self.g[m], self.s, self.yx
        a, b = self.xy2(m)

        def total(sec, z):
            if m in DN:
                return g[s, sec, z, yx].astype(F32) + a[sec, z].astype(F32) + b[sec, z].astype(F32)
            return g[s, z, yx].astype(F32) + a[z].astype(F32) + b[z].astype(F32)

        for slot in (5, 6, 7):
            zz = self.zz[slot - 5]
            if m in DN:
                for sec in (0, 1):
                    g[s, sec, zz, yx] = total(sec, zz).astype(BF)
            else:
                g[s, zz, yx] = total(0, zz).astype(BF)
            self.start(self.rs(m, slot))
        if m in DN:
            for sec in (0, 1):
                self.ch[m][sec] = total(sec, self.z)
        else:
            self.ch[m][...] = total(0, self.z)

    def rs4(self, m):
        if m in PLANE_REDUCE:
            return
        for slot in (5, 6, 7):
            self.rs(m, slot).wait_recv()
        zi = self.zi[m]
        self.ch[m][...] += zi[0].astype(F32) + zi[1].astype(F32) + zi[2].astype(F32)
        self.start(self.rs(m, 8))

    def rs5(self, m):
        if m in DN:
            mine = self.ch[m][self.s]
        else:
            rows = self.fo[m].shape[0]
            mine = self.ch[m][pl.ds(self.s * rows, rows)]
        self.rs(m, 8).wait_recv()
        return mine, self.fo[m][...]


def kernel(inner, sizes, *refs):
    (byte_ids, lengths, groups, emb, lang, scorer, prenorm, midnorm, rel, wq, wk, wv, wo, wi0, wi1, wd, cot) = refs[:17]
    (enc_out, g_elt, g_q, g_k, g_v, g_o, g_0, g_1, g_d, g_rel) = refs[17:27]
    rest = refs[27:]
    take = lambda k: rest[N * k : N * k + N]
    w, g, sb, x1, y1, zi, ch, tmp, fo = (take(k) for k in range(9))
    rest = rest[9 * N :]
    sems, rest = rest[:6], rest[6:]
    (pi, cb, prow, gthi, gtlo, rows_ref, hid, nrm, nrmt, qs, ks, vs, bvec, pmat, mixed, mixp, mid, sec_ref, sect,
     acc, encb, dq, dk, dv, dvec, relbuf, relin, cp) = rest
    tokens, width, half, ffh = sizes
    quarter = ffh // 4
    net = Net(inner, w, g, sb, x1, y1, zi, ch, tmp, fo, sems)
    s = net.s
    net.hello()

    def lanes(ref, h, n):
        return ref[:, pl.ds(pl.multiple_of(h * n, 128), n)]

    def wmat(m, h):
        return w[m][h].reshape(width, w[m].shape[-1])

    def gput(m, h, value):
        g[m][h] = value.astype(BF).reshape(g[m].shape[1:])

    rows_d = wq.shape[0]
    vocab, langs = emb.shape[1], lang.shape[0]

    def turned(value, at):
        rows = value.shape[0]
        more = -rows % 8
        if more:
            value = jnp.concatenate([value, jnp.zeros((more, rows_d), F32)], axis=0)
        row = iota((rows + more, 512), 0)
        spot = (row + at == iota((rows + more, 512), 1)) & (row < rows)
        return dot_tn(value.astype(BF), jnp.where(spot, 1.0, 0.0).astype(BF))

    vectors = jnp.concatenate([scorer[...], prenorm[...], midnorm[...]], axis=0)
    spread = jnp.where(iota((vocab, 512), 0) == iota((vocab, 512), 1), 1.0, 0.0).astype(BF)
    elt = dot(emb[...].astype(BF), spread) + turned(lang[...], vocab) + turned(vectors, 256 + SCORER)
    wide = {}

    def halves(m, h):
        if m == ELT:
            return jnp.where(h == 0, elt[:, :256], elt[:, 256:])
        if m in (WQ, WK, WV):
            return lanes({WQ: wq, WK: wk, WV: wv}[m], h, half)
        if m in GU:
            cols = pl.ds(pl.multiple_of(h * ffh + (m - GU0) * quarter, 128), quarter)
            return jnp.concatenate([wi0[:, cols], wi1[:, cols]], axis=1)
        value = wide[m]
        return jnp.where(h == 0, value[:, :half], value[:, half:])

    def exchange(m):
        tmp[m][...] = halves(m, 1 - s)
        net.ag0(m)
        mine = halves(m, s)
        if m in DN:
            ch[m][s] = mine
        else:
            ch[m][pl.ds(s * rows_d, rows_d)] = mine

    for m in (ELT, WQ, WK, WV, *GU):
        exchange(m)
    first = (0, 1,)
    for m in first:
        net.own(m)
        net.ag1(m)

    col = iota((1, width), 1)
    chip = over(col, 2 * rows_d)
    inside = col - chip * (2 * rows_d)
    natural = jnp.where(inside < rows_d, chip * rows_d + inside, half + (chip - 1) * rows_d + inside)
    pi[...] = jnp.where(iota((width, width), 0) == natural, 1.0, 0.0).astype(BF)
    wide[WO] = dot(wo[...].astype(BF), pi[...])
    down_p = dot(wd[...].astype(BF), pi[...])
    wide[DNA], wide[DNB] = down_p[: wd.shape[0] // 2], down_p[wd.shape[0] // 2 :]
    for m in (WO, *DN):
        exchange(m)
    for m in ALL:
        if m not in first:
            net.own(m)

    span = 2 * tokens
    heads, buckets = rel.shape
    pairs = width // 128
    keep = {}
    mdel = acc

    def turn_cotangent():
        cp[...] = dot(cot[s], pi[...]).astype(BF)


    def bias_lines():
        ohb = jnp.where(iota((buckets, span), 0) == bucket_ids(iota((buckets, span), 1) - (tokens - 1)), 1.0, 0.0)
        bv = sum(dot(part, ohb.astype(BF)) for part in split3(rel[...]))
        for h in range(heads):
            bvec[h] = bv[h : h + 1, :]

    length = jnp.where(s == 0, lengths[:, 0:1], lengths[:, 1:2])
    group = jnp.where(s == 0, groups[:, 0:1], groups[:, 1:2])

    def block_of(p, size):
        return p if size == 1 else p >> 1 if size == 2 else over(p, 3) if size == 3 else p >> 2

    def count_blocks():
        col = iota((1, span), 1)
        pos = jnp.where(col < tokens, 2 * col, 2 * (col - tokens) + 1)
        symbol = iota((VOC, span), 0)
        onehot = jnp.where(((symbol == byte_ids[s]) | (symbol == group + vocab)) & (col < length), 1.0, 0.0).astype(BF)
        rowi = iota((span, 1), 0)
        for size in range(1, BLOCKS + 1):
            pool = jnp.where(block_of(rowi, size) == block_of(pos, size), 1.0, 0.0).astype(BF)
            cb[size - 1] = dot(onehot, pool).astype(BF)

    def table():
        return wmat(ELT, 0), wmat(ELT, 1)[:, :128]

    def choose_blocks():
        e0, e1 = table()
        picks = jnp.where(iota((8, 128), 1) == iota((8, 128), 0) + SCORER, 1.0, 0.0).astype(BF)
        rows_ref[...] = dot_nt(picks, e1)
        ew = jnp.concatenate([dot_tn(e0, e1), dot_tn(e1, e1)[: VOC - 256]], axis=0)[:, SCORER : SCORER + 1]
        ratings = [jnp.sum(cb[b].astype(F32) * ew, axis=0, keepdims=True) / (b + 1) for b in range(BLOCKS)]
        top = functools.reduce(jnp.maximum, ratings)
        raised = [jnp.exp(r - top) for r in ratings]
        total = sum(raised)
        chosen = [r / total for r in raised]
        mixw = 0.0
        for b in range(BLOCKS):
            prow[b : b + 1, :] = chosen[b]
            mixw = mixw + cb[b].astype(F32) * (chosen[b] / (2.0 * (b + 1)))
        gt = mixw[:, :tokens] + mixw[:, tokens:]
        gt = jnp.concatenate([gt, jnp.zeros((384 - VOC, tokens), F32)], axis=0).T
        gthi[...] = gt.astype(BF)
        gtlo[...] = (gt - gt.astype(BF).astype(F32)).astype(BF)

    def make_hidden():
        e0, e1 = table()
        latent = (
            dot_nt(gthi[:, :256], e0) + dot_nt(gthi[:, 256:], e1)
            + dot_nt(gtlo[:, :256], e0) + dot_nt(gtlo[:, 256:], e1)
        )
        hid[...] = latent.astype(BF)

        hidden = hid[...].astype(F32)
        r1 = lax.rsqrt(jnp.mean(hidden * hidden, -1, keepdims=True) + EPSILON)
        normed = hidden * r1 * rows_ref[1:2, :]
        nrm[...] = normed.astype(BF)
        nrmt[...] = normed.T.astype(BF)

    def project(m, ref):
        for h in (0, 1):
            out = dot(nrm[...], wmat(m, h)).astype(BF)
            for i in range(half // 128):
                ref[h * (half // 128) + i] = out[:, i * 128 : (i + 1) * 128]

    tcol = iota((1, tokens), 1)
    valid_key = DOWN * tcol < length
    lane = iota((1, 128), 1)
    masks = [jnp.where(lane < 64, 1.0 - e, float(e)).astype(BF) for e in (0, 1)]

    def forward_pair(i, carry):
        q2, k2, v2 = qs[i], ks[i], vs[i]
        out = 0.0
        for e in (0, 1):
            h = 2 * i + e
            line = jnp.broadcast_to(bvec[h], (tokens, span))
            bias = pltpu.roll(line, tokens + 1, 1, stride=1, stride_axis=0)[:, :tokens]
            scores = jnp.where(valid_key, dot_nt(q2, k2 * masks[e]) + bias, NEGATIVE)
            up = jnp.exp(scores - jnp.max(scores, -1, keepdims=True))
            prob = up * (1.0 / jnp.sum(up, -1, keepdims=True))
            pmat[h] = prob
            out = out + dot(prob.astype(BF), v2 * masks[e])
        mixed[:, pl.ds(pl.multiple_of(i * 128, 128), 128)] = out.astype(BF)
        return carry

    def forward_pairs(k):
        lax.fori_loop(2 * k, 2 * k + 2, forward_pair, 0)

    def make_middle():
        mixp[...] = dot(mixed[...], pi[...]).astype(BF)
        for h in (0, 1):
            cols = slice(h * half, (h + 1) * half)
            mid[:, cols] = hid[:, cols].astype(F32) + dot(mixp[...], wmat(WO, h))
        middle = mid[...]
        r2 = lax.rsqrt(jnp.mean(middle * middle, -1, keepdims=True) + EPSILON)
        second = middle * r2 * rows_ref[2:3, :]
        sec_ref[...] = second.astype(BF)
        sect[...] = second.T.astype(BF)
        acc[...] = jnp.zeros_like(acc)
        encb[...] = mid[...]

    def feed(c):
        def one(h, carry):
            wgu = w[GU0 + c][h].reshape(width, 2 * quarter)
            wdn = [
                jnp.concatenate([w[m][j, h, c] for m in DN], axis=1).reshape(quarter, half) for j in (0, 1)
            ]
            both = dot(sec_ref[...], wgu)
            gate, upper = both[:, :quarter], both[:, quarter:]
            pdelta = dot_nt(cp[:, :half], wdn[0]) + dot_nt(cp[:, half:], wdn[1])
            square = gate * gate
            tanh = jnp.tanh(0.7978845608 * (gate + 0.044715 * square * gate))
            act = 0.5 * gate * (1.0 + tanh)
            slope = 0.5 * (1.0 + tanh) + 0.5 * gate * (1.0 - tanh * tanh) * 0.7978845608 * (1.0 + 0.134145 * square)
            product = (act * upper).astype(BF)
            delta = jnp.concatenate([(pdelta * upper * slope).astype(BF), (pdelta * act).astype(BF)], axis=1)
            gput(GU0 + c, h, dot(sect[...], delta))
            for j in (0, 1):
                out = slice(j * half, (j + 1) * half)
                grad = dot_tn(product, cp[:, out]).astype(BF).reshape(4, -1, half)
                few = grad.shape[1] // 2
                g[DNA][j, h, c], g[DNB][j, h, c] = grad[:, :few], grad[:, few:]
                encb[:, out] += dot(product, wdn[j])
            acc[...] += dot_nt(delta, wgu)
            return carry

        lax.fori_loop(0, 2, one, 0)

    def middle_back():
        middle = mid[...]
        r2 = lax.rsqrt(jnp.mean(middle * middle, -1, keepdims=True) + EPSILON)
        n2 = middle * r2
        sdelta = acc[...]
        scaled = sdelta * rows_ref[2:3, :]
        rows_ref[4:5, :] = jnp.sum(sdelta * n2, axis=0, keepdims=True)
        mdel[...] = cp[...].astype(F32) + r2 * (scaled - n2 * jnp.mean(scaled * n2, -1, keepdims=True))
        sec_ref[...] = mdel[...].astype(BF)
        for h in (0, 1):
            gput(WO, h, dot_tn(mixp[...], sec_ref[:, h * half : (h + 1) * half]))

    def mixed_back():
        back = dot_nt(sec_ref[:, :half], wmat(WO, 0)) + dot_nt(sec_ref[:, half:], wmat(WO, 1))
        mixp[...] = dot_nt(back.astype(BF), pi[...]).astype(BF)
        mid[...] = jnp.zeros_like(mid)

    flip = jnp.where(iota((tokens, tokens), 0) + iota((tokens, tokens), 1) == tokens - 1, 1.0, 0.0).astype(BF)

    def backward_pair(i, carry):
        cols = pl.ds(pl.multiple_of(i * 128, 128), 128)
        q2, k2, v2, m2 = qs[i], ks[i], vs[i], mixp[:, cols]
        outq = outk = outv = 0.0
        for e in (0, 1):
            h = 2 * i + e
            prob = pmat[h]
            wdelta = dot_nt(m2, v2 * masks[e])
            lean = jnp.sum(prob * wdelta, -1, keepdims=True)
            sd = jnp.where(valid_key, prob * (wdelta - lean), 0.0).astype(BF)
            outq = outq + dot(sd, k2 * masks[e])
            outk = outk + dot_tn(sd, q2 * masks[e])
            outv = outv + dot_tn(prob.astype(BF), m2 * masks[e])
            reverse = jnp.concatenate([dot(sd, flip), jnp.zeros((tokens, tokens), F32)], axis=1)
            skew = pltpu.roll(reverse, 0, 1, stride=1, stride_axis=0)
            dvec[h] = jnp.sum(skew, axis=0, keepdims=True)
        dq[:, cols], dk[:, cols], dv[:, cols] = outq.astype(BF), outk.astype(BF), outv.astype(BF)
        return carry

    def backward_pairs(k):
        lax.fori_loop(2 * k, 2 * k + 2, backward_pair, 0)

    def relative_back():
        ohr = jnp.where(iota((128, span), 0) == bucket_ids((tokens - 1) - iota((128, span), 1)), 1.0, 0.0).astype(BF)
        lines = jnp.concatenate([dvec[h] for h in range(heads)] + [jnp.zeros((16 - heads, span), F32)], axis=0)
        relbuf[0] = sum(dot_nt(part, ohr) for part in split3(lines))
        rel_step(0)

    levels = (
        ((0, net.sib),), ((1, net.xn),), ((2, net.yn),), ((3, net.zn[0]), (4, net.zn[1]), (5, net.zn[2])),
    )

    def rel_copy(slot, level, device):
        return net.copy(relbuf.at[level], relin.at[slot], net.mi_s.at[1 + slot], net.mi_r.at[1 + slot], device)

    def rel_step(level):
        if level:
            for slot, device in levels[level - 1]:
                rel_copy(slot, level - 1, device).wait_recv()
        if level in (1, 2, 3):
            relbuf[level] = relbuf[level - 1] + relin[level - 1]
        if level < 4:
            for slot, device in levels[level]:
                net.start(rel_copy(slot, level, device))
            return
        place = [jnp.where(net.z == k, 1.0, 0.0) for k in range(4)]
        level = [relbuf[3], relin[3], relin[4], relin[5]]
        summed = 0.0
        for k in range(4):
            summed = summed + sum(place[z] * level[(z - k) % 4] for z in range(4))
        g_rel[...] = summed

    def weight_back(k):
        m, ref = ((WQ, dq), (WK, dk), (WV, dv))[k]
        for h in (0, 1):
            part = ref[:, h * half : (h + 1) * half]
            gput(m, h, dot(nrmt[...], part))
            mid[...] += dot_nt(part, wmat(m, h))

    def hidden_back():
        hidden = hid[...].astype(F32)
        norm_delta = mid[...]
        r1 = lax.rsqrt(jnp.mean(hidden * hidden, -1, keepdims=True) + EPSILON)
        n1 = hidden * r1
        scaled = norm_delta * rows_ref[1:2, :]
        rows_ref[3:4, :] = jnp.sum(norm_delta * n1, axis=0, keepdims=True)
        delta = mdel[...] + r1 * (scaled - n1 * jnp.mean(scaled * n1, -1, keepdims=True))
        sec_ref[...] = delta.astype(BF)

    def choice_back():
        e0, e1 = table()
        hdel = sec_ref[...]
        back = jnp.concatenate([dot(hdel, e0), dot(hdel, e1)], axis=1).T[:VOC]
        back = jnp.concatenate([back, back], axis=1)
        pdel = [jnp.sum(cb[b].astype(F32) * back, axis=0, keepdims=True) / (2.0 * (b + 1)) for b in range(BLOCKS)]
        lean = sum(prow[b : b + 1, :] * pdel[b] for b in range(BLOCKS))
        flow = 0.0
        for b in range(BLOCKS):
            flow = flow + cb[b].astype(F32) * (prow[b : b + 1, :] * (pdel[b] - lean) / (b + 1))
        gs = jnp.sum(flow, axis=1, keepdims=True)
        lane_v = iota((VOC, 128), 1)
        parts = [p.astype(F32) for p in split3(gs)]
        gs3 = jnp.where(lane_v == 0, parts[0], jnp.where(lane_v == 1, parts[1], jnp.where(lane_v == 2, parts[2], 0.0)))
        gs3 = gs3.astype(BF)
        keep[0] = gs3

    def table_back():
        e0, e1 = table()
        hdel, gs3 = sec_ref[...], keep[0]
        lane_w = iota((width, 128), 1)
        wcol = jnp.where(lane_w < 3, e1.astype(F32)[:, SCORER : SCORER + 1], 0.0).astype(BF)
        gput(ELT, 0, dot_tn(hdel, gthi[:, :256]) + dot_tn(hdel, gtlo[:, :256]) + dot_nt(wcol, gs3[:256]))
        gs_tail = jnp.concatenate([gs3[256:], jnp.zeros((128 + 256 - VOC, 128), BF)], axis=0)
        tail = dot_tn(hdel, gthi[:, 256:]) + dot_tn(hdel, gtlo[:, 256:]) + dot_nt(wcol, gs_tail)
        scorer_grad = jnp.sum(dot(e0, gs3[:256]) + dot(e1, gs_tail), axis=1, keepdims=True)
        gains = [p.astype(F32) for p in (*split3(rows_ref[3:4, :]), *split3(rows_ref[4:5, :]))]
        gains = jnp.concatenate([*gains, jnp.zeros((10, width), F32)], axis=0).astype(BF)
        place_row, place_col = iota((16, 128), 0), iota((16, 128), 1)
        place = (place_row < 6) & (place_col == jnp.where(place_row < 3, SCORER + 1, SCORER + 2))
        tail = tail + dot_tn(gains, jnp.where(place, 1.0, 0.0).astype(BF))
        tail = jnp.where(lane_w == SCORER, scorer_grad, tail)
        gput(ELT, 1, jnp.concatenate([tail, jnp.zeros((width, 128), F32)], axis=1))


    enc_copy = net.copy(
        mixed.at[:, pl.ds(pl.multiple_of((1 - s) * half, 128), half)], enc_out.at[s],
        net.mi_s.at[0], net.mi_r.at[0], net.sib,
    )

    def send_encoded():
        encoded = dot_nt(encb[...].astype(BF), pi[...]).astype(BF)
        for h in (0, 1):
            mixed[:, h * half : (h + 1) * half] = encoded[:, h * half : (h + 1) * half]
        enc_out[s] = lanes(mixed, s, half)
        net.start(enc_copy)

    def last(m):
        mine, other = net.rs5(m)
        if m == WO or m in DN:
            first = jnp.where(s == 0, mine, other)
            second = jnp.where(s == 0, other, mine)
            both = jnp.concatenate([first, second], axis=1)
            value = sum(dot_nt(part, pi[...]) for part in split3(both))
            if m == WO:
                g_o[...] = value
            else:
                rows = value.shape[0]
                g_d[(m - DNA) * rows : (m - DNA + 1) * rows, :] = value
            return
        for h, value in ((s, mine), (1 - s, other)):
            if m in GU:
                cols = pl.ds(pl.multiple_of(h * ffh + (m - GU0) * quarter, 128), quarter)
                g_0[:, cols] = value[:, :quarter]
                g_1[:, cols] = value[:, quarter:]
            else:
                n = value.shape[1]
                target = {ELT: g_elt, WQ: g_q, WK: g_k, WV: g_v}[m]
                target[:, pl.ds(pl.multiple_of(h * n, 128), n)] = value

    pieces = (
        turn_cotangent, bias_lines, count_blocks, choose_blocks, make_hidden,
        *(functools.partial(project, *item) for item in ((WQ, qs), (WK, ks), (WV, vs))),
        *(functools.partial(forward_pairs, k) for k in range(pairs // 2)),
        make_middle,
        *(functools.partial(feed, c) for c in range(4)),
        middle_back, mixed_back,
        *(functools.partial(backward_pairs, k) for k in range(pairs // 2)),
        relative_back,
        *(functools.partial(weight_back, k) for k in range(3)),
        hidden_back, choice_back, table_back, send_encoded,
    )
    steps = {
        "A": net.ag1, "Z": net.ag2, "X": net.ag3, "D": net.ag4, "S": net.ag5,
        "a": net.rs0, "b": net.rs1, "c": net.rs2, "d": net.rs3, "e": net.rs4, "f": last,
        "p": lambda k: pieces[k](), "r": rel_step,
    }
    for kind, index in SCHEDULE:
        steps[kind](index)
    enc_copy.wait_recv()
    net.finish()


VMEM = pl.BlockSpec(memory_space=pltpu.VMEM)


def call(inner, *args):
    wq, wi0, wd, cot = args[9], args[13], args[15], args[16]
    rows_d, width = wq.shape
    rows_f = wd.shape[0] // 2
    half, ffh = width // 2, wi0.shape[1] // 2
    tokens = cot.shape[1]
    span = 2 * tokens
    heads, buckets = args[8].shape
    wide = {m: 256 if m == ELT else ffh // 2 if m in GU else half for m in ALL}
    chip = {m: (2, rows_f) if m in DN else (2 * rows_d,) for m in ALL}
    mine = {m: rows_f if m in DN else rows_d for m in ALL}

    def full(m):
        return (2, 4, 4, rows_f, wide[m]) if m in DN else (4, 4, 2 * rows_d, wide[m])

    def part(m):
        return (2, 2, rows_f, wide[m]) if m in DN else (2, 2 * rows_d, wide[m])

    scratch = []
    scratch += [pltpu.VMEM((2, *full(m)), BF) for m in ALL]
    scratch += [pltpu.VMEM((2, *full(m)), BF) for m in ALL]
    scratch += [pltpu.VMEM(full(m), BF) for m in ALL]
    scratch += [
        pltpu.VMEM((3, *part(m)[1:]) if m in PLANE_REDUCE else part(m), BF) for m in ALL
    ]
    scratch += [pltpu.VMEM((16, 128) if m in PLANE_REDUCE else part(m), BF) for m in ALL]
    scratch += [
        pltpu.VMEM((3, *((4,) if m in PLANE_REDUCE else ()), *chip[m], wide[m]), BF) for m in ALL
    ]
    scratch += [pltpu.VMEM((*chip[m], wide[m]), F32) for m in ALL]
    scratch += [pltpu.VMEM((mine[m], wide[m]), F32) for m in ALL]
    scratch += [pltpu.VMEM((mine[m], wide[m]), F32) for m in ALL]
    dma = pltpu.SemaphoreType.DMA
    scratch += [dma((N, 12)), dma((N, 12)), dma((N, 9)), dma((N, 9)), dma((7,)), dma((7,))]
    act = (tokens, width)
    scratch += [
        pltpu.VMEM((width, width), BF),
        pltpu.VMEM((BLOCKS, VOC, span), BF),
        pltpu.VMEM((8, span), F32),
        pltpu.VMEM((tokens, 384), BF),
        pltpu.VMEM((tokens, 384), BF),
        pltpu.VMEM((8, width), F32),
        pltpu.VMEM(act, BF),
        pltpu.VMEM(act, BF),
        pltpu.VMEM((width, tokens), BF),
        pltpu.VMEM((width // 128, tokens, 128), BF),
        pltpu.VMEM((width // 128, tokens, 128), BF),
        pltpu.VMEM((width // 128, tokens, 128), BF),
        pltpu.VMEM((heads, 1, span), F32),
        pltpu.VMEM((heads, tokens, tokens), F32),
        pltpu.VMEM(act, BF),
        pltpu.VMEM(act, BF),
        pltpu.VMEM(act, F32),
        pltpu.VMEM(act, BF),
        pltpu.VMEM((width, tokens), BF),
        pltpu.VMEM(act, F32),
        pltpu.VMEM(act, F32),
        pltpu.VMEM(act, BF),
        pltpu.VMEM(act, BF),
        pltpu.VMEM(act, BF),
        pltpu.VMEM((heads, 1, span), F32),
        pltpu.VMEM((4, 16, 128), F32),
        pltpu.VMEM((6, 16, 128), F32),
        pltpu.VMEM(act, BF),
    ]
    outs = [
        jax.ShapeDtypeStruct((MICRO, tokens, half), BF),
        jax.ShapeDtypeStruct((rows_d, 512), F32),
        *[jax.ShapeDtypeStruct(item.shape, F32) for item in args[9:16]],
        jax.ShapeDtypeStruct((16, 128), F32),
    ]
    return pl.pallas_call(
        functools.partial(kernel, inner, (tokens, width, half, ffh)),
        out_shape=outs,
        in_specs=[VMEM] * len(args),
        out_specs=[VMEM] * len(outs),
        scratch_shapes=scratch,
        compiler_params=pltpu.CompilerParams(
            collective_id=0, has_side_effects=True, vmem_limit_bytes=63 * 2**20
        ),
    )(*args)


def settle(vocab, langs, heads, buckets, *refs):
    ins, outs = refs[:10], refs[10:]
    outs[0][:, 0] = ins[0][...]
    rows = ins[1].shape[0]
    outs[1][...] = ins[1][:, :vocab]
    table = ins[1][:, 256:]
    table = jnp.concatenate([table, jnp.zeros((128 - rows, 256), F32)], axis=0).T[:, :rows]
    at = vocab - 256
    outs[2][...] = table[at : at + langs]
    at = at + langs
    for k, i in enumerate((3, 4, 9)):
        outs[i][...] = table[at + k : at + k + 1]
    for i, k in zip((5, 6, 7, 8, 10, 11, 12), range(2, 9)):
        outs[i][...] = ins[k][...]
    outs[13][...] = ins[9][:heads, :buckets]


def body(
    byte_ids, lengths, groups, embedding, language, scorer, prenorm, query_weight, key_weight, value_weight,
    output_weight, midnorm, gate_weight, up_weight, down_weight, relative, cotangent,
):
    inner = lax.axis_size("dp") // OUTER
    vocab, langs = embedding.shape[0], language.shape[0]
    tables = [embedding.T, language, scorer[None], prenorm[None], midnorm[None]]
    weights = [query_weight, key_weight, value_weight, output_weight, gate_weight, up_weight, down_weight]
    teams = [[o * inner + i for i in range(inner)] for o in range(OUTER)]
    if inner > 1:
        tables = [
            lax.all_gather(item, "dp", axis_index_groups=teams, axis=min(i, 1), tiled=True)
            for i, item in enumerate(tables)
        ]
        weights = [lax.all_gather(item, "dp", axis_index_groups=teams, axis=0, tiled=True) for item in weights]
    results = call(inner, byte_ids, lengths.T, groups.T, *tables, relative.T, *weights, cotangent[:, 0])
    if inner > 1:
        grads = [
            lax.psum_scatter(item, "dp", axis_index_groups=teams, scatter_dimension=0, tiled=True)
            for item in results[1:9]
        ]
        results = [results[0], *grads, lax.psum(results[9], "dp", axis_index_groups=teams)]
    buckets, heads = relative.shape
    rows = results[1].shape[0]
    line = jax.ShapeDtypeStruct((1, rows), F32)
    like = [jax.ShapeDtypeStruct(item.shape, F32) for item in results[2:9]]
    shapes = [
        jax.ShapeDtypeStruct(cotangent.shape[:3] + (results[0].shape[2],), BF),
        jax.ShapeDtypeStruct((rows, vocab), F32),
        jax.ShapeDtypeStruct((langs, rows), F32),
        line, line, *like[:4], line, *like[4:],
        jax.ShapeDtypeStruct((heads, buckets), F32),
    ]
    outs = pl.pallas_call(
        functools.partial(settle, vocab, langs, heads, buckets),
        out_shape=shapes,
        in_specs=[VMEM] * 10,
        out_specs=[VMEM] * 14,
        compiler_params=pltpu.CompilerParams(vmem_limit_bytes=60 * 2**20),
    )(*results)
    return tuple(item[0] if i in (3, 4, 9) else item.T if i in (1, 13) else item for i, item in enumerate(outs))


def solution(mesh):
    both = ("section", "dp")
    wide = P(both, None)
    return jax.shard_map(
        body,
        mesh=mesh,
        in_specs=(
            P(None, "dp", None), P(None, "dp"), P(None, "dp"), P(None, both), P(None, both), P(both), P(both),
            wide, wide, wide, wide, P(both), wide, wide, wide, P(), P(None, "dp", None, None),
        ),
        out_specs=(
            P(None, "dp", None, "section"), P(None, both), P(None, both), P(both), P(both),
            wide, wide, wide, wide, P(both), wide, wide, wide, P(),
        ),
        check_vma=False,
    )
```

```python
import functools

import jax
import jax.numpy as jnp
from jax import lax
from jax.experimental import pallas as pl
from jax.experimental.pallas import tpu as pltpu
from jax.sharding import PartitionSpec as P

BLOCKS = 4
DOWN = 2
MICRO = 2
OUTER = 16
EPSILON = 1e-06
NEGATIVE = -1000000000.0
LIMITS = (12, 16, 23, 32, 46, 64, 91)
MESH = pl.DeviceIdType.MESH
BF = jnp.bfloat16
F32 = jnp.float32
I32 = jnp.int32

ELT, WQ, WK, WV, WO, DNA, DNB, GU0, GU1, GU2, GU3 = range(11)
DN = (DNA, DNB)
GU = (GU0, GU1, GU2, GU3)
ALL = tuple(range(11))
N = len(ALL)
PLANE_GATHER = (10,)
PLANE_REDUCE = ()
SCHEDULE = (
    ("A", 10), ("Z", 0), ("A", 2), ("p", 0), ("Z", 1), ("A", 3), ("X", 0), ("Z", 2), ("A", 4), ("X", 1), ("D", 0),
    ("S", 0), ("p", 3), ("Z", 3), ("A", 5), ("X", 2), ("D", 1), ("p", 4), ("S", 1), ("p", 5), ("Z", 4), ("A", 6),
    ("X", 3), ("D", 2), ("S", 2), ("p", 6), ("Z", 5), ("A", 7), ("X", 4), ("D", 3), ("S", 3), ("p", 7), ("p", 8),
    ("Z", 6), ("A", 8), ("X", 5), ("D", 4), ("p", 9), ("S", 4), ("p", 10), ("Z", 7), ("A", 9), ("X", 6), ("D", 5),
    ("p", 11), ("S", 5), ("Z", 8), ("X", 7), ("D", 6), ("S", 6), ("Z", 9), ("Z", 10), ("X", 8), ("D", 7), ("S", 7),
    ("p", 12), ("a", 7), ("X", 9), ("b", 7), ("D", 8), ("S", 8), ("p", 13), ("a", 8), ("D", 9), ("b", 8), ("S", 9),
    ("c", 7), ("p", 14), ("a", 9), ("b", 9), ("c", 8), ("d", 7), ("X", 10), ("S", 10), ("p", 15), ("a", 10), ("a", 5),
    ("a", 6), ("c", 9), ("b", 10), ("d", 8), ("e", 7), ("p", 16), ("b", 5), ("a", 4), ("c", 10), ("b", 6), ("d", 9),
    ("e", 8), ("p", 17), ("p", 18), ("p", 19), ("c", 5), ("d", 10), ("e", 9), ("f", 7), ("p", 20), ("p", 21),
    ("p", 22), ("a", 1), ("c", 6), ("b", 4), ("d", 5), ("e", 10), ("p", 23), ("a", 2), ("p", 24), ("a", 3), ("b", 1),
    ("c", 4), ("d", 6), ("e", 5), ("f", 8), ("p", 25), ("r", 1), ("p", 26), ("b", 2), ("c", 1), ("d", 4), ("e", 6),
    ("p", 27), ("a", 0), ("r", 2), ("b", 3), ("c", 2), ("d", 1), ("e", 4), ("f", 9), ("f", 10), ("p", 28), ("r", 3),
    ("b", 0), ("c", 3), ("d", 2), ("e", 1), ("f", 5), ("f", 6), ("r", 4), ("c", 0), ("d", 3), ("e", 2), ("f", 1),
    ("f", 4), ("d", 0), ("e", 3), ("f", 2), ("e", 0), ("f", 3), ("f", 0),
)
VOC = 288
SCORER = 19


def dot(a, b):
    return lax.dot_general(a, b, (((1,), (0,)), ((), ())), preferred_element_type=F32)


def dot_nt(a, b):
    return lax.dot_general(a, b, (((1,), (1,)), ((), ())), preferred_element_type=F32)


def dot_tn(a, b):
    return lax.dot_general(a, b, (((0,), (0,)), ((), ())), preferred_element_type=F32)


def split3(x):
    hi = x.astype(BF)
    rest = x - hi.astype(F32)
    mid = rest.astype(BF)
    return hi, mid, (rest - mid.astype(F32)).astype(BF)


def iota(shape, axis):
    return lax.broadcasted_iota(I32, shape, axis)


def over(value, n):
    return (value * (65536 // n + 1)) >> 16


def bucket_ids(offsets):
    distance = jnp.abs(offsets)
    larger = 8 + sum(((distance >= limit).astype(I32) for limit in LIMITS))
    inside = jnp.where(distance < 8, distance, larger)
    return jnp.where(offsets > 0, 16, 0).astype(I32) + inside


class Net:
    def __init__(self, inner, w, g, sb, x1, y1, zi, ch, tmp, fo, sems):
        self.w, self.g, self.sb, self.x1, self.y1 = w, g, sb, x1, y1
        self.zi, self.ch, self.tmp, self.fo = zi, ch, tmp, fo
        self.ag_s, self.ag_r, self.rs_s, self.rs_r, self.mi_s, self.mi_r = sems
        self.s = lax.axis_index("section")
        self.d = lax.axis_index("dp")
        outer = self.d // inner
        self.z = outer // 4
        self.yx = outer % 4
        y, x = self.yx // 2, self.yx % 2
        self.sib = (1 - self.s, self.d)
        self.yx_x = self.yx + 1 - 2 * x
        self.yx_y = self.yx + 2 - 4 * y
        self.yx_d = 3 - self.yx
        self.xn = (self.s, self.d + (1 - 2 * x) * inner)
        self.yn = (self.s, self.d + (1 - 2 * y) * 2 * inner)
        self.dn = (self.s, self.d + (1 - 2 * x) * inner + (1 - 2 * y) * 2 * inner)
        self.zz = [(self.z + k) % 4 for k in (1, 2, 3)]
        self.zn = [(self.s, self.d + (zz - self.z) * 4 * inner) for zz in self.zz]
        self.sent = []

    def greet(self):
        barrier = pltpu.get_barrier_semaphore()
        for device in (self.sib, self.xn, self.yn, self.dn, *self.zn):
            pl.semaphore_signal(barrier, inc=1, device_id=device, device_id_type=MESH)

    def meet(self):
        pl.semaphore_wait(pltpu.get_barrier_semaphore(), 7)

    def copy(self, src, dst, send, recv, device):
        return pltpu.make_async_remote_copy(
            src_ref=src, dst_ref=dst, send_sem=send, recv_sem=recv,
            device_id=device, device_id_type=MESH,
        )

    def start(self, copy):
        copy.start()
        self.sent.append(copy)

    def finish(self):
        for copy in self.sent:
            copy.wait_send()
        self.sent = []

    def blk(self, ref, m, h, z, yx):
        return ref.at[h, :, z, yx] if m in DN else ref.at[h, z, yx]

    def grp(self, ref, m, h, yx):
        return ref.at[h, :, :, yx] if m in DN else ref.at[h, :, yx]

    def part(self, ref, m, h, z0, yx):
        return ref.at[h, :, pl.ds(z0, 2), yx] if m in DN else ref.at[h, pl.ds(z0, 2), yx]

    def plane(self, ref, m, h, z):
        return ref.at[h, :, z] if m in DN else ref.at[h, z]

    def xy2(self, m):
        if m in DN:
            return self.sb[m].at[0, pl.ds(0, 2)], self.sb[m].at[0, pl.ds(2, 2)]
        return self.sb[m].at[0], self.sb[m].at[1]

    def ag(self, m, slot):
        w, s = self.w[m], self.s
        pair = lambda src, dst, dev: self.copy(src, dst, self.ag_s.at[m, slot], self.ag_r.at[m, slot], dev)
        if slot == 0:
            if m in DN:
                dst = self.ch[m].at[s]
            else:
                rows = self.tmp[m].shape[0]
                dst = self.ch[m].at[pl.ds(s * rows, rows)]
            return pair(self.tmp[m], dst, self.sib)
        if m in PLANE_GATHER:
            if slot <= 3:
                ref = self.blk(w, m, s, self.z, self.yx)
                return pair(ref, ref, (self.xn, self.yn, self.dn)[slot - 1])
            ref = self.plane(w, m, s, (self.z, *self.zz)[(0, 0, 0, 0, 3, 2, 1)[slot - 4]] if slot > 7 else self.z)
            return pair(ref, ref, self.sib if slot >= 7 else self.zn[slot - 4])
        if slot <= 3:
            ref = self.blk(w, m, s, self.z, self.yx)
            return pair(ref, ref, self.zn[slot - 1])
        if slot <= 5:
            ref = self.grp(w, m, s, self.yx)
            return pair(ref, ref, self.xn if slot == 4 else self.yn)
        if slot == 6:
            ref = self.part(w, m, s, 0, self.yx_x)
            return pair(ref, ref, self.yn)
        if slot == 7:
            ref = self.part(w, m, s, 2, self.yx_y)
            return pair(ref, ref, self.xn)
        ref = self.grp(w, m, s, (self.yx, self.yx_x, self.yx_y, self.yx_d)[slot - 8])
        return pair(ref, ref, self.sib)

    def ag0(self, m):
        self.start(self.ag(m, 0))

    def own(self, m):
        self.ag(m, 0).wait_recv()
        chunk = self.ch[m][...].astype(BF)
        if m in DN:
            for sec in (0, 1):
                self.w[m][self.s, sec, self.z, self.yx] = chunk[sec]
        else:
            self.w[m][self.s, self.z, self.yx] = chunk

    def ag1(self, m):
        for slot in (1, 2, 3):
            self.start(self.ag(m, slot))

    def ag2(self, m):
        for slot in (1, 2, 3):
            self.ag(m, slot).wait_recv()
        for slot in (4, 5, 6, 7) if m in PLANE_GATHER else (4, 5, 8):
            self.start(self.ag(m, slot))

    def ag3(self, m):
        chain = ((4, (8,)), (5, (9,)), (6, (10,))) if m in PLANE_GATHER else ((4, (6, 9)), (5, (7, 10)))
        for slot, onward in chain:
            self.ag(m, slot).wait_recv()
            for then in onward:
                self.start(self.ag(m, then))

    def ag4(self, m):
        if m in PLANE_GATHER:
            return
        for slot in (6, 7):
            self.ag(m, slot).wait_recv()
        self.start(self.ag(m, 11))

    def ag5(self, m):
        for slot in (7, 8, 9, 10) if m in PLANE_GATHER else (8, 9, 10, 11):
            self.ag(m, slot).wait_recv()

    def rs(self, m, slot):
        g, s = self.g[m], self.s
        pair = lambda src, dst, dev: self.copy(src, dst, self.rs_s.at[m, slot], self.rs_r.at[m, slot], dev)
        if slot == 0:
            return pair(g.at[1 - s], self.sb[m], self.sib)
        if m in PLANE_REDUCE and slot <= 6:
            if slot <= 3:
                return pair(self.plane(g, m, s, self.zz[slot - 1]), self.zi[m].at[slot - 1], self.zn[slot - 1])
            k = slot - 4
            ref = self.blk(g, m, s, self.z, (self.yx_x, self.yx_y, self.yx_d)[k])
            return pair(ref, self.x1[m].at[k], (self.xn, self.yn, self.dn)[k])
        if slot == 1:
            return pair(self.part(g, m, s, 0, self.yx_d), self.x1[m], self.xn)
        if slot == 2:
            return pair(self.part(g, m, s, 2, self.yx_d), self.y1[m], self.yn)
        if slot == 3:
            return pair(self.grp(g, m, s, self.yx_x), self.xy2(m)[0], self.xn)
        if slot == 4:
            return pair(self.grp(g, m, s, self.yx_y), self.xy2(m)[1], self.yn)
        if slot <= 7:
            k = slot - 5
            return pair(self.blk(g, m, s, self.zz[k], self.yx), self.zi[m].at[k], self.zn[k])
        if m in DN:
            src = self.ch[m].at[1 - s]
        else:
            rows = self.fo[m].shape[0]
            src = self.ch[m].at[pl.ds((1 - s) * rows, rows)]
        return pair(src, self.fo[m], self.sib)

    def rs0(self, m):
        self.start(self.rs(m, 0))

    def rs1(self, m):
        self.rs(m, 0).wait_recv()
        g, sb, s = self.g[m], self.sb[m], self.s

        def add(i, carry):
            if m in DN:
                at = (i // 4, i % 4)
                g[s, at[0], at[1]] = (g[s, at[0], at[1]].astype(F32) + sb[at[0], at[1]].astype(F32)).astype(BF)
            else:
                g[s, i // 4, i % 4] = (g[s, i // 4, i % 4].astype(F32) + sb[i // 4, i % 4].astype(F32)).astype(BF)
            return carry

        lax.fori_loop(0, 8 if m in DN else 16, add, 0)
        for slot in (1, 2, 3) if m in PLANE_REDUCE else (1, 2):
            self.start(self.rs(m, slot))

    def rs2(self, m):
        g, s = self.g[m], self.s
        if m in PLANE_REDUCE:
            for slot in (1, 2, 3):
                self.rs(m, slot).wait_recv()
            zi = self.zi[m]

            def whole(yx):
                parts = [zi[k, yx].astype(F32) for k in (0, 1, 2)]
                return g[s, self.z, yx].astype(F32) + (parts[0] + parts[1] + parts[2])

            for slot, yx in ((4, self.yx_x), (5, self.yx_y), (6, self.yx_d)):
                g[s, self.z, yx] = whole(yx).astype(BF)
                self.start(self.rs(m, slot))
            self.ch[m][...] = whole(self.yx)
            return
        for slot, ref, z0, yx in ((1, self.x1[m], 0, self.yx_y), (2, self.y1[m], 2, self.yx_x)):
            self.rs(m, slot).wait_recv()
            for j in (0, 1):
                if m in DN:
                    for sec in (0, 1):
                        mine = g[s, sec, z0 + j, yx].astype(F32)
                        g[s, sec, z0 + j, yx] = (mine + ref[sec, j].astype(F32)).astype(BF)
                else:
                    mine = g[s, z0 + j, yx].astype(F32)
                    g[s, z0 + j, yx] = (mine + ref[j].astype(F32)).astype(BF)
        self.start(self.rs(m, 3))
        self.start(self.rs(m, 4))

    def rs3(self, m):
        if m in PLANE_REDUCE:
            for slot in (4, 5, 6):
                self.rs(m, slot).wait_recv()
            x1 = self.x1[m]
            self.ch[m][...] += x1[0].astype(F32) + x1[1].astype(F32) + x1[2].astype(F32)
            self.start(self.rs(m, 8))
            return
        self.rs(m, 3).wait_recv()
        self.rs(m, 4).wait_recv()
        g, s, yx = self.g[m], self.s, self.yx
        a, b = self.xy2(m)

        def total(sec, z):
            if m in DN:
                return g[s, sec, z, yx].astype(F32) + a[sec, z].astype(F32) + b[sec, z].astype(F32)
            return g[s, z, yx].astype(F32) + a[z].astype(F32) + b[z].astype(F32)

        for slot in (5, 6, 7):
            zz = self.zz[slot - 5]
            if m in DN:
                for sec in (0, 1):
                    g[s, sec, zz, yx] = total(sec, zz).astype(BF)
            else:
                g[s, zz, yx] = total(0, zz).astype(BF)
            self.start(self.rs(m, slot))
        if m in DN:
            for sec in (0, 1):
                self.ch[m][sec] = total(sec, self.z)
        else:
            self.ch[m][...] = total(0, self.z)

    def rs4(self, m):
        if m in PLANE_REDUCE:
            return
        for slot in (5, 6, 7):
            self.rs(m, slot).wait_recv()
        zi = self.zi[m]
        self.ch[m][...] += zi[0].astype(F32) + zi[1].astype(F32) + zi[2].astype(F32)
        self.start(self.rs(m, 8))

    def rs5(self, m):
        if m in DN:
            mine = self.ch[m][self.s]
        else:
            rows = self.fo[m].shape[0]
            mine = self.ch[m][pl.ds(self.s * rows, rows)]
        self.rs(m, 8).wait_recv()
        return mine, self.fo[m][...]


def kernel(inner, sizes, *refs):
    (byte_ids, lengths, groups, emb, lang, scorer, prenorm, midnorm, rel) = refs[:9]
    given = refs[9:17]
    (enc_out, g_elt, g_q, g_k, g_v, g_o, g_0, g_1, g_d, g_rel) = refs[17:27]
    rest = refs[27:]
    take = lambda k: rest[N * k : N * k + N]
    w, g, sb, x1, y1, zi, ch, tmp, fo = (take(k) for k in range(9))
    rest = rest[9 * N :]
    sems, rest = rest[:6], rest[6:]
    (pi, cb, prow, gthi, gtlo, rows_ref, hid, nrm, nrmt, qs, ks, vs, bvec, pmat, mixed, mixp, mid, sec_ref, sect,
     acc, encb, dq, dk, dv, dvec, relbuf, relin, cp) = rest[:28]
    held, arrived = rest[28:36], rest[36]
    (wq, wk, wv, wo, wi0, wi1, wd, cot) = held
    tokens, width, half, ffh = sizes
    quarter = ffh // 4
    net = Net(inner, w, g, sb, x1, y1, zi, ch, tmp, fo, sems)
    s = net.s
    net.greet()
    fetches = [pltpu.make_async_copy(a, b, arrived.at[k]) for k, (a, b) in enumerate(zip(given, held))]
    for fetch in fetches:
        fetch.start()

    def lanes(ref, h, n):
        return ref[:, pl.ds(pl.multiple_of(h * n, 128), n)]

    def wmat(m, h):
        return w[m][h].reshape(width, w[m].shape[-1])

    def gput(m, h, value):
        g[m][h] = value.astype(BF).reshape(g[m].shape[1:])

    rows_d = wq.shape[0]
    vocab, langs = emb.shape[1], lang.shape[0]

    def turned(value, at):
        rows = value.shape[0]
        more = -rows % 8
        if more:
            value = jnp.concatenate([value, jnp.zeros((more, rows_d), F32)], axis=0)
        row = iota((rows + more, 512), 0)
        spot = (row + at == iota((rows + more, 512), 1)) & (row < rows)
        return dot_tn(value.astype(BF), jnp.where(spot, 1.0, 0.0).astype(BF))

    col = iota((1, width), 1)
    chip = over(col, 2 * rows_d)
    inside = col - chip * (2 * rows_d)
    natural = jnp.where(inside < rows_d, chip * rows_d + inside, half + (chip - 1) * rows_d + inside)
    pi[...] = jnp.where(iota((width, width), 0) == natural, 1.0, 0.0).astype(BF)
    vectors = jnp.concatenate([scorer[...], prenorm[...], midnorm[...]], axis=0)
    spread = jnp.where(iota((vocab, 512), 0) == iota((vocab, 512), 1), 1.0, 0.0).astype(BF)
    elt = dot(emb[...].astype(BF), spread) + turned(lang[...], vocab) + turned(vectors, 256 + SCORER)
    wide = {}

    def halves(m, h):
        if m == ELT:
            return jnp.where(h == 0, elt[:, :256], elt[:, 256:])
        if m in (WQ, WK, WV):
            return lanes({WQ: wq, WK: wk, WV: wv}[m], h, half)
        if m in GU:
            cols = pl.ds(pl.multiple_of(h * ffh + (m - GU0) * quarter, 128), quarter)
            return jnp.concatenate([wi0[:, cols], wi1[:, cols]], axis=1)
        value = wide[m]
        return jnp.where(h == 0, value[:, :half], value[:, half:])

    def exchange(m):
        tmp[m][...] = halves(m, 1 - s)
        net.ag0(m)
        mine = halves(m, s)
        if m in DN:
            ch[m][s] = mine
        else:
            ch[m][pl.ds(s * rows_d, rows_d)] = mine

    span = 2 * tokens
    heads, buckets = rel.shape
    pairs = width // 128
    keep = {}
    mdel = acc

    def turn_cotangent():
        cp[...] = dot(cot[s], pi[...]).astype(BF)


    def bias_lines():
        ohb = jnp.where(iota((buckets, span), 0) == bucket_ids(iota((buckets, span), 1) - (tokens - 1)), 1.0, 0.0)
        bv = sum(dot(part, ohb.astype(BF)) for part in split3(rel[...]))
        for h in range(heads):
            bvec[h] = bv[h : h + 1, :]

    length = jnp.where(s == 0, lengths[:, 0:1], lengths[:, 1:2])
    group = jnp.where(s == 0, groups[:, 0:1], groups[:, 1:2])

    def block_of(p, size):
        return p if size == 1 else p >> 1 if size == 2 else over(p, 3) if size == 3 else p >> 2

    def count_blocks():
        col = iota((1, span), 1)
        pos = jnp.where(col < tokens, 2 * col, 2 * (col - tokens) + 1)
        symbol = iota((VOC, span), 0)
        onehot = jnp.where(((symbol == byte_ids[s]) | (symbol == group + vocab)) & (col < length), 1.0, 0.0).astype(BF)
        rowi = iota((span, 1), 0)
        for size in range(1, BLOCKS + 1):
            pool = jnp.where(block_of(rowi, size) == block_of(pos, size), 1.0, 0.0).astype(BF)
            cb[size - 1] = dot(onehot, pool).astype(BF)

    def table():
        return wmat(ELT, 0), wmat(ELT, 1)[:, :128]

    def choose_blocks():
        e0, e1 = table()
        picks = jnp.where(iota((8, 128), 1) == iota((8, 128), 0) + SCORER, 1.0, 0.0).astype(BF)
        rows_ref[...] = dot_nt(picks, e1)
        ew = jnp.concatenate([dot_tn(e0, e1), dot_tn(e1, e1)[: VOC - 256]], axis=0)[:, SCORER : SCORER + 1]
        ratings = [jnp.sum(cb[b].astype(F32) * ew, axis=0, keepdims=True) / (b + 1) for b in range(BLOCKS)]
        top = functools.reduce(jnp.maximum, ratings)
        raised = [jnp.exp(r - top) for r in ratings]
        total = sum(raised)
        chosen = [r / total for r in raised]
        mixw = 0.0
        for b in range(BLOCKS):
            prow[b : b + 1, :] = chosen[b]
            mixw = mixw + cb[b].astype(F32) * (chosen[b] / (2.0 * (b + 1)))
        gt = mixw[:, :tokens] + mixw[:, tokens:]
        gt = jnp.concatenate([gt, jnp.zeros((384 - VOC, tokens), F32)], axis=0).T
        gthi[...] = gt.astype(BF)
        gtlo[...] = (gt - gt.astype(BF).astype(F32)).astype(BF)

    def make_hidden():
        e0, e1 = table()
        latent = (
            dot_nt(gthi[:, :256], e0) + dot_nt(gthi[:, 256:], e1)
            + dot_nt(gtlo[:, :256], e0) + dot_nt(gtlo[:, 256:], e1)
        )
        hid[...] = latent.astype(BF)

        hidden = hid[...].astype(F32)
        r1 = lax.rsqrt(jnp.mean(hidden * hidden, -1, keepdims=True) + EPSILON)
        normed = hidden * r1 * rows_ref[1:2, :]
        nrm[...] = normed.astype(BF)
        nrmt[...] = normed.T.astype(BF)

    def project(m, ref):
        for h in (0, 1):
            out = dot(nrm[...], wmat(m, h)).astype(BF)
            for i in range(half // 128):
                ref[h * (half // 128) + i] = out[:, i * 128 : (i + 1) * 128]

    tcol = iota((1, tokens), 1)
    valid_key = DOWN * tcol < length
    lane = iota((1, 128), 1)
    masks = [jnp.where(lane < 64, 1.0 - e, float(e)).astype(BF) for e in (0, 1)]

    def forward_pair(i, carry):
        q2, k2, v2 = qs[i], ks[i], vs[i]
        out = 0.0
        for e in (0, 1):
            h = 2 * i + e
            line = jnp.broadcast_to(bvec[h], (tokens, span))
            bias = pltpu.roll(line, tokens + 1, 1, stride=1, stride_axis=0)[:, :tokens]
            scores = jnp.where(valid_key, dot_nt(q2, k2 * masks[e]) + bias, NEGATIVE)
            up = jnp.exp(scores - jnp.max(scores, -1, keepdims=True))
            prob = up * (1.0 / jnp.sum(up, -1, keepdims=True))
            pmat[h] = prob
            out = out + dot(prob.astype(BF), v2 * masks[e])
        mixed[:, pl.ds(pl.multiple_of(i * 128, 128), 128)] = out.astype(BF)
        return carry

    def forward_pairs(k):
        lax.fori_loop(2 * k, 2 * k + 2, forward_pair, 0)

    def make_middle():
        mixp[...] = dot(mixed[...], pi[...]).astype(BF)
        for h in (0, 1):
            cols = slice(h * half, (h + 1) * half)
            mid[:, cols] = hid[:, cols].astype(F32) + dot(mixp[...], wmat(WO, h))
        middle = mid[...]
        r2 = lax.rsqrt(jnp.mean(middle * middle, -1, keepdims=True) + EPSILON)
        second = middle * r2 * rows_ref[2:3, :]
        sec_ref[...] = second.astype(BF)
        sect[...] = second.T.astype(BF)
        acc[...] = jnp.zeros_like(acc)
        encb[...] = mid[...]

    def feed(c):
        def one(h, carry):
            wgu = w[GU0 + c][h].reshape(width, 2 * quarter)
            wdn = [
                jnp.concatenate([w[m][j, h, c] for m in DN], axis=1).reshape(quarter, half) for j in (0, 1)
            ]
            both = dot(sec_ref[...], wgu)
            gate, upper = both[:, :quarter], both[:, quarter:]
            pdelta = dot_nt(cp[:, :half], wdn[0]) + dot_nt(cp[:, half:], wdn[1])
            square = gate * gate
            tanh = jnp.tanh(0.7978845608 * (gate + 0.044715 * square * gate))
            act = 0.5 * gate * (1.0 + tanh)
            slope = 0.5 * (1.0 + tanh) + 0.5 * gate * (1.0 - tanh * tanh) * 0.7978845608 * (1.0 + 0.134145 * square)
            product = (act * upper).astype(BF)
            delta = jnp.concatenate([(pdelta * upper * slope).astype(BF), (pdelta * act).astype(BF)], axis=1)
            gput(GU0 + c, h, dot(sect[...], delta))
            for j in (0, 1):
                out = slice(j * half, (j + 1) * half)
                grad = dot_tn(product, cp[:, out]).astype(BF).reshape(4, -1, half)
                few = grad.shape[1] // 2
                g[DNA][j, h, c], g[DNB][j, h, c] = grad[:, :few], grad[:, few:]
                encb[:, out] += dot(product, wdn[j])
            acc[...] += dot_nt(delta, wgu)
            return carry

        lax.fori_loop(0, 2, one, 0)

    def middle_back():
        middle = mid[...]
        r2 = lax.rsqrt(jnp.mean(middle * middle, -1, keepdims=True) + EPSILON)
        n2 = middle * r2
        sdelta = acc[...]
        scaled = sdelta * rows_ref[2:3, :]
        rows_ref[4:5, :] = jnp.sum(sdelta * n2, axis=0, keepdims=True)
        mdel[...] = cp[...].astype(F32) + r2 * (scaled - n2 * jnp.mean(scaled * n2, -1, keepdims=True))
        sec_ref[...] = mdel[...].astype(BF)
        for h in (0, 1):
            gput(WO, h, dot_tn(mixp[...], sec_ref[:, h * half : (h + 1) * half]))

    def mixed_back():
        back = dot_nt(sec_ref[:, :half], wmat(WO, 0)) + dot_nt(sec_ref[:, half:], wmat(WO, 1))
        mixp[...] = dot_nt(back.astype(BF), pi[...]).astype(BF)
        mid[...] = jnp.zeros_like(mid)

    flip = jnp.where(iota((tokens, tokens), 0) + iota((tokens, tokens), 1) == tokens - 1, 1.0, 0.0).astype(BF)

    def backward_pair(i, carry):
        cols = pl.ds(pl.multiple_of(i * 128, 128), 128)
        q2, k2, v2, m2 = qs[i], ks[i], vs[i], mixp[:, cols]
        outq = outk = outv = 0.0
        for e in (0, 1):
            h = 2 * i + e
            prob = pmat[h]
            wdelta = dot_nt(m2, v2 * masks[e])
            lean = jnp.sum(prob * wdelta, -1, keepdims=True)
            sd = jnp.where(valid_key, prob * (wdelta - lean), 0.0).astype(BF)
            outq = outq + dot(sd, k2 * masks[e])
            outk = outk + dot_tn(sd, q2 * masks[e])
            outv = outv + dot_tn(prob.astype(BF), m2 * masks[e])
            reverse = jnp.concatenate([dot(sd, flip), jnp.zeros((tokens, tokens), F32)], axis=1)
            skew = pltpu.roll(reverse, 0, 1, stride=1, stride_axis=0)
            dvec[h] = jnp.sum(skew, axis=0, keepdims=True)
        dq[:, cols], dk[:, cols], dv[:, cols] = outq.astype(BF), outk.astype(BF), outv.astype(BF)
        return carry

    def backward_pairs(k):
        lax.fori_loop(2 * k, 2 * k + 2, backward_pair, 0)

    def relative_back():
        ohr = jnp.where(iota((128, span), 0) == bucket_ids((tokens - 1) - iota((128, span), 1)), 1.0, 0.0).astype(BF)
        lines = jnp.concatenate([dvec[h] for h in range(heads)] + [jnp.zeros((16 - heads, span), F32)], axis=0)
        relbuf[0] = sum(dot_nt(part, ohr) for part in split3(lines))
        rel_step(0)

    levels = (
        ((0, net.sib),), ((1, net.xn),), ((2, net.yn),), ((3, net.zn[0]), (4, net.zn[1]), (5, net.zn[2])),
    )

    def rel_copy(slot, level, device):
        return net.copy(relbuf.at[level], relin.at[slot], net.mi_s.at[1 + slot], net.mi_r.at[1 + slot], device)

    def rel_step(level):
        if level:
            for slot, device in levels[level - 1]:
                rel_copy(slot, level - 1, device).wait_recv()
        if level in (1, 2, 3):
            relbuf[level] = relbuf[level - 1] + relin[level - 1]
        if level < 4:
            for slot, device in levels[level]:
                net.start(rel_copy(slot, level, device))
            return
        place = [jnp.where(net.z == k, 1.0, 0.0) for k in range(4)]
        level = [relbuf[3], relin[3], relin[4], relin[5]]
        summed = 0.0
        for k in range(4):
            summed = summed + sum(place[z] * level[(z - k) % 4] for z in range(4))
        g_rel[...] = summed

    def weight_back(k):
        m, ref = ((WQ, dq), (WK, dk), (WV, dv))[k]
        for h in (0, 1):
            part = ref[:, h * half : (h + 1) * half]
            gput(m, h, dot(nrmt[...], part))
            mid[...] += dot_nt(part, wmat(m, h))

    def hidden_back():
        hidden = hid[...].astype(F32)
        norm_delta = mid[...]
        r1 = lax.rsqrt(jnp.mean(hidden * hidden, -1, keepdims=True) + EPSILON)
        n1 = hidden * r1
        scaled = norm_delta * rows_ref[1:2, :]
        rows_ref[3:4, :] = jnp.sum(norm_delta * n1, axis=0, keepdims=True)
        delta = mdel[...] + r1 * (scaled - n1 * jnp.mean(scaled * n1, -1, keepdims=True))
        sec_ref[...] = delta.astype(BF)

    def choice_back():
        e0, e1 = table()
        hdel = sec_ref[...]
        back = jnp.concatenate([dot(hdel, e0), dot(hdel, e1)], axis=1).T[:VOC]
        back = jnp.concatenate([back, back], axis=1)
        pdel = [jnp.sum(cb[b].astype(F32) * back, axis=0, keepdims=True) / (2.0 * (b + 1)) for b in range(BLOCKS)]
        lean = sum(prow[b : b + 1, :] * pdel[b] for b in range(BLOCKS))
        flow = 0.0
        for b in range(BLOCKS):
            flow = flow + cb[b].astype(F32) * (prow[b : b + 1, :] * (pdel[b] - lean) / (b + 1))
        gs = jnp.sum(flow, axis=1, keepdims=True)
        lane_v = iota((VOC, 128), 1)
        parts = [p.astype(F32) for p in split3(gs)]
        gs3 = jnp.where(lane_v == 0, parts[0], jnp.where(lane_v == 1, parts[1], jnp.where(lane_v == 2, parts[2], 0.0)))
        gs3 = gs3.astype(BF)
        keep[0] = gs3

    def table_back():
        e0, e1 = table()
        hdel, gs3 = sec_ref[...], keep[0]
        lane_w = iota((width, 128), 1)
        wcol = jnp.where(lane_w < 3, e1.astype(F32)[:, SCORER : SCORER + 1], 0.0).astype(BF)
        gput(ELT, 0, dot_tn(hdel, gthi[:, :256]) + dot_tn(hdel, gtlo[:, :256]) + dot_nt(wcol, gs3[:256]))
        gs_tail = jnp.concatenate([gs3[256:], jnp.zeros((128 + 256 - VOC, 128), BF)], axis=0)
        tail = dot_tn(hdel, gthi[:, 256:]) + dot_tn(hdel, gtlo[:, 256:]) + dot_nt(wcol, gs_tail)
        scorer_grad = jnp.sum(dot(e0, gs3[:256]) + dot(e1, gs_tail), axis=1, keepdims=True)
        gains = [p.astype(F32) for p in (*split3(rows_ref[3:4, :]), *split3(rows_ref[4:5, :]))]
        gains = jnp.concatenate([*gains, jnp.zeros((10, width), F32)], axis=0).astype(BF)
        place_row, place_col = iota((16, 128), 0), iota((16, 128), 1)
        place = (place_row < 6) & (place_col == jnp.where(place_row < 3, SCORER + 1, SCORER + 2))
        tail = tail + dot_tn(gains, jnp.where(place, 1.0, 0.0).astype(BF))
        tail = jnp.where(lane_w == SCORER, scorer_grad, tail)
        gput(ELT, 1, jnp.concatenate([tail, jnp.zeros((width, 128), F32)], axis=1))


    enc_copy = net.copy(
        mixed.at[:, pl.ds(pl.multiple_of((1 - s) * half, 128), half)], enc_out.at[s],
        net.mi_s.at[0], net.mi_r.at[0], net.sib,
    )

    def send_encoded():
        encoded = dot_nt(encb[...].astype(BF), pi[...]).astype(BF)
        for h in (0, 1):
            mixed[:, h * half : (h + 1) * half] = encoded[:, h * half : (h + 1) * half]
        enc_out[s] = lanes(mixed, s, half)
        net.start(enc_copy)

    def last(m):
        mine, other = net.rs5(m)
        if m == WO or m in DN:
            first = jnp.where(s == 0, mine, other)
            second = jnp.where(s == 0, other, mine)
            both = jnp.concatenate([first, second], axis=1)
            value = sum(dot_nt(part, pi[...]) for part in split3(both))
            if m == WO:
                g_o[...] = value
            else:
                rows = value.shape[0]
                g_d[(m - DNA) * rows : (m - DNA + 1) * rows, :] = value
            return
        for h, value in ((s, mine), (1 - s, other)):
            if m in GU:
                cols = pl.ds(pl.multiple_of(h * ffh + (m - GU0) * quarter, 128), quarter)
                g_0[:, cols] = value[:, :quarter]
                g_1[:, cols] = value[:, quarter:]
            else:
                n = value.shape[1]
                target = {ELT: g_elt, WQ: g_q, WK: g_k, WV: g_v}[m]
                target[:, pl.ds(pl.multiple_of(h * n, 128), n)] = value

    pieces = (
        turn_cotangent, bias_lines, count_blocks, choose_blocks, make_hidden,
        *(functools.partial(project, *item) for item in ((WQ, qs), (WK, ks), (WV, vs))),
        *(functools.partial(forward_pairs, k) for k in range(pairs // 2)),
        make_middle,
        *(functools.partial(feed, c) for c in range(4)),
        middle_back, mixed_back,
        *(functools.partial(backward_pairs, k) for k in range(pairs // 2)),
        relative_back,
        *(functools.partial(weight_back, k) for k in range(3)),
        hidden_back, choice_back, table_back, send_encoded,
    )
    steps = {
        "A": net.ag1, "Z": net.ag2, "X": net.ag3, "D": net.ag4, "S": net.ag5,
        "a": net.rs0, "b": net.rs1, "c": net.rs2, "d": net.rs3, "e": net.rs4, "f": last,
        "p": lambda k: pieces[k](), "r": rel_step,
    }
    bias_lines()
    count_blocks()
    for fetch in fetches[:7]:
        fetch.wait()
    net.meet()
    for m in (ELT, WQ, WK, WV, *GU):
        exchange(m)
    first = (0, 1,)
    for m in first:
        net.own(m)
        net.ag1(m)

    wide[WO] = dot(wo[...].astype(BF), pi[...])
    down_p = dot(wd[...].astype(BF), pi[...])
    wide[DNA], wide[DNB] = down_p[: wd.shape[0] // 2], down_p[wd.shape[0] // 2 :]
    for m in (WO, *DN):
        exchange(m)
    for m in ALL:
        if m not in first:
            net.own(m)
    fetches[7].wait()
    for kind, index in SCHEDULE:
        steps[kind](index)
    enc_copy.wait_recv()
    net.finish()


VMEM = pl.BlockSpec(memory_space=pltpu.VMEM)


def call(inner, *args):
    wq, wi0, wd, cot = args[9], args[13], args[15], args[16]
    rows_d, width = wq.shape
    rows_f = wd.shape[0] // 2
    half, ffh = width // 2, wi0.shape[1] // 2
    tokens = cot.shape[1]
    span = 2 * tokens
    heads, buckets = args[8].shape
    wide = {m: 256 if m == ELT else ffh // 2 if m in GU else half for m in ALL}
    chip = {m: (2, rows_f) if m in DN else (2 * rows_d,) for m in ALL}
    mine = {m: rows_f if m in DN else rows_d for m in ALL}

    def full(m):
        return (2, 4, 4, rows_f, wide[m]) if m in DN else (4, 4, 2 * rows_d, wide[m])

    def part(m):
        return (2, 2, rows_f, wide[m]) if m in DN else (2, 2 * rows_d, wide[m])

    scratch = []
    scratch += [pltpu.VMEM((2, *full(m)), BF) for m in ALL]
    scratch += [pltpu.VMEM((2, *full(m)), BF) for m in ALL]
    scratch += [pltpu.VMEM(full(m), BF) for m in ALL]
    scratch += [
        pltpu.VMEM((3, *part(m)[1:]) if m in PLANE_REDUCE else part(m), BF) for m in ALL
    ]
    scratch += [pltpu.VMEM((16, 128) if m in PLANE_REDUCE else part(m), BF) for m in ALL]
    scratch += [
        pltpu.VMEM((3, *((4,) if m in PLANE_REDUCE else ()), *chip[m], wide[m]), BF) for m in ALL
    ]
    scratch += [pltpu.VMEM((*chip[m], wide[m]), F32) for m in ALL]
    scratch += [pltpu.VMEM((mine[m], wide[m]), F32) for m in ALL]
    scratch += [pltpu.VMEM((mine[m], wide[m]), F32) for m in ALL]
    dma = pltpu.SemaphoreType.DMA
    scratch += [dma((N, 12)), dma((N, 12)), dma((N, 9)), dma((N, 9)), dma((7,)), dma((7,))]
    act = (tokens, width)
    scratch += [
        pltpu.VMEM((width, width), BF),
        pltpu.VMEM((BLOCKS, VOC, span), BF),
        pltpu.VMEM((8, span), F32),
        pltpu.VMEM((tokens, 384), BF),
        pltpu.VMEM((tokens, 384), BF),
        pltpu.VMEM((8, width), F32),
        pltpu.VMEM(act, BF),
        pltpu.VMEM(act, BF),
        pltpu.VMEM((width, tokens), BF),
        pltpu.VMEM((width // 128, tokens, 128), BF),
        pltpu.VMEM((width // 128, tokens, 128), BF),
        pltpu.VMEM((width // 128, tokens, 128), BF),
        pltpu.VMEM((heads, 1, span), F32),
        pltpu.VMEM((heads, tokens, tokens), F32),
        pltpu.VMEM(act, BF),
        pltpu.VMEM(act, BF),
        pltpu.VMEM(act, F32),
        pltpu.VMEM(act, BF),
        pltpu.VMEM((width, tokens), BF),
        pltpu.VMEM(act, F32),
        pltpu.VMEM(act, F32),
        pltpu.VMEM(act, BF),
        pltpu.VMEM(act, BF),
        pltpu.VMEM(act, BF),
        pltpu.VMEM((heads, 1, span), F32),
        pltpu.VMEM((4, 16, 128), F32),
        pltpu.VMEM((6, 16, 128), F32),
        pltpu.VMEM(act, BF),
        *[pltpu.VMEM(item.shape, item.dtype) for item in args[9:]],
        dma((8,)),
    ]
    outs = [
        jax.ShapeDtypeStruct((MICRO, tokens, half), BF),
        jax.ShapeDtypeStruct((rows_d, 512), F32),
        *[jax.ShapeDtypeStruct(item.shape, F32) for item in args[9:16]],
        jax.ShapeDtypeStruct((16, 128), F32),
    ]
    return pl.pallas_call(
        functools.partial(kernel, inner, (tokens, width, half, ffh)),
        out_shape=outs,
        in_specs=[VMEM] * 9 + [pl.BlockSpec(memory_space=pl.ANY)] * 8,
        out_specs=[VMEM] * len(outs),
        scratch_shapes=scratch,
        compiler_params=pltpu.CompilerParams(
            collective_id=0, has_side_effects=True, vmem_limit_bytes=63 * 2**20
        ),
    )(*args)


def settle(vocab, langs, heads, buckets, *refs):
    ins, outs = refs[:10], refs[10:]
    outs[0][:, 0] = ins[0][...]
    rows = ins[1].shape[0]
    outs[1][...] = ins[1][:, :vocab]
    table = ins[1][:, 256:]
    table = jnp.concatenate([table, jnp.zeros((128 - rows, 256), F32)], axis=0).T[:, :rows]
    at = vocab - 256
    outs[2][...] = table[at : at + langs]
    at = at + langs
    for k, i in enumerate((3, 4, 9)):
        outs[i][...] = table[at + k : at + k + 1]
    for i, k in zip((5, 6, 7, 8, 10, 11, 12), range(2, 9)):
        outs[i][...] = ins[k][...]
    outs[13][...] = ins[9][:heads, :buckets]


def body(
    byte_ids, lengths, groups, embedding, language, scorer, prenorm, query_weight, key_weight, value_weight,
    output_weight, midnorm, gate_weight, up_weight, down_weight, relative, cotangent,
):
    inner = lax.axis_size("dp") // OUTER
    vocab, langs = embedding.shape[0], language.shape[0]
    tables = [embedding.T, language, scorer[None], prenorm[None], midnorm[None]]
    weights = [query_weight, key_weight, value_weight, output_weight, gate_weight, up_weight, down_weight]
    teams = [[o * inner + i for i in range(inner)] for o in range(OUTER)]
    if inner > 1:
        tables = [
            lax.all_gather(item, "dp", axis_index_groups=teams, axis=min(i, 1), tiled=True)
            for i, item in enumerate(tables)
        ]
        weights = [lax.all_gather(item, "dp", axis_index_groups=teams, axis=0, tiled=True) for item in weights]
    results = call(inner, byte_ids, lengths.T, groups.T, *tables, relative.T, *weights, cotangent[:, 0])
    if inner > 1:
        grads = [
            lax.psum_scatter(item, "dp", axis_index_groups=teams, scatter_dimension=0, tiled=True)
            for item in results[1:9]
        ]
        results = [results[0], *grads, lax.psum(results[9], "dp", axis_index_groups=teams)]
    buckets, heads = relative.shape
    rows = results[1].shape[0]
    line = jax.ShapeDtypeStruct((1, rows), F32)
    like = [jax.ShapeDtypeStruct(item.shape, F32) for item in results[2:9]]
    shapes = [
        jax.ShapeDtypeStruct(cotangent.shape[:3] + (results[0].shape[2],), BF),
        jax.ShapeDtypeStruct((rows, vocab), F32),
        jax.ShapeDtypeStruct((langs, rows), F32),
        line, line, *like[:4], line, *like[4:],
        jax.ShapeDtypeStruct((heads, buckets), F32),
    ]
    outs = pl.pallas_call(
        functools.partial(settle, vocab, langs, heads, buckets),
        out_shape=shapes,
        in_specs=[VMEM] * 10,
        out_specs=[VMEM] * 14,
        compiler_params=pltpu.CompilerParams(vmem_limit_bytes=60 * 2**20),
    )(*results)
    return tuple(item[0] if i in (3, 4, 9) else item.T if i in (1, 13) else item for i, item in enumerate(outs))


def solution(mesh):
    both = ("section", "dp")
    wide = P(both, None)
    return jax.shard_map(
        body,
        mesh=mesh,
        in_specs=(
            P(None, "dp", None), P(None, "dp"), P(None, "dp"), P(None, both), P(None, both), P(both), P(both),
            wide, wide, wide, wide, P(both), wide, wide, wide, P(), P(None, "dp", None, None),
        ),
        out_specs=(
            P(None, "dp", None, "section"), P(None, both), P(None, both), P(both), P(both),
            wide, wide, wide, wide, P(both), wide, wide, wide, P(),
        ),
        check_vma=False,
    )
```

```python
import functools

import jax
import jax.numpy as jnp
from jax import lax
from jax.experimental import pallas as pl
from jax.experimental.pallas import tpu as pltpu
from jax.sharding import PartitionSpec as P

BLOCKS = 4
DOWN = 2
MICRO = 2
OUTER = 16
EPSILON = 1e-06
NEGATIVE = -1000000000.0
LIMITS = (12, 16, 23, 32, 46, 64, 91)
MESH = pl.DeviceIdType.MESH
BF = jnp.bfloat16
F32 = jnp.float32
I32 = jnp.int32

ELT, WQ, WK, WV, WO, DNA, DNB, GU0, GU1, GU2, GU3 = range(11)
DN = (DNA, DNB)
GU = (GU0, GU1, GU2, GU3)
ALL = tuple(range(11))
N = len(ALL)
PLANE_GATHER = (10,)
PLANE_REDUCE = ()
SCHEDULE = (
    ("A", 10), ("Z", 0), ("A", 2), ("p", 0), ("Z", 1), ("A", 3), ("X", 0), ("Z", 2), ("A", 4), ("X", 1), ("D", 0),
    ("S", 0), ("p", 3), ("Z", 3), ("A", 5), ("X", 2), ("D", 1), ("p", 4), ("S", 1), ("p", 5), ("Z", 4), ("A", 6),
    ("X", 3), ("D", 2), ("S", 2), ("p", 6), ("Z", 5), ("A", 7), ("X", 4), ("D", 3), ("S", 3), ("p", 7), ("p", 8),
    ("Z", 6), ("A", 8), ("X", 5), ("D", 4), ("p", 9), ("S", 4), ("p", 10), ("Z", 7), ("A", 9), ("X", 6), ("D", 5),
    ("p", 11), ("S", 5), ("Z", 8), ("X", 7), ("D", 6), ("S", 6), ("Z", 9), ("Z", 10), ("X", 8), ("D", 7), ("S", 7),
    ("q", 0), ("q", 1), ("a", 7), ("X", 9), ("b", 7), ("D", 8), ("S", 8), ("q", 2), ("q", 3), ("a", 8), ("D", 9),
    ("b", 8), ("S", 9), ("q", 4), ("c", 7), ("q", 5), ("a", 9), ("b", 9), ("c", 8), ("X", 10), ("S", 10), ("q", 6),
    ("d", 7), ("q", 7), ("a", 10), ("a", 5), ("a", 6), ("c", 9), ("b", 10), ("d", 8), ("e", 7), ("p", 16), ("b", 5),
    ("a", 4), ("c", 10), ("b", 6), ("d", 9), ("e", 8), ("p", 17), ("p", 18), ("p", 19), ("c", 5), ("d", 10), ("e", 9),
    ("f", 7), ("p", 20), ("p", 21), ("p", 22), ("a", 1), ("c", 6), ("b", 4), ("d", 5), ("e", 10), ("p", 23), ("a", 2),
    ("p", 24), ("a", 3), ("b", 1), ("c", 4), ("d", 6), ("e", 5), ("f", 8), ("p", 25), ("r", 1), ("p", 26), ("b", 2),
    ("c", 1), ("d", 4), ("e", 6), ("p", 27), ("a", 0), ("r", 2), ("b", 3), ("c", 2), ("d", 1), ("e", 4), ("f", 9),
    ("f", 10), ("p", 28), ("r", 3), ("b", 0), ("c", 3), ("d", 2), ("e", 1), ("f", 5), ("f", 6), ("r", 4), ("c", 0),
    ("d", 3), ("e", 2), ("f", 1), ("f", 4), ("d", 0), ("e", 3), ("f", 2), ("e", 0), ("f", 3), ("f", 0),
)
VOC = 288
SCORER = 19


def dot(a, b):
    return lax.dot_general(a, b, (((1,), (0,)), ((), ())), preferred_element_type=F32)


def dot_nt(a, b):
    return lax.dot_general(a, b, (((1,), (1,)), ((), ())), preferred_element_type=F32)


def dot_tn(a, b):
    return lax.dot_general(a, b, (((0,), (0,)), ((), ())), preferred_element_type=F32)


def split3(x):
    hi = x.astype(BF)
    rest = x - hi.astype(F32)
    mid = rest.astype(BF)
    return hi, mid, (rest - mid.astype(F32)).astype(BF)


def iota(shape, axis):
    return lax.broadcasted_iota(I32, shape, axis)


def over(value, n):
    return (value * (65536 // n + 1)) >> 16


def bucket_ids(offsets):
    distance = jnp.abs(offsets)
    larger = 8 + sum(((distance >= limit).astype(I32) for limit in LIMITS))
    inside = jnp.where(distance < 8, distance, larger)
    return jnp.where(offsets > 0, 16, 0).astype(I32) + inside


class Net:
    def __init__(self, inner, w, g, sb, x1, y1, zi, ch, tmp, fo, sems):
        self.w, self.g, self.sb, self.x1, self.y1 = w, g, sb, x1, y1
        self.zi, self.ch, self.tmp, self.fo = zi, ch, tmp, fo
        self.ag_s, self.ag_r, self.rs_s, self.rs_r, self.mi_s, self.mi_r = sems
        self.s = lax.axis_index("section")
        self.d = lax.axis_index("dp")
        outer = self.d // inner
        self.z = outer // 4
        self.yx = outer % 4
        y, x = self.yx // 2, self.yx % 2
        self.sib = (1 - self.s, self.d)
        self.yx_x = self.yx + 1 - 2 * x
        self.yx_y = self.yx + 2 - 4 * y
        self.yx_d = 3 - self.yx
        self.xn = (self.s, self.d + (1 - 2 * x) * inner)
        self.yn = (self.s, self.d + (1 - 2 * y) * 2 * inner)
        self.dn = (self.s, self.d + (1 - 2 * x) * inner + (1 - 2 * y) * 2 * inner)
        self.zz = [(self.z + k) % 4 for k in (1, 2, 3)]
        self.zn = [(self.s, self.d + (zz - self.z) * 4 * inner) for zz in self.zz]
        self.sent = []

    def greet(self):
        barrier = pltpu.get_barrier_semaphore()
        for device in (self.sib, self.xn, self.yn, self.dn, *self.zn):
            pl.semaphore_signal(barrier, inc=1, device_id=device, device_id_type=MESH)

    def meet(self):
        pl.semaphore_wait(pltpu.get_barrier_semaphore(), 7)

    def copy(self, src, dst, send, recv, device):
        return pltpu.make_async_remote_copy(
            src_ref=src, dst_ref=dst, send_sem=send, recv_sem=recv,
            device_id=device, device_id_type=MESH,
        )

    def start(self, copy):
        copy.start()
        self.sent.append(copy)

    def finish(self):
        for copy in self.sent:
            copy.wait_send()
        self.sent = []

    def blk(self, ref, m, h, z, yx):
        return ref.at[h, :, z, yx] if m in DN else ref.at[h, z, yx]

    def grp(self, ref, m, h, yx):
        return ref.at[h, :, :, yx] if m in DN else ref.at[h, :, yx]

    def part(self, ref, m, h, z0, yx):
        return ref.at[h, :, pl.ds(z0, 2), yx] if m in DN else ref.at[h, pl.ds(z0, 2), yx]

    def plane(self, ref, m, h, z):
        return ref.at[h, :, z] if m in DN else ref.at[h, z]

    def xy2(self, m):
        if m in DN:
            return self.sb[m].at[0, pl.ds(0, 2)], self.sb[m].at[0, pl.ds(2, 2)]
        return self.sb[m].at[0], self.sb[m].at[1]

    def ag(self, m, slot):
        w, s = self.w[m], self.s
        pair = lambda src, dst, dev: self.copy(src, dst, self.ag_s.at[m, slot], self.ag_r.at[m, slot], dev)
        if slot == 0:
            if m in DN:
                dst = self.ch[m].at[s]
            else:
                rows = self.tmp[m].shape[0]
                dst = self.ch[m].at[pl.ds(s * rows, rows)]
            return pair(self.tmp[m], dst, self.sib)
        if m in PLANE_GATHER:
            if slot <= 3:
                ref = self.blk(w, m, s, self.z, self.yx)
                return pair(ref, ref, (self.xn, self.yn, self.dn)[slot - 1])
            ref = self.plane(w, m, s, (self.z, *self.zz)[(0, 0, 0, 0, 3, 2, 1)[slot - 4]] if slot > 7 else self.z)
            return pair(ref, ref, self.sib if slot >= 7 else self.zn[slot - 4])
        if slot <= 3:
            ref = self.blk(w, m, s, self.z, self.yx)
            return pair(ref, ref, self.zn[slot - 1])
        if slot <= 5:
            ref = self.grp(w, m, s, self.yx)
            return pair(ref, ref, self.xn if slot == 4 else self.yn)
        if slot == 6:
            ref = self.part(w, m, s, 0, self.yx_x)
            return pair(ref, ref, self.yn)
        if slot == 7:
            ref = self.part(w, m, s, 2, self.yx_y)
            return pair(ref, ref, self.xn)
        ref = self.grp(w, m, s, (self.yx, self.yx_x, self.yx_y, self.yx_d)[slot - 8])
        return pair(ref, ref, self.sib)

    def ag0(self, m):
        self.start(self.ag(m, 0))

    def own(self, m):
        self.ag(m, 0).wait_recv()
        chunk = self.ch[m][...].astype(BF)
        if m in DN:
            for sec in (0, 1):
                self.w[m][self.s, sec, self.z, self.yx] = chunk[sec]
        else:
            self.w[m][self.s, self.z, self.yx] = chunk

    def ag1(self, m):
        for slot in (1, 2, 3):
            self.start(self.ag(m, slot))

    def ag2(self, m):
        for slot in (1, 2, 3):
            self.ag(m, slot).wait_recv()
        for slot in (4, 5, 6, 7) if m in PLANE_GATHER else (4, 5, 8):
            self.start(self.ag(m, slot))

    def ag3(self, m):
        chain = ((4, (8,)), (5, (9,)), (6, (10,))) if m in PLANE_GATHER else ((4, (6, 9)), (5, (7, 10)))
        for slot, onward in chain:
            self.ag(m, slot).wait_recv()
            for then in onward:
                self.start(self.ag(m, then))

    def ag4(self, m):
        if m in PLANE_GATHER:
            return
        for slot in (6, 7):
            self.ag(m, slot).wait_recv()
        self.start(self.ag(m, 11))

    def ag5(self, m):
        for slot in (7, 8, 9, 10) if m in PLANE_GATHER else (8, 9, 10, 11):
            self.ag(m, slot).wait_recv()

    def rs(self, m, slot):
        g, s = self.g[m], self.s
        pair = lambda src, dst, dev: self.copy(src, dst, self.rs_s.at[m, slot], self.rs_r.at[m, slot], dev)
        if slot == 0:
            return pair(g.at[1 - s], self.sb[m], self.sib)
        if m in PLANE_REDUCE and slot <= 6:
            if slot <= 3:
                return pair(self.plane(g, m, s, self.zz[slot - 1]), self.zi[m].at[slot - 1], self.zn[slot - 1])
            k = slot - 4
            ref = self.blk(g, m, s, self.z, (self.yx_x, self.yx_y, self.yx_d)[k])
            return pair(ref, self.x1[m].at[k], (self.xn, self.yn, self.dn)[k])
        if slot == 1:
            return pair(self.part(g, m, s, 0, self.yx_d), self.x1[m], self.xn)
        if slot == 2:
            return pair(self.part(g, m, s, 2, self.yx_d), self.y1[m], self.yn)
        if slot == 3:
            return pair(self.grp(g, m, s, self.yx_x), self.xy2(m)[0], self.xn)
        if slot == 4:
            return pair(self.grp(g, m, s, self.yx_y), self.xy2(m)[1], self.yn)
        if slot <= 7:
            k = slot - 5
            return pair(self.blk(g, m, s, self.zz[k], self.yx), self.zi[m].at[k], self.zn[k])
        if m in DN:
            src = self.ch[m].at[1 - s]
        else:
            rows = self.fo[m].shape[0]
            src = self.ch[m].at[pl.ds((1 - s) * rows, rows)]
        return pair(src, self.fo[m], self.sib)

    def rs0(self, m):
        self.start(self.rs(m, 0))

    def rs1(self, m):
        self.rs(m, 0).wait_recv()
        g, sb, s = self.g[m], self.sb[m], self.s

        def add(i, carry):
            if m in DN:
                at = (i // 4, i % 4)
                g[s, at[0], at[1]] = (g[s, at[0], at[1]].astype(F32) + sb[at[0], at[1]].astype(F32)).astype(BF)
            else:
                g[s, i // 4, i % 4] = (g[s, i // 4, i % 4].astype(F32) + sb[i // 4, i % 4].astype(F32)).astype(BF)
            return carry

        lax.fori_loop(0, 8 if m in DN else 16, add, 0)
        for slot in (1, 2, 3) if m in PLANE_REDUCE else (1, 2):
            self.start(self.rs(m, slot))

    def rs2(self, m):
        g, s = self.g[m], self.s
        if m in PLANE_REDUCE:
            for slot in (1, 2, 3):
                self.rs(m, slot).wait_recv()
            zi = self.zi[m]

            def whole(yx):
                parts = [zi[k, yx].astype(F32) for k in (0, 1, 2)]
                return g[s, self.z, yx].astype(F32) + (parts[0] + parts[1] + parts[2])

            for slot, yx in ((4, self.yx_x), (5, self.yx_y), (6, self.yx_d)):
                g[s, self.z, yx] = whole(yx).astype(BF)
                self.start(self.rs(m, slot))
            self.ch[m][...] = whole(self.yx)
            return
        for slot, ref, z0, yx in ((1, self.x1[m], 0, self.yx_y), (2, self.y1[m], 2, self.yx_x)):
            self.rs(m, slot).wait_recv()
            for j in (0, 1):
                if m in DN:
                    for sec in (0, 1):
                        mine = g[s, sec, z0 + j, yx].astype(F32)
                        g[s, sec, z0 + j, yx] = (mine + ref[sec, j].astype(F32)).astype(BF)
                else:
                    mine = g[s, z0 + j, yx].astype(F32)
                    g[s, z0 + j, yx] = (mine + ref[j].astype(F32)).astype(BF)
        self.start(self.rs(m, 3))
        self.start(self.rs(m, 4))

    def rs3(self, m):
        if m in PLANE_REDUCE:
            for slot in (4, 5, 6):
                self.rs(m, slot).wait_recv()
            x1 = self.x1[m]
            self.ch[m][...] += x1[0].astype(F32) + x1[1].astype(F32) + x1[2].astype(F32)
            self.start(self.rs(m, 8))
            return
        self.rs(m, 3).wait_recv()
        self.rs(m, 4).wait_recv()
        g, s, yx = self.g[m], self.s, self.yx
        a, b = self.xy2(m)

        def total(sec, z):
            if m in DN:
                return g[s, sec, z, yx].astype(F32) + a[sec, z].astype(F32) + b[sec, z].astype(F32)
            return g[s, z, yx].astype(F32) + a[z].astype(F32) + b[z].astype(F32)

        for slot in (5, 6, 7):
            zz = self.zz[slot - 5]
            if m in DN:
                for sec in (0, 1):
                    g[s, sec, zz, yx] = total(sec, zz).astype(BF)
            else:
                g[s, zz, yx] = total(0, zz).astype(BF)
            self.start(self.rs(m, slot))
        if m in DN:
            for sec in (0, 1):
                self.ch[m][sec] = total(sec, self.z)
        else:
            self.ch[m][...] = total(0, self.z)

    def rs4(self, m):
        if m in PLANE_REDUCE:
            return
        for slot in (5, 6, 7):
            self.rs(m, slot).wait_recv()
        zi = self.zi[m]
        self.ch[m][...] += zi[0].astype(F32) + zi[1].astype(F32) + zi[2].astype(F32)
        self.start(self.rs(m, 8))

    def rs5(self, m):
        if m in DN:
            mine = self.ch[m][self.s]
        else:
            rows = self.fo[m].shape[0]
            mine = self.ch[m][pl.ds(self.s * rows, rows)]
        self.rs(m, 8).wait_recv()
        return mine, self.fo[m][...]


def kernel(inner, sizes, *refs):
    (byte_ids, lengths, groups, emb, lang, scorer, prenorm, midnorm, rel) = refs[:9]
    given = refs[9:17]
    enc_out, g_elt, *final, g_rel = refs[17:27]
    rest = refs[27:]
    take = lambda k: rest[N * k : N * k + N]
    w, g, sb, x1, y1, zi, ch, tmp, fo = (take(k) for k in range(9))
    rest = rest[9 * N :]
    sems, rest = rest[:6], rest[6:]
    (pi, cb, prow, gthi, gtlo, rows_ref, hid, nrm, nrmt, qs, ks, vs, bvec, pmat, mixed, mixp, mid, sec_ref, sect,
     acc, encb, dq, dk, dv, dvec, relbuf, relin, cp) = rest[:28]
    held, arrived = rest[28:36], rest[36]
    made, written = rest[37:44], rest[44]
    (g_q, g_k, g_v, g_o, g_0, g_1, g_d) = made
    (wq, wk, wv, wo, wi0, wi1, wd, cot) = held
    tokens, width, half, ffh = sizes
    quarter = ffh // 4
    net = Net(inner, w, g, sb, x1, y1, zi, ch, tmp, fo, sems)
    s = net.s
    net.greet()
    fetches = [pltpu.make_async_copy(a, b, arrived.at[k]) for k, (a, b) in enumerate(zip(given, held))]
    for fetch in fetches:
        fetch.start()

    def lanes(ref, h, n):
        return ref[:, pl.ds(pl.multiple_of(h * n, 128), n)]

    def wmat(m, h):
        return w[m][h].reshape(width, w[m].shape[-1])

    def gput(m, h, value):
        g[m][h] = value.astype(BF).reshape(g[m].shape[1:])

    rows_d = wq.shape[0]
    vocab, langs = emb.shape[1], lang.shape[0]

    def turned(value, at):
        rows = value.shape[0]
        more = -rows % 8
        if more:
            value = jnp.concatenate([value, jnp.zeros((more, rows_d), F32)], axis=0)
        row = iota((rows + more, 512), 0)
        spot = (row + at == iota((rows + more, 512), 1)) & (row < rows)
        return dot_tn(value.astype(BF), jnp.where(spot, 1.0, 0.0).astype(BF))

    col = iota((1, width), 1)
    chip = over(col, 2 * rows_d)
    inside = col - chip * (2 * rows_d)
    natural = jnp.where(inside < rows_d, chip * rows_d + inside, half + (chip - 1) * rows_d + inside)
    pi[...] = jnp.where(iota((width, width), 0) == natural, 1.0, 0.0).astype(BF)
    vectors = jnp.concatenate([scorer[...], prenorm[...], midnorm[...]], axis=0)
    spread = jnp.where(iota((vocab, 512), 0) == iota((vocab, 512), 1), 1.0, 0.0).astype(BF)
    elt = dot(emb[...].astype(BF), spread) + turned(lang[...], vocab) + turned(vectors, 256 + SCORER)
    wide = {}

    def halves(m, h):
        if m == ELT:
            return jnp.where(h == 0, elt[:, :256], elt[:, 256:])
        if m in (WQ, WK, WV):
            return lanes({WQ: wq, WK: wk, WV: wv}[m], h, half)
        if m in GU:
            cols = pl.ds(pl.multiple_of(h * ffh + (m - GU0) * quarter, 128), quarter)
            return jnp.concatenate([wi0[:, cols], wi1[:, cols]], axis=1)
        value = wide[m]
        return jnp.where(h == 0, value[:, :half], value[:, half:])

    def exchange(m):
        tmp[m][...] = halves(m, 1 - s)
        net.ag0(m)
        mine = halves(m, s)
        if m in DN:
            ch[m][s] = mine
        else:
            ch[m][pl.ds(s * rows_d, rows_d)] = mine

    span = 2 * tokens
    heads, buckets = rel.shape
    pairs = width // 128
    keep = {}
    mdel = acc

    def turn_cotangent():
        cp[...] = dot(cot[s], pi[...]).astype(BF)


    def bias_lines():
        ohb = jnp.where(iota((buckets, span), 0) == bucket_ids(iota((buckets, span), 1) - (tokens - 1)), 1.0, 0.0)
        bv = sum(dot(part, ohb.astype(BF)) for part in split3(rel[...]))
        for h in range(heads):
            bvec[h] = bv[h : h + 1, :]

    length = jnp.where(s == 0, lengths[:, 0:1], lengths[:, 1:2])
    group = jnp.where(s == 0, groups[:, 0:1], groups[:, 1:2])

    def block_of(p, size):
        return p if size == 1 else p >> 1 if size == 2 else over(p, 3) if size == 3 else p >> 2

    def count_blocks():
        col = iota((1, span), 1)
        pos = jnp.where(col < tokens, 2 * col, 2 * (col - tokens) + 1)
        symbol = iota((VOC, span), 0)
        onehot = jnp.where(((symbol == byte_ids[s]) | (symbol == group + vocab)) & (col < length), 1.0, 0.0).astype(BF)
        rowi = iota((span, 1), 0)
        for size in range(1, BLOCKS + 1):
            pool = jnp.where(block_of(rowi, size) == block_of(pos, size), 1.0, 0.0).astype(BF)
            cb[size - 1] = dot(onehot, pool).astype(BF)

    def table():
        return wmat(ELT, 0), wmat(ELT, 1)[:, :128]

    def choose_blocks():
        e0, e1 = table()
        picks = jnp.where(iota((8, 128), 1) == iota((8, 128), 0) + SCORER, 1.0, 0.0).astype(BF)
        rows_ref[...] = dot_nt(picks, e1)
        ew = jnp.concatenate([dot_tn(e0, e1), dot_tn(e1, e1)[: VOC - 256]], axis=0)[:, SCORER : SCORER + 1]
        ratings = [jnp.sum(cb[b].astype(F32) * ew, axis=0, keepdims=True) / (b + 1) for b in range(BLOCKS)]
        top = functools.reduce(jnp.maximum, ratings)
        raised = [jnp.exp(r - top) for r in ratings]
        total = sum(raised)
        chosen = [r / total for r in raised]
        mixw = 0.0
        for b in range(BLOCKS):
            prow[b : b + 1, :] = chosen[b]
            mixw = mixw + cb[b].astype(F32) * (chosen[b] / (2.0 * (b + 1)))
        gt = mixw[:, :tokens] + mixw[:, tokens:]
        gt = jnp.concatenate([gt, jnp.zeros((384 - VOC, tokens), F32)], axis=0).T
        gthi[...] = gt.astype(BF)
        gtlo[...] = (gt - gt.astype(BF).astype(F32)).astype(BF)

    def make_hidden():
        e0, e1 = table()
        latent = (
            dot_nt(gthi[:, :256], e0) + dot_nt(gthi[:, 256:], e1)
            + dot_nt(gtlo[:, :256], e0) + dot_nt(gtlo[:, 256:], e1)
        )
        hid[...] = latent.astype(BF)

        hidden = hid[...].astype(F32)
        r1 = lax.rsqrt(jnp.mean(hidden * hidden, -1, keepdims=True) + EPSILON)
        normed = hidden * r1 * rows_ref[1:2, :]
        nrm[...] = normed.astype(BF)
        nrmt[...] = normed.T.astype(BF)

    def project(m, ref):
        for h in (0, 1):
            out = dot(nrm[...], wmat(m, h)).astype(BF)
            for i in range(half // 128):
                ref[h * (half // 128) + i] = out[:, i * 128 : (i + 1) * 128]

    tcol = iota((1, tokens), 1)
    valid_key = DOWN * tcol < length
    lane = iota((1, 128), 1)
    masks = [jnp.where(lane < 64, 1.0 - e, float(e)).astype(BF) for e in (0, 1)]

    def forward_pair(i, carry):
        q2, k2, v2 = qs[i], ks[i], vs[i]
        out = 0.0
        for e in (0, 1):
            h = 2 * i + e
            line = jnp.broadcast_to(bvec[h], (tokens, span))
            bias = pltpu.roll(line, tokens + 1, 1, stride=1, stride_axis=0)[:, :tokens]
            scores = jnp.where(valid_key, dot_nt(q2, k2 * masks[e]) + bias, NEGATIVE)
            up = jnp.exp(scores - jnp.max(scores, -1, keepdims=True))
            prob = up * (1.0 / jnp.sum(up, -1, keepdims=True))
            pmat[h] = prob
            out = out + dot(prob.astype(BF), v2 * masks[e])
        mixed[:, pl.ds(pl.multiple_of(i * 128, 128), 128)] = out.astype(BF)
        return carry

    def forward_pairs(k):
        lax.fori_loop(2 * k, 2 * k + 2, forward_pair, 0)

    def make_middle():
        mixp[...] = dot(mixed[...], pi[...]).astype(BF)
        for h in (0, 1):
            cols = slice(h * half, (h + 1) * half)
            mid[:, cols] = hid[:, cols].astype(F32) + dot(mixp[...], wmat(WO, h))
        middle = mid[...]
        r2 = lax.rsqrt(jnp.mean(middle * middle, -1, keepdims=True) + EPSILON)
        second = middle * r2 * rows_ref[2:3, :]
        sec_ref[...] = second.astype(BF)
        sect[...] = second.T.astype(BF)
        acc[...] = jnp.zeros_like(acc)
        encb[...] = mid[...]

    def feed(k):
        c, half_at = k // 2, k % 2

        def one(h, carry):
            wgu = w[GU0 + c][h].reshape(width, 2 * quarter)
            wdn = [
                jnp.concatenate([w[m][j, h, c] for m in DN], axis=1).reshape(quarter, half) for j in (0, 1)
            ]
            both = dot(sec_ref[...], wgu)
            gate, upper = both[:, :quarter], both[:, quarter:]
            pdelta = dot_nt(cp[:, :half], wdn[0]) + dot_nt(cp[:, half:], wdn[1])
            square = gate * gate
            tanh = jnp.tanh(0.7978845608 * (gate + 0.044715 * square * gate))
            act = 0.5 * gate * (1.0 + tanh)
            slope = 0.5 * (1.0 + tanh) + 0.5 * gate * (1.0 - tanh * tanh) * 0.7978845608 * (1.0 + 0.134145 * square)
            product = (act * upper).astype(BF)
            delta = jnp.concatenate([(pdelta * upper * slope).astype(BF), (pdelta * act).astype(BF)], axis=1)
            gput(GU0 + c, h, dot(sect[...], delta))
            for j in (0, 1):
                out = slice(j * half, (j + 1) * half)
                grad = dot_tn(product, cp[:, out]).astype(BF).reshape(4, -1, half)
                few = grad.shape[1] // 2
                g[DNA][j, h, c], g[DNB][j, h, c] = grad[:, :few], grad[:, few:]
                encb[:, out] += dot(product, wdn[j])
            acc[...] += dot_nt(delta, wgu)
            return carry

        lax.fori_loop(half_at, half_at + 1, one, 0)

    def middle_back():
        middle = mid[...]
        r2 = lax.rsqrt(jnp.mean(middle * middle, -1, keepdims=True) + EPSILON)
        n2 = middle * r2
        sdelta = acc[...]
        scaled = sdelta * rows_ref[2:3, :]
        rows_ref[4:5, :] = jnp.sum(sdelta * n2, axis=0, keepdims=True)
        mdel[...] = cp[...].astype(F32) + r2 * (scaled - n2 * jnp.mean(scaled * n2, -1, keepdims=True))
        sec_ref[...] = mdel[...].astype(BF)
        for h in (0, 1):
            gput(WO, h, dot_tn(mixp[...], sec_ref[:, h * half : (h + 1) * half]))

    def mixed_back():
        back = dot_nt(sec_ref[:, :half], wmat(WO, 0)) + dot_nt(sec_ref[:, half:], wmat(WO, 1))
        mixp[...] = dot_nt(back.astype(BF), pi[...]).astype(BF)
        mid[...] = jnp.zeros_like(mid)

    flip = jnp.where(iota((tokens, tokens), 0) + iota((tokens, tokens), 1) == tokens - 1, 1.0, 0.0).astype(BF)

    def backward_pair(i, carry):
        cols = pl.ds(pl.multiple_of(i * 128, 128), 128)
        q2, k2, v2, m2 = qs[i], ks[i], vs[i], mixp[:, cols]
        outq = outk = outv = 0.0
        for e in (0, 1):
            h = 2 * i + e
            prob = pmat[h]
            wdelta = dot_nt(m2, v2 * masks[e])
            lean = jnp.sum(prob * wdelta, -1, keepdims=True)
            sd = jnp.where(valid_key, prob * (wdelta - lean), 0.0).astype(BF)
            outq = outq + dot(sd, k2 * masks[e])
            outk = outk + dot_tn(sd, q2 * masks[e])
            outv = outv + dot_tn(prob.astype(BF), m2 * masks[e])
            reverse = jnp.concatenate([dot(sd, flip), jnp.zeros((tokens, tokens), F32)], axis=1)
            skew = pltpu.roll(reverse, 0, 1, stride=1, stride_axis=0)
            dvec[h] = jnp.sum(skew, axis=0, keepdims=True)
        dq[:, cols], dk[:, cols], dv[:, cols] = outq.astype(BF), outk.astype(BF), outv.astype(BF)
        return carry

    def backward_pairs(k):
        lax.fori_loop(2 * k, 2 * k + 2, backward_pair, 0)

    def relative_back():
        ohr = jnp.where(iota((128, span), 0) == bucket_ids((tokens - 1) - iota((128, span), 1)), 1.0, 0.0).astype(BF)
        lines = jnp.concatenate([dvec[h] for h in range(heads)] + [jnp.zeros((16 - heads, span), F32)], axis=0)
        relbuf[0] = sum(dot_nt(part, ohr) for part in split3(lines))
        rel_step(0)

    levels = (
        ((0, net.sib),), ((1, net.xn),), ((2, net.yn),), ((3, net.zn[0]), (4, net.zn[1]), (5, net.zn[2])),
    )

    def rel_copy(slot, level, device):
        return net.copy(relbuf.at[level], relin.at[slot], net.mi_s.at[1 + slot], net.mi_r.at[1 + slot], device)

    def rel_step(level):
        if level:
            for slot, device in levels[level - 1]:
                rel_copy(slot, level - 1, device).wait_recv()
        if level in (1, 2, 3):
            relbuf[level] = relbuf[level - 1] + relin[level - 1]
        if level < 4:
            for slot, device in levels[level]:
                net.start(rel_copy(slot, level, device))
            return
        place = [jnp.where(net.z == k, 1.0, 0.0) for k in range(4)]
        level = [relbuf[3], relin[3], relin[4], relin[5]]
        summed = 0.0
        for k in range(4):
            summed = summed + sum(place[z] * level[(z - k) % 4] for z in range(4))
        g_rel[...] = summed

    def weight_back(k):
        m, ref = ((WQ, dq), (WK, dk), (WV, dv))[k]
        for h in (0, 1):
            part = ref[:, h * half : (h + 1) * half]
            gput(m, h, dot(nrmt[...], part))
            mid[...] += dot_nt(part, wmat(m, h))

    def hidden_back():
        hidden = hid[...].astype(F32)
        norm_delta = mid[...]
        r1 = lax.rsqrt(jnp.mean(hidden * hidden, -1, keepdims=True) + EPSILON)
        n1 = hidden * r1
        scaled = norm_delta * rows_ref[1:2, :]
        rows_ref[3:4, :] = jnp.sum(norm_delta * n1, axis=0, keepdims=True)
        delta = mdel[...] + r1 * (scaled - n1 * jnp.mean(scaled * n1, -1, keepdims=True))
        sec_ref[...] = delta.astype(BF)

    def choice_back():
        e0, e1 = table()
        hdel = sec_ref[...]
        back = jnp.concatenate([dot(hdel, e0), dot(hdel, e1)], axis=1).T[:VOC]
        back = jnp.concatenate([back, back], axis=1)
        pdel = [jnp.sum(cb[b].astype(F32) * back, axis=0, keepdims=True) / (2.0 * (b + 1)) for b in range(BLOCKS)]
        lean = sum(prow[b : b + 1, :] * pdel[b] for b in range(BLOCKS))
        flow = 0.0
        for b in range(BLOCKS):
            flow = flow + cb[b].astype(F32) * (prow[b : b + 1, :] * (pdel[b] - lean) / (b + 1))
        gs = jnp.sum(flow, axis=1, keepdims=True)
        lane_v = iota((VOC, 128), 1)
        parts = [p.astype(F32) for p in split3(gs)]
        gs3 = jnp.where(lane_v == 0, parts[0], jnp.where(lane_v == 1, parts[1], jnp.where(lane_v == 2, parts[2], 0.0)))
        gs3 = gs3.astype(BF)
        keep[0] = gs3

    def table_back():
        e0, e1 = table()
        hdel, gs3 = sec_ref[...], keep[0]
        lane_w = iota((width, 128), 1)
        wcol = jnp.where(lane_w < 3, e1.astype(F32)[:, SCORER : SCORER + 1], 0.0).astype(BF)
        gput(ELT, 0, dot_tn(hdel, gthi[:, :256]) + dot_tn(hdel, gtlo[:, :256]) + dot_nt(wcol, gs3[:256]))
        gs_tail = jnp.concatenate([gs3[256:], jnp.zeros((128 + 256 - VOC, 128), BF)], axis=0)
        tail = dot_tn(hdel, gthi[:, 256:]) + dot_tn(hdel, gtlo[:, 256:]) + dot_nt(wcol, gs_tail)
        scorer_grad = jnp.sum(dot(e0, gs3[:256]) + dot(e1, gs_tail), axis=1, keepdims=True)
        gains = [p.astype(F32) for p in (*split3(rows_ref[3:4, :]), *split3(rows_ref[4:5, :]))]
        gains = jnp.concatenate([*gains, jnp.zeros((10, width), F32)], axis=0).astype(BF)
        place_row, place_col = iota((16, 128), 0), iota((16, 128), 1)
        place = (place_row < 6) & (place_col == jnp.where(place_row < 3, SCORER + 1, SCORER + 2))
        tail = tail + dot_tn(gains, jnp.where(place, 1.0, 0.0).astype(BF))
        tail = jnp.where(lane_w == SCORER, scorer_grad, tail)
        gput(ELT, 1, jnp.concatenate([tail, jnp.zeros((width, 128), F32)], axis=1))


    enc_copy = net.copy(
        mixed.at[:, pl.ds(pl.multiple_of((1 - s) * half, 128), half)], enc_out.at[s],
        net.mi_s.at[0], net.mi_r.at[0], net.sib,
    )

    def send_encoded():
        encoded = dot_nt(encb[...].astype(BF), pi[...]).astype(BF)
        for h in (0, 1):
            mixed[:, h * half : (h + 1) * half] = encoded[:, h * half : (h + 1) * half]
        enc_out[s] = lanes(mixed, s, half)
        net.start(enc_copy)

    def last(m):
        mine, other = net.rs5(m)
        if m == WO or m in DN:
            first = jnp.where(s == 0, mine, other)
            second = jnp.where(s == 0, other, mine)
            both = jnp.concatenate([first, second], axis=1)
            value = sum(dot_nt(part, pi[...]) for part in split3(both))
            if m == WO:
                g_o[...] = value
            else:
                rows = value.shape[0]
                g_d[(m - DNA) * rows : (m - DNA + 1) * rows, :] = value
            return
        for h, value in ((s, mine), (1 - s, other)):
            if m in GU:
                cols = pl.ds(pl.multiple_of(h * ffh + (m - GU0) * quarter, 128), quarter)
                g_0[:, cols] = value[:, :quarter]
                g_1[:, cols] = value[:, quarter:]
            else:
                n = value.shape[1]
                target = {ELT: g_elt, WQ: g_q, WK: g_k, WV: g_v}[m]
                target[:, pl.ds(pl.multiple_of(h * n, 128), n)] = value

    pieces = (
        turn_cotangent, bias_lines, count_blocks, choose_blocks, make_hidden,
        *(functools.partial(project, *item) for item in ((WQ, qs), (WK, ks), (WV, vs))),
        *(functools.partial(forward_pairs, k) for k in range(pairs // 2)),
        make_middle,
        *(None for c in range(4)),
        middle_back, mixed_back,
        *(functools.partial(backward_pairs, k) for k in range(pairs // 2)),
        relative_back,
        *(functools.partial(weight_back, k) for k in range(3)),
        hidden_back, choice_back, table_back, send_encoded,
    )
    steps = {
        "A": net.ag1, "Z": net.ag2, "X": net.ag3, "D": net.ag4, "S": net.ag5,
        "a": net.rs0, "b": net.rs1, "c": net.rs2, "d": net.rs3, "e": net.rs4, "f": last,
        "p": lambda k: pieces[k](), "q": feed, "r": rel_step,
    }
    bias_lines()
    count_blocks()
    for fetch in fetches[:7]:
        fetch.wait()
    net.meet()
    for m in (ELT, WQ, WK, WV, *GU):
        exchange(m)
    first = (0, 1,)
    for m in first:
        net.own(m)
        net.ag1(m)

    wide[WO] = dot(wo[...].astype(BF), pi[...])
    down_p = dot(wd[...].astype(BF), pi[...])
    wide[DNA], wide[DNB] = down_p[: wd.shape[0] // 2], down_p[wd.shape[0] // 2 :]
    for m in (WO, *DN):
        exchange(m)
    for m in ALL:
        if m not in first:
            net.own(m)
    fetches[7].wait()
    groups_of = ((WQ,), (WK,), (WV,), (WO,), GU, GU, DN)
    writes = [pltpu.make_async_copy(a, b, written.at[k]) for k, (a, b) in enumerate(zip(made, final))]
    missing = set(ALL)
    for kind, index in SCHEDULE:
        steps[kind](index)
        if kind == "f":
            missing.discard(index)
            for write, groups in zip(writes, groups_of):
                if index in groups and not missing.intersection(groups):
                    write.start()
    enc_copy.wait_recv()
    net.finish()
    for write in writes:
        write.wait()


VMEM = pl.BlockSpec(memory_space=pltpu.VMEM)
ANY = pl.BlockSpec(memory_space=pl.ANY)


def call(inner, *args):
    wq, wi0, wd, cot = args[9], args[13], args[15], args[16]
    rows_d, width = wq.shape
    rows_f = wd.shape[0] // 2
    half, ffh = width // 2, wi0.shape[1] // 2
    tokens = cot.shape[1]
    span = 2 * tokens
    heads, buckets = args[8].shape
    wide = {m: 256 if m == ELT else ffh // 2 if m in GU else half for m in ALL}
    chip = {m: (2, rows_f) if m in DN else (2 * rows_d,) for m in ALL}
    mine = {m: rows_f if m in DN else rows_d for m in ALL}

    def full(m):
        return (2, 4, 4, rows_f, wide[m]) if m in DN else (4, 4, 2 * rows_d, wide[m])

    def part(m):
        return (2, 2, rows_f, wide[m]) if m in DN else (2, 2 * rows_d, wide[m])

    scratch = []
    scratch += [pltpu.VMEM((2, *full(m)), BF) for m in ALL]
    scratch += [pltpu.VMEM((2, *full(m)), BF) for m in ALL]
    scratch += [pltpu.VMEM(full(m), BF) for m in ALL]
    scratch += [
        pltpu.VMEM((3, *part(m)[1:]) if m in PLANE_REDUCE else part(m), BF) for m in ALL
    ]
    scratch += [pltpu.VMEM((16, 128) if m in PLANE_REDUCE else part(m), BF) for m in ALL]
    scratch += [
        pltpu.VMEM((3, *((4,) if m in PLANE_REDUCE else ()), *chip[m], wide[m]), BF) for m in ALL
    ]
    scratch += [pltpu.VMEM((*chip[m], wide[m]), F32) for m in ALL]
    scratch += [pltpu.VMEM((mine[m], wide[m]), F32) for m in ALL]
    scratch += [pltpu.VMEM((mine[m], wide[m]), F32) for m in ALL]
    dma = pltpu.SemaphoreType.DMA
    scratch += [dma((N, 12)), dma((N, 12)), dma((N, 9)), dma((N, 9)), dma((7,)), dma((7,))]
    act = (tokens, width)
    scratch += [
        pltpu.VMEM((width, width), BF),
        pltpu.VMEM((BLOCKS, VOC, span), BF),
        pltpu.VMEM((8, span), F32),
        pltpu.VMEM((tokens, 384), BF),
        pltpu.VMEM((tokens, 384), BF),
        pltpu.VMEM((8, width), F32),
        pltpu.VMEM(act, BF),
        pltpu.VMEM(act, BF),
        pltpu.VMEM((width, tokens), BF),
        pltpu.VMEM((width // 128, tokens, 128), BF),
        pltpu.VMEM((width // 128, tokens, 128), BF),
        pltpu.VMEM((width // 128, tokens, 128), BF),
        pltpu.VMEM((heads, 1, span), F32),
        pltpu.VMEM((heads, tokens, tokens), F32),
        pltpu.VMEM(act, BF),
        pltpu.VMEM(act, BF),
        pltpu.VMEM(act, F32),
        pltpu.VMEM(act, BF),
        pltpu.VMEM((width, tokens), BF),
        pltpu.VMEM(act, F32),
        pltpu.VMEM(act, F32),
        pltpu.VMEM(act, BF),
        pltpu.VMEM(act, BF),
        pltpu.VMEM(act, BF),
        pltpu.VMEM((heads, 1, span), F32),
        pltpu.VMEM((4, 16, 128), F32),
        pltpu.VMEM((6, 16, 128), F32),
        pltpu.VMEM(act, BF),
        *[pltpu.VMEM(item.shape, item.dtype) for item in args[9:]],
        dma((8,)),
        *[pltpu.VMEM(item.shape, F32) for item in args[9:16]],
        dma((7,)),
    ]
    outs = [
        jax.ShapeDtypeStruct((MICRO, tokens, half), BF),
        jax.ShapeDtypeStruct((rows_d, 512), F32),
        *[jax.ShapeDtypeStruct(item.shape, F32) for item in args[9:16]],
        jax.ShapeDtypeStruct((16, 128), F32),
    ]
    return pl.pallas_call(
        functools.partial(kernel, inner, (tokens, width, half, ffh)),
        out_shape=outs,
        in_specs=[VMEM] * 9 + [ANY] * 8,
        out_specs=[VMEM] * 2 + [ANY] * 7 + [VMEM],
        scratch_shapes=scratch,
        compiler_params=pltpu.CompilerParams(
            collective_id=0, has_side_effects=True, vmem_limit_bytes=63 * 2**20
        ),
    )(*args)


def settle(vocab, langs, heads, buckets, *refs):
    ins, outs = refs[:10], refs[10:]
    outs[0][:, 0] = ins[0][...]
    rows = ins[1].shape[0]
    outs[1][...] = ins[1][:, :vocab]
    table = ins[1][:, 256:]
    table = jnp.concatenate([table, jnp.zeros((128 - rows, 256), F32)], axis=0).T[:, :rows]
    at = vocab - 256
    outs[2][...] = table[at : at + langs]
    at = at + langs
    for k, i in enumerate((3, 4, 9)):
        outs[i][...] = table[at + k : at + k + 1]
    for i, k in zip((5, 6, 7, 8, 10, 11, 12), range(2, 9)):
        outs[i][...] = ins[k][...]
    outs[13][...] = ins[9][:heads, :buckets]


def body(
    byte_ids, lengths, groups, embedding, language, scorer, prenorm, query_weight, key_weight, value_weight,
    output_weight, midnorm, gate_weight, up_weight, down_weight, relative, cotangent,
):
    inner = lax.axis_size("dp") // OUTER
    vocab, langs = embedding.shape[0], language.shape[0]
    tables = [embedding.T, language, scorer[None], prenorm[None], midnorm[None]]
    weights = [query_weight, key_weight, value_weight, output_weight, gate_weight, up_weight, down_weight]
    teams = [[o * inner + i for i in range(inner)] for o in range(OUTER)]
    if inner > 1:
        tables = [
            lax.all_gather(item, "dp", axis_index_groups=teams, axis=min(i, 1), tiled=True)
            for i, item in enumerate(tables)
        ]
        weights = [lax.all_gather(item, "dp", axis_index_groups=teams, axis=0, tiled=True) for item in weights]
    results = call(inner, byte_ids, lengths.T, groups.T, *tables, relative.T, *weights, cotangent[:, 0])
    if inner > 1:
        grads = [
            lax.psum_scatter(item, "dp", axis_index_groups=teams, scatter_dimension=0, tiled=True)
            for item in results[1:9]
        ]
        results = [results[0], *grads, lax.psum(results[9], "dp", axis_index_groups=teams)]
    buckets, heads = relative.shape
    rows = results[1].shape[0]
    line = jax.ShapeDtypeStruct((1, rows), F32)
    like = [jax.ShapeDtypeStruct(item.shape, F32) for item in results[2:9]]
    shapes = [
        jax.ShapeDtypeStruct(cotangent.shape[:3] + (results[0].shape[2],), BF),
        jax.ShapeDtypeStruct((rows, vocab), F32),
        jax.ShapeDtypeStruct((langs, rows), F32),
        line, line, *like[:4], line, *like[4:],
        jax.ShapeDtypeStruct((heads, buckets), F32),
    ]
    outs = pl.pallas_call(
        functools.partial(settle, vocab, langs, heads, buckets),
        out_shape=shapes,
        in_specs=[VMEM] * 10,
        out_specs=[VMEM] * 14,
        compiler_params=pltpu.CompilerParams(vmem_limit_bytes=60 * 2**20),
    )(*results)
    return tuple(item[0] if i in (3, 4, 9) else item.T if i in (1, 13) else item for i, item in enumerate(outs))


def solution(mesh):
    both = ("section", "dp")
    wide = P(both, None)
    return jax.shard_map(
        body,
        mesh=mesh,
        in_specs=(
            P(None, "dp", None), P(None, "dp"), P(None, "dp"), P(None, both), P(None, both), P(both), P(both),
            wide, wide, wide, wide, P(both), wide, wide, wide, P(), P(None, "dp", None, None),
        ),
        out_specs=(
            P(None, "dp", None, "section"), P(None, both), P(None, both), P(both), P(both),
            wide, wide, wide, wide, P(both), wide, wide, wide, P(),
        ),
        check_vma=False,
    )
```
